32 devices in a mesh: rep: 4 (over z), fsdp: 8 (over y, x, core).
Axes of the slice: x: 2, y: 2, z: 4, core: 2. Of those that a mesh axis runs over, the one named last changes fastest.
Arguments:
- tokens: bfloat16 [16384, 640], P(('rep', 'fsdp')), may hold values from -60 to 60
- cotangent: bfloat16 [16384, 640], P(('rep', 'fsdp')), may hold values from -6 to 6
- prefix: int32 [16], replicated, may hold values from 1 to 1023
- w_qkv: bfloat16 [640, 1536], P('fsdp'), may hold values from -0.3043692 to 0.3043692
- w_out: bfloat16 [1024, 640], P('fsdp'), may hold values from -0.2359375 to 0.2359375
- w_gate: bfloat16 [640, 2048], P('fsdp'), may hold values from -0.23321798 to 0.23321798
- w_up: bfloat16 [640, 2048], P('fsdp'), may hold values from -0.23321798 to 0.23321798
- w_down: bfloat16 [2048, 640], P('fsdp'), may hold values from -0.16683301 to 0.16683301
- gains: bfloat16 [640, 4], P('fsdp'), may hold values from 0.4 to 2.5
- moment_qkv: float32 [640, 1536], P('fsdp'), may hold values from -16 to 16
- moment_out: float32 [1024, 640], P('fsdp'), may hold values from -16 to 16
- moment_gate: float32 [640, 2048], P('fsdp'), may hold values from -16 to 16
- moment_up: float32 [640, 2048], P('fsdp'), may hold values from -16 to 16
- moment_down: float32 [2048, 640], P('fsdp'), may hold values from -16 to 16
- gain_first: float32 [640, 4], P('fsdp'), may hold values from -96 to 96
- gain_second: float32 [640, 4], P('fsdp'), may hold values from 819.2 to 3276.8
Outputs:
- output: float32 [16384, 640], P(('rep', 'fsdp'))
- grad_tokens: float32 [16384, 640], P(('rep', 'fsdp'))
- grad_qkv: float32 [640, 1536], P('fsdp')
- grad_out: float32 [1024, 640], P('fsdp')
- grad_gate: float32 [640, 2048], P('fsdp')
- grad_up: float32 [640, 2048], P('fsdp')
- grad_down: float32 [2048, 640], P('fsdp')
- grad_gains: float32 [640, 4], P('fsdp')
- moment_qkv_new: float32 [640, 1536], P('fsdp')
- moment_out_new: float32 [1024, 640], P('fsdp')
- moment_gate_new: float32 [640, 2048], P('fsdp')
- moment_up_new: float32 [640, 2048], P('fsdp')
- moment_down_new: float32 [2048, 640], P('fsdp')
- master_qkv: float32 [640, 1536], P('fsdp')
- master_out: float32 [1024, 640], P('fsdp')
- master_gate: float32 [640, 2048], P('fsdp')
- master_up: float32 [640, 2048], P('fsdp')
- master_down: float32 [2048, 640], P('fsdp')
- first_new: float32 [640, 4], P('fsdp')
- second_new: float32 [640, 4], P('fsdp')
- master_gains: float32 [640, 4], P('fsdp')
- statistics: float32 [4], replicated
The draws below stay inside these ranges and needn't reach their ends.
All inputs are finite; a program needn't handle non-finite values.
Results may differ from the reference program's by a relative error of at most 0.02.
The reference program's roundings to bfloat16 on the way count: a program that leaves them out, or rounds other values in their place, can miss the bound.
Values may be sent and summed in bfloat16 or wider, within the bound.
A program may use at most 256 MiB of HBM per device.

```python
import math
import jax
import jax.numpy as jnp
from jax import lax

D = 640
HEADS = 4
HEAD_DIM = 256
FF = 2048
NS_STEPS = 5
ADAM_STEP = 10
SEQ = 1024
TOKENS = 16384
SEQS = 16
ATTN = 1024
QKV = 1536


def shared_scales(key):
    key_ratio, key_gain = jax.random.split(key)
    log_ratio = jax.random.uniform(key_ratio, (D,), jnp.float32, -math.log(3.0), math.log(3.0))
    log_gain = jax.random.uniform(key_gain, (D, 4), jnp.float32, math.log(0.4), math.log(2.5))
    return (log_ratio, log_gain)


def draw_tokens(key, part):
    log_ratio, log_gain = shared_scales(key)
    key = jax.random.fold_in(key, 11)
    key_base, key_rows, key_sign, key_size = jax.random.split(key, 4)
    magnitude = jax.random.uniform(key_size, (SEQS,), jnp.float32, 0.5, 1.0)
    upper = jax.random.bernoulli(key_sign, 0.5, (SEQS,))
    base = jax.random.normal(key_base, (TOKENS, D), jnp.float32)
    row_scale = jnp.exp(jax.random.uniform(key_rows, (TOKENS, 1), jnp.float32, jnp.log(0.25), jnp.log(2.5)))
    exponent = jnp.where(upper, magnitude, -magnitude)
    row_exponent = jnp.repeat(exponent, SEQ)[:, None]
    col_scale = jnp.exp(row_exponent * log_ratio[None, :])
    rising = 0.5 + jnp.arange(TOKENS, dtype=jnp.float32)[:, None] / TOKENS
    values = jnp.clip(base * row_scale * col_scale * rising, -60.0, 60.0)
    return values.astype(jnp.bfloat16)


def draw_gains(key, part):
    log_ratio, log_gain = shared_scales(key)
    return jnp.exp(log_gain).astype(jnp.bfloat16)


def draw_w_qkv(key, part):
    log_ratio, log_gain = shared_scales(key)
    key = jax.random.fold_in(key, 12)
    base = jax.random.truncated_normal(key, -3.0, 3.0, (D, QKV), jnp.float32)
    column_head = jnp.arange(QKV) // HEAD_DIM
    direction = jnp.where(column_head < HEADS // 2, 1.0, jnp.where(column_head < HEADS, -1.0, 0.0))
    level = jnp.where(column_head < HEADS, 0.85, 1.0)
    scale = level[None, :] * jnp.exp(direction[None, :] * log_ratio[:, None]) / math.sqrt(D)
    return (base * scale).astype(jnp.bfloat16)


def spread_columns(key, log_ratio):
    base = jax.random.truncated_normal(key, -3.0, 3.0, (D, FF), jnp.float32)
    direction = jnp.where(jnp.arange(FF) < FF // 2, 1.0, -1.0)
    scale = 0.65 * jnp.exp(direction[None, :] * log_ratio[:, None]) / math.sqrt(D)
    return (base * scale).astype(jnp.bfloat16)


def draw_w_gate(key, part):
    log_ratio, log_gain = shared_scales(key)
    key = jax.random.fold_in(key, 13)
    return spread_columns(key, log_ratio)


def draw_w_up(key, part):
    log_ratio, log_gain = shared_scales(key)
    key = jax.random.fold_in(key, 14)
    return spread_columns(key, log_ratio)


def draw_w_out(key, part):
    log_ratio, log_gain = shared_scales(key)
    key = jax.random.fold_in(key, 15)
    base = jax.random.truncated_normal(key, -3.0, 3.0, (ATTN, D), jnp.float32)
    row_head = jnp.arange(ATTN) // HEAD_DIM
    direction = jnp.where(row_head < HEADS // 2, 1.0, -1.0)
    scale = jnp.exp(direction[:, None] * log_gain[None, :, 1]) / math.sqrt(ATTN)
    return (base * scale).astype(jnp.bfloat16)


def draw_w_down(key, part):
    log_ratio, log_gain = shared_scales(key)
    key = jax.random.fold_in(key, 16)
    base = jax.random.truncated_normal(key, -3.0, 3.0, (FF, D), jnp.float32)
    direction = jnp.where(jnp.arange(FF) < FF // 2, 1.0, -1.0)
    scale = jnp.exp(direction[:, None] * log_gain[None, :, 3]) / math.sqrt(FF)
    return (base * scale).astype(jnp.bfloat16)


def place_ends(entries, rng, low, largest):
    longest = entries.shape.index(max(entries.shape))
    spots = []
    for shift in (0, 1):
        where = [jax.random.randint(jax.random.fold_in(rng, axis), (), 0, length) for axis, length in enumerate(entries.shape)]
        where[longest] = (where[longest] + shift) % entries.shape[longest]
        spots.append(tuple(where))
    return entries.at[spots[0]].set(low).at[spots[1]].set(largest)


def level_of(stream_key, shape, pieces, least, high):
    factor_of, own = 1.0, jax.random.fold_in(stream_key, 6)
    for dim, blocks in pieces:
        steps = jnp.exp(jax.random.uniform(jax.random.fold_in(own, dim), (blocks,), jnp.float32, least / len(pieces), high / len(pieces)))
        factor_of = factor_of * jnp.repeat(steps, shape[dim] // blocks).reshape([-1 if axis == dim else 1 for axis in range(len(shape))])
    return factor_of


def centred(stream_key, shape, deviation, most, pieces=(), kind=jnp.bfloat16):
    entries = deviation * jax.random.normal(stream_key, shape, jnp.float32)
    if pieces:
        entries = entries * level_of(stream_key, shape, pieces, -0.22, 0.18)
    return jnp.clip(entries, -most, most).astype(kind)


def setup_inputs(seed: int = 0) -> dict:
    arg_keys = jax.random.split(jax.random.key(seed), 17)
    tokens = draw_tokens(jax.random.fold_in(arg_keys[16], 71), 0)
    cotangent = centred(arg_keys[1], (TOKENS, D), 1.0, 6.0, ((0, 32),))
    prefix = place_ends(jax.random.randint(arg_keys[2], (SEQS,), 1, SEQ), jax.random.fold_in(arg_keys[2], 1), 1, SEQ - 1).astype(jnp.int32)
    w_qkv = draw_w_qkv(jax.random.fold_in(arg_keys[16], 71), 0)
    w_out = draw_w_out(jax.random.fold_in(arg_keys[16], 71), 0)
    w_gate = draw_w_gate(jax.random.fold_in(arg_keys[16], 71), 0)
    w_up = draw_w_up(jax.random.fold_in(arg_keys[16], 71), 0)
    w_down = draw_w_down(jax.random.fold_in(arg_keys[16], 71), 0)
    gains = draw_gains(jax.random.fold_in(arg_keys[16], 71), 0)
    moment_qkv = centred(arg_keys[9], (D, QKV), (0.02 * TOKENS ** 0.5), 16.0, ((0, 8),), jnp.float32)
    moment_out = centred(arg_keys[10], (ATTN, D), (0.02 * TOKENS ** 0.5), 16.0, ((0, 8),), jnp.float32)
    moment_gate = centred(arg_keys[11], (D, FF), (0.02 * TOKENS ** 0.5), 16.0, ((0, 8),), jnp.float32)
    moment_up = centred(arg_keys[12], (D, FF), (0.02 * TOKENS ** 0.5), 16.0, ((0, 8),), jnp.float32)
    moment_down = centred(arg_keys[13], (FF, D), (0.02 * TOKENS ** 0.5), 16.0, ((0, 8),), jnp.float32)
    gain_first = centred(arg_keys[14], (D, 4), (0.12 * TOKENS ** 0.5), 96.0, ((0, 8),), jnp.float32)
    gain_second = jnp.clip(jnp.exp(math.log(3276.8) - 1.3862944 * jax.random.uniform(arg_keys[15], (D, 4), jnp.float32) ** level_of(arg_keys[15], (D, 4), ((0, 8),), -0.2, 0.2)), 819.2, 3276.8)
    return dict(tokens=tokens, cotangent=cotangent, prefix=prefix, w_qkv=w_qkv, w_out=w_out, w_gate=w_gate, w_up=w_up, w_down=w_down, gains=gains, moment_qkv=moment_qkv, moment_out=moment_out, moment_gate=moment_gate, moment_up=moment_up, moment_down=moment_down, gain_first=gain_first, gain_second=gain_second)


norm_epsilon = 1e-06
soft_cap = 50.0
rotary_base = 10000.0
newton_first = 3.4445
newton_second = -4.775
newton_third = 2.0315
momentum_decay = 0.95
muon_rate = 1.0
first_decay = 0.9
second_decay = 0.95
adam_rate = 1.0
weight_decay = 0.1
adam_epsilon = 1e-08
frobenius_epsilon = 1e-07
masked_score = -1000000000.0
highest = lax.Precision.HIGHEST

@jax.custom_vjp
def low(v):
    return lax.optimization_barrier(v.astype(jnp.bfloat16)).astype(jnp.float32)

@jax.custom_vjp
def low_back(v):
    return v

def low_keep(v):
    return (low(v), None)

def low_pass(kept, grad):
    return (grad,)

def back_keep(v):
    return (v, None)

def back_low(kept, grad):
    return (low(grad),)
low.defvjp(low_keep, low_pass)
low_back.defvjp(back_keep, back_low)

def matmul(left, right):
    return jnp.dot(left, right, preferred_element_type=jnp.float32, precision=highest)

def rms_scale(values, gain):
    return values * lax.rsqrt(lax.optimization_barrier(jnp.mean(values * values, axis=-1, keepdims=True)) + norm_epsilon) * gain

def gated_product(gate, upward):
    return 0.5 * gate * (1.0 + jnp.tanh(0.7978845608028654 * (gate + 0.044715 * gate * gate * gate))) * upward

def rotary_tables(positions, head_dim):
    half_dim = head_dim // 2
    frequency = rotary_base ** (-(jnp.arange(half_dim, dtype=jnp.float32) * 2.0 / head_dim))
    angles = positions.astype(jnp.float32)[:, None] * frequency[None, :]
    return (jnp.cos(angles), jnp.sin(angles))

def rotary(values, cosine, sine):
    half_dim = values.shape[-1] // 2
    first_half = values[..., :half_dim]
    second_half = values[..., half_dim:]
    return jnp.concatenate([first_half * cosine - second_half * sine, second_half * cosine + first_half * sine], axis=-1)

def attend_sequence(queries, keys, values, prefix_len):
    block_rows = min(512, SEQ)
    score_scale = HEAD_DIM ** (-0.5)
    key_positions = jnp.arange(SEQ, dtype=jnp.int32)

    def one_block(inputs):
        query_block, start = inputs
        raw_scores = low_back(jnp.einsum('rhd,kd->hrk', query_block, keys, precision=highest, preferred_element_type=jnp.float32))
        capped = soft_cap * jnp.tanh(raw_scores * score_scale / soft_cap)
        query_positions = start + jnp.arange(block_rows, dtype=jnp.int32)
        allowed = (key_positions[None, :] <= query_positions[:, None]) | (key_positions[None, :] < prefix_len)
        capped = jnp.where(allowed[None], capped, masked_score)
        top_score = lax.optimization_barrier(jnp.max(capped, axis=-1, keepdims=True))
        weights_exp = jnp.exp(capped - top_score)
        softmaxed = weights_exp / lax.optimization_barrier(jnp.sum(weights_exp, axis=-1, keepdims=True))
        softmaxed_low = low(softmaxed)
        return jnp.einsum('hrk,kd->rhd', softmaxed_low, values, precision=highest, preferred_element_type=jnp.float32)
    blocks = queries.reshape(SEQ // block_rows, block_rows, HEADS, HEAD_DIM)
    starts = jnp.arange(SEQ // block_rows, dtype=jnp.int32) * block_rows
    outputs = lax.map(jax.checkpoint(one_block), (blocks, starts))
    return outputs.reshape(SEQ, HEADS * HEAD_DIM)

def block_forward(weights, inputs):
    w_qkv, w_out, w_gate, w_up, w_down, gains = weights
    residual, prefix_block = inputs
    block_seqs = prefix_block.shape[0]
    attn_width = HEADS * HEAD_DIM
    positions = jnp.tile(jnp.arange(SEQ, dtype=jnp.int32), block_seqs)
    normed_one = low(rms_scale(residual, gains[:, 0]))
    projected = low_back(matmul(normed_one, w_qkv))
    cosine, sine = rotary_tables(positions, HEAD_DIM)
    queries = low(rotary(projected[:, :attn_width].reshape(-1, HEADS, HEAD_DIM), cosine[:, None, :], sine[:, None, :]))
    keys = low(rotary(projected[:, attn_width:attn_width + HEAD_DIM], cosine, sine))
    values = low(projected[:, attn_width + HEAD_DIM:])
    attended = jax.vmap(attend_sequence)(queries.reshape(block_seqs, SEQ, HEADS, HEAD_DIM), keys.reshape(block_seqs, SEQ, HEAD_DIM), values.reshape(block_seqs, SEQ, HEAD_DIM), prefix_block)
    attended = low(low_back(attended.reshape(-1, attn_width)))
    branch_one = low_back(matmul(attended, w_out))
    first_out = rms_scale(branch_one, gains[:, 1])
    hidden = residual + first_out
    normed_two = low(rms_scale(hidden, gains[:, 2]))
    gate = low_back(matmul(normed_two, w_gate))
    upward = low_back(matmul(normed_two, w_up))
    active = low(gated_product(gate, upward))
    branch_two = low_back(matmul(active, w_down))
    second_out = rms_scale(branch_two, gains[:, 3])
    final = hidden + second_out
    valid = (positions >= jnp.repeat(prefix_block, SEQ)).astype(jnp.float32)
    squares = jnp.stack([jnp.sum(valid * lax.optimization_barrier(jnp.sum(stream * stream, axis=-1))) for stream in (residual, first_out, second_out, final)])
    return (final, (squares, jnp.sum(valid)))

def orthogonalize(matrix):
    row_count, col_count = matrix.shape
    frobenius = jnp.sqrt(jnp.sum(matrix * matrix))
    current = matrix / (frobenius + frobenius_epsilon)
    if row_count > col_count:
        current = current.T
    for repeat_number in range(NS_STEPS):
        gram = jnp.dot(current, current.T, precision=highest, preferred_element_type=jnp.float32)
        squared = jnp.dot(gram, gram, precision=highest, preferred_element_type=jnp.float32)
        mixer = newton_second * gram + newton_third * squared
        current = newton_first * current + jnp.dot(mixer, current, precision=highest, preferred_element_type=jnp.float32)
    if row_count > col_count:
        current = current.T
    return current

def reference(tokens, cotangent, prefix, w_qkv, w_out, w_gate, w_up, w_down, gains, moment_qkv, moment_out, moment_gate, moment_up, moment_down, gain_first, gain_second):
    block_seqs = 2
    block_rows = block_seqs * SEQ
    gains_wide = gains.astype(jnp.float32)

    def forward_all(residual, weight_qkv, weight_out, weight_gate, weight_up, weight_down, gain_table):
        weights = (weight_qkv, weight_out, weight_gate, weight_up, weight_down, gain_table)
        stepper = jax.checkpoint(block_forward)

        def scan_body(carry, inputs):
            return (carry, stepper(weights, inputs))
        inputs = (residual.reshape(-1, block_rows, D), prefix.reshape(-1, block_seqs))
        carry, (finals, (squares, counts)) = lax.scan(scan_body, jnp.zeros((), jnp.float32), inputs)
        return (finals.reshape(TOKENS, D), (lax.optimization_barrier(jnp.sum(squares, axis=0)), jnp.sum(counts)))
    weights_wide = (w_qkv.astype(jnp.float32), w_out.astype(jnp.float32), w_gate.astype(jnp.float32), w_up.astype(jnp.float32), w_down.astype(jnp.float32))
    final, pullback, (squares, count) = jax.vjp(forward_all, tokens.astype(jnp.float32), weights_wide[0], weights_wide[1], weights_wide[2], weights_wide[3], weights_wide[4], gains_wide, has_aux=True)
    gradients = pullback(cotangent.astype(jnp.float32))
    statistics = jnp.sqrt(squares / (count * D))
    grad_tokens = gradients[0]
    matrix_grads = gradients[1:6]
    grad_gains = gradients[6]
    moments = (moment_qkv, moment_out, moment_gate, moment_up, moment_down)
    new_moments = []
    masters = []
    for number in range(5):
        new_moment = momentum_decay * moments[number] + (1.0 - momentum_decay) * matrix_grads[number]
        nesterov = (1.0 - momentum_decay) * matrix_grads[number] + momentum_decay * new_moment
        ortho = orthogonalize(nesterov)
        row_count, col_count = nesterov.shape
        factor = max(1.0, row_count / col_count) ** 0.5
        new_moments.append(new_moment)
        masters.append(weights_wide[number] - muon_rate * factor * ortho)
    first_new = first_decay * gain_first + (1.0 - first_decay) * grad_gains
    second_new = second_decay * gain_second + (1.0 - second_decay) * grad_gains * grad_gains
    first_hat = first_new / (1.0 - first_decay ** ADAM_STEP)
    second_hat = second_new / (1.0 - second_decay ** ADAM_STEP)
    master_gains = gains_wide - adam_rate * (first_hat / (jnp.sqrt(second_hat) + adam_epsilon) + weight_decay * gains_wide)
    return (final, grad_tokens, matrix_grads[0], matrix_grads[1], matrix_grads[2], matrix_grads[3], matrix_grads[4], grad_gains, new_moments[0], new_moments[1], new_moments[2], new_moments[3], new_moments[4], masters[0], masters[1], masters[2], masters[3], masters[4], first_new, second_new, master_gains, statistics)
```

```python
import jax
import jax.numpy as jnp
from jax import lax
from jax.experimental import pallas as pl
from jax.experimental.pallas import tpu as pltpu
from jax.sharding import PartitionSpec as P

D = 640
HEADS = 4
HEAD_DIM = 256
NS_STEPS = 5
ADAM_STEP = 10


norm_epsilon = 1e-06
soft_cap = 50.0
rotary_base = 10000.0
newton_first = 3.4445
newton_second = -4.775
newton_third = 2.0315
momentum_decay = 0.95
muon_rate = 1.0
first_decay = 0.9
second_decay = 0.95
adam_rate = 1.0
weight_decay = 0.1
adam_epsilon = 1e-08
frobenius_epsilon = 1e-07
masked_score = -1000000000.0


def swapped(x, axis, bit):
    return lax.ppermute(x, axis, [(i, i ^ 1 << bit) for i in range(lax.axis_size(axis))])


def rms_scale(values, gain):
    return (
        values * lax.rsqrt(jnp.mean(values * values, axis=-1, keepdims=True) + norm_epsilon) * gain
    )


def gated_product(gate, upward):
    return (
        0.5
        * gate
        * (1.0 + jnp.tanh(0.7978845608028654 * (gate + 0.044715 * gate * gate * gate)))
        * upward
    )


def rotary_tables(positions, head_dim):
    half_dim = head_dim // 2
    frequency = rotary_base ** (-(jnp.arange(half_dim, dtype=jnp.float32) * 2.0 / head_dim))
    angles = positions.astype(jnp.float32)[:, None] * frequency[None, :]
    return (jnp.cos(angles), jnp.sin(angles))


def rotary(values, cosine, sine):
    half_dim = values.shape[-1] // 2
    first_half = values[..., :half_dim]
    second_half = values[..., half_dim:]
    return jnp.concatenate(
        [first_half * cosine - second_half * sine, second_half * cosine + first_half * sine],
        axis=-1,
    )


GROUP = 8
MESH = pl.DeviceIdType.MESH
f32 = jnp.float32
bf16 = jnp.bfloat16


def dot(a, b):
    return lax.dot_general(a, b, (((1,), (0,)), ((), ())), preferred_element_type=f32)


def dot_nt(a, b):
    return lax.dot_general(a, b, (((1,), (1,)), ((), ())), preferred_element_type=f32)


def dot_tn(a, b):
    return lax.dot_general(a, b, (((0,), (0,)), ((), ())), preferred_element_type=f32)


def place():
    size = lax.axis_size("fsdp")
    lanes = size // GROUP
    here = lax.axis_index("fsdp")
    return lax.axis_index("rep"), here // lanes, lax.rem(here, lanes), lanes


OWNERS = (6, 7, 0, 2, 4)
FLIPPED = (False, True, False, False, True)


def gram_into(x_ref, gram):
    rows = gram.shape[0]
    starts = list(range(0, rows, 256))
    for j in starts:
        n = min(256, rows - j)
        gram[j:rows, j : j + n] = dot_nt(x_ref[j:rows, :], x_ref[j : j + n, :])
    for j in starts:
        n = min(256, rows - j)
        if j + n < rows:
            gram[j : j + n, j + n : rows] = gram[j + n : rows, j : j + n].T


def newton_step(x_ref, gram, mixer, high, low, first, refined):
    gram_into(x_ref, gram)
    rows = gram.shape[0]
    same = lax.broadcasted_iota(jnp.int32, (rows, rows), 0) == lax.broadcasted_iota(
        jnp.int32, (rows, rows), 1
    )
    whole = gram[...]
    scale = None
    if first:
        scale = 1.0 / (jnp.sqrt(jnp.sum(jnp.where(same, whole, 0.0))) + frobenius_epsilon)
        whole = whole * (scale * scale)
        gram[...] = whole
    high[...] = whole.astype(bf16)
    squared = dot(high[...], high[...])
    if refined:
        low[...] = (gram[...] - high[...].astype(f32)).astype(bf16)
        squared = squared + dot(high[...], low[...]) + dot(low[...], high[...])
    mix = (
        jnp.where(same, newton_first, 0.0) + newton_second * gram[...] + newton_third * squared
    )
    if first:
        mix = mix * scale
    mixer[...] = mix.astype(bf16)
    width = x_ref.shape[1]
    tile = 1024 if width % 1024 == 0 else width

    @pl.loop(0, width // tile)
    def _(t):
        cols = pl.ds(pl.multiple_of(t * tile, tile), tile)
        x_ref[:, cols] = dot(mixer[...], x_ref[:, cols]).astype(bf16)


def muon_kernel(shapes, *refs):
    grads, moments, weights = refs[0:5], refs[5:10], refs[10:15]
    news, masters = refs[15:20], refs[20:25]
    outgoing, arrived = refs[25:30], refs[30:35]
    x_all, gram, mixer, high, low = refs[35:40]
    gather_send, gather_recv, scatter_send, scatter_recv = refs[40:44]
    rep, me, lane, lanes = place()

    def device(member):
        return (rep, member * lanes + lane)

    owner_here = me == OWNERS[0]
    for owner in OWNERS[1:]:
        owner_here = owner_here | (me == owner)

    @pl.when(owner_here)
    def _():
        x_all[...] = jnp.zeros_like(x_all)

    barrier = pltpu.get_barrier_semaphore()
    for step in range(1, GROUP):
        pl.semaphore_signal(
            barrier, inc=1, device_id=device(me ^ step), device_id_type=MESH
        )

    def block(number, member):
        rows, cols = shapes[number]
        if FLIPPED[number]:
            return x_all.at[:, pl.ds(member * rows, rows)]
        return x_all.at[pl.ds(member * rows, rows), pl.ds(0, cols)]

    for number in range(5):
        grad = grads[number][...]
        new = momentum_decay * moments[number][...] + (1.0 - momentum_decay) * grad
        news[number][...] = new
        nesterov = (1.0 - momentum_decay) * grad + momentum_decay * new
        if FLIPPED[number]:
            nesterov = nesterov.T
        outgoing[number][...] = nesterov.astype(bf16)
    pl.semaphore_wait(barrier, GROUP - 1)

    def gather_copy(number, member, sender):
        rows, _ = shapes[number]
        if FLIPPED[number]:
            start = pl.multiple_of(sender * rows, rows)
            target = x_all.at[:, pl.ds(start, rows)]
        else:
            start = pl.multiple_of(sender * rows, 16)
            target = x_all.at[pl.ds(start, rows), pl.ds(0, shapes[number][1])]
        return pltpu.make_async_remote_copy(
            src_ref=outgoing[number],
            dst_ref=target,
            send_sem=gather_send.at[number],
            recv_sem=gather_recv.at[sender],
            device_id=device(member),
            device_id_type=MESH,
        )

    for number in (2, 3, 4, 0, 1):

        @pl.when(me != OWNERS[number])
        def _():
            gather_copy(number, OWNERS[number], me).start()

    for number in range(5):
        owner = OWNERS[number]

        @pl.when(me == owner)
        def _():
            rows, cols = shapes[number]
            if FLIPPED[number]:
                x_all[:, owner * rows : (owner + 1) * rows] = outgoing[number][...]
            else:
                x_all[owner * rows : (owner + 1) * rows, 0:cols] = outgoing[number][...]
            for step in range(1, GROUP):
                gather_copy(number, owner, owner ^ step).wait_recv()

    @pl.when(owner_here)
    def _():
        newton_step(x_all, gram, mixer, high, low, True, False)

        @pl.loop(0, NS_STEPS - 3)
        def _(k):
            newton_step(x_all, gram, mixer, high, low, False, False)

        @pl.loop(0, 2)
        def _(k):
            newton_step(x_all, gram, mixer, high, low, False, True)

    def scatter_copy(number, member):
        rows, cols = shapes[number]
        return pltpu.make_async_remote_copy(
            src_ref=block(number, member),
            dst_ref=arrived[number],
            send_sem=scatter_send.at[member],
            recv_sem=scatter_recv.at[number],
            device_id=device(member),
            device_id_type=MESH,
        )

    for number in range(5):
        owner = OWNERS[number]

        @pl.when(me == owner)
        def _():
            for step in range(1, GROUP):
                scatter_copy(number, owner ^ step).start()
            arrived[number][...] = block(number, owner)[...]

    for number in range(5):
        owner = OWNERS[number]

        @pl.when(me != owner)
        def _():
            scatter_copy(number, owner).wait_recv()

        rows, cols = shapes[number]
        factor = max(1.0, rows * GROUP / cols) ** 0.5 * muon_rate
        update = arrived[number][...].astype(f32)
        if FLIPPED[number]:
            update = update.T
        masters[number][...] = weights[number][...].astype(f32) - factor * update

    for number in range(5):
        owner = OWNERS[number]

        @pl.when(me == owner)
        def _():
            for step in range(1, GROUP):
                scatter_copy(number, owner ^ step).wait_send()

        @pl.when(me != owner)
        def _():
            gather_copy(number, owner, me).wait_send()


def muon(grads, moments, weights):
    shapes = tuple(g.shape for g in grads)
    flipped = [s[::-1] if flip else s for s, flip in zip(shapes, FLIPPED)]
    side = flipped[0][0] * GROUP
    width = max(s[1] if not flip else s[1] * GROUP for s, flip in zip(flipped, FLIPPED))
    vmem = pl.BlockSpec(memory_space=pltpu.VMEM)
    out = pl.pallas_call(
        lambda *refs: muon_kernel(shapes, *refs),
        out_shape=[jax.ShapeDtypeStruct(s, f32) for s in shapes + shapes],
        in_specs=[vmem] * 15,
        out_specs=[vmem] * 10,
        scratch_shapes=[pltpu.VMEM(s, bf16) for s in flipped]
        + [pltpu.VMEM(s, bf16) for s in flipped]
        + [
            pltpu.VMEM((side, width), bf16),
            pltpu.VMEM((side, side), f32),
            pltpu.VMEM((side, side), bf16),
            pltpu.VMEM((side, side), bf16),
            pltpu.VMEM((side, side), bf16),
            pltpu.SemaphoreType.DMA((5,)),
            pltpu.SemaphoreType.DMA((GROUP,)),
            pltpu.SemaphoreType.DMA((GROUP,)),
            pltpu.SemaphoreType.DMA((5,)),
        ],
        compiler_params=pltpu.CompilerParams(
            collective_id=1, has_side_effects=True, vmem_limit_bytes=60 * 2**20
        ),
        name="muon",
    )(*grads, *moments, *weights)
    return out[:5], out[5:]


def shards(
    tokens,
    cotangent,
    prefix,
    w_qkv,
    w_out,
    w_gate,
    w_up,
    w_down,
    gains,
    moment_qkv,
    moment_out,
    moment_gate,
    moment_up,
    moment_down,
    gain_first,
    gain_second,
):
    row_count = tokens.shape[0]
    fsdp_size = lax.axis_size("fsdp")
    fsdp_place = lax.axis_index("fsdp")
    rep_place = lax.axis_index("rep")
    parity = fsdp_place % 2
    sequence_id = (rep_place * fsdp_size + fsdp_place) // 2
    table_ids = jnp.arange(prefix.shape[0], dtype=jnp.int32)
    prefix_len = jnp.sum(jnp.where(table_ids == sequence_id, prefix, 0))
    positions = parity * row_count + jnp.arange(row_count, dtype=jnp.int32)
    key_positions = jnp.arange(2 * row_count, dtype=jnp.int32)
    score_scale = HEAD_DIM ** (-0.5)
    attn_width = HEADS * HEAD_DIM
    qkv_whole, out_whole, gains_low = (
        lax.all_gather(w_qkv, "fsdp", axis=0, tiled=True),
        lax.all_gather(w_out, "fsdp", axis=0, tiled=True),
        lax.all_gather(gains, "fsdp", axis=0, tiled=True),
    )
    gate_whole, up_whole, down_whole = (
        lax.all_gather(w_gate, "fsdp", axis=0, tiled=True),
        lax.all_gather(w_up, "fsdp", axis=0, tiled=True),
        lax.all_gather(w_down, "fsdp", axis=0, tiled=True),
    )
    gains_whole = gains_low.astype(jnp.float32)
    residual = tokens.astype(jnp.float32)
    normed_one, norm_one_back = jax.vjp(rms_scale, residual, gains_whole[:, 0])
    normed_one_low = normed_one.astype(jnp.bfloat16)
    projected = jnp.dot(normed_one_low, qkv_whole, preferred_element_type=jnp.float32)
    cosine, sine = rotary_tables(positions, HEAD_DIM)
    queries = rotary(
        projected[:, :attn_width].reshape(row_count, HEADS, HEAD_DIM),
        cosine[:, None, :],
        sine[:, None, :],
    ).astype(jnp.bfloat16)
    own_keys = rotary(projected[:, attn_width : attn_width + HEAD_DIM], cosine, sine).astype(
        jnp.bfloat16
    )
    own_values = projected[:, attn_width + HEAD_DIM :].astype(jnp.bfloat16)
    other_keys, other_values = swapped((own_keys, own_values), "fsdp", 0)
    leading = parity == 0
    all_keys = jnp.where(
        leading,
        jnp.concatenate([own_keys, other_keys], axis=0),
        jnp.concatenate([other_keys, own_keys], axis=0),
    )
    all_values = jnp.where(
        leading,
        jnp.concatenate([own_values, other_values], axis=0),
        jnp.concatenate([other_values, own_values], axis=0),
    )
    raw_scores = jnp.einsum("rhd,kd->hrk", queries, all_keys, preferred_element_type=jnp.float32)
    bent_scores = jnp.tanh(raw_scores * score_scale / soft_cap)
    capped = soft_cap * bent_scores
    allowed = (key_positions[None, :] <= positions[:, None]) | (key_positions[None, :] < prefix_len)
    capped = jnp.where(allowed[None], capped, masked_score)
    top_score = jnp.max(capped, axis=-1, keepdims=True)
    weights_exp = jnp.exp(capped - top_score)
    softmaxed = weights_exp / jnp.sum(weights_exp, axis=-1, keepdims=True)
    softmaxed_low = softmaxed.astype(jnp.bfloat16)
    attended = jnp.einsum(
        "hrk,kd->rhd", softmaxed_low, all_values, preferred_element_type=jnp.float32
    )
    attended = attended.reshape(row_count, attn_width).astype(jnp.bfloat16)
    branch_one = jnp.dot(attended, out_whole, preferred_element_type=jnp.float32)
    first_out, first_back = jax.vjp(rms_scale, branch_one, gains_whole[:, 1])
    hidden = residual + first_out
    normed_two, norm_two_back = jax.vjp(rms_scale, hidden, gains_whole[:, 2])
    normed_two_low = normed_two.astype(jnp.bfloat16)
    gate = jnp.dot(normed_two_low, gate_whole, preferred_element_type=jnp.float32)
    upward = jnp.dot(normed_two_low, up_whole, preferred_element_type=jnp.float32)
    active, active_back = jax.vjp(gated_product, gate, upward)
    active_low = active.astype(jnp.bfloat16)
    branch_two = jnp.dot(active_low, down_whole, preferred_element_type=jnp.float32)
    second_out, second_back = jax.vjp(rms_scale, branch_two, gains_whole[:, 3])
    final = hidden + second_out
    valid = (positions >= prefix_len).astype(jnp.float32)
    squares = jnp.stack(
        [
            jnp.sum(valid * jnp.sum(stream * stream, axis=-1))
            for stream in (residual, first_out, second_out, final)
        ]
    )
    total_squares, total_count = lax.psum((squares, jnp.sum(valid)), ("rep", "fsdp"))
    statistics = jnp.sqrt(total_squares / (total_count * D))
    qkv_back, out_back = qkv_whole, out_whole
    gate_back, up_back, down_back = gate_whole, up_whole, down_whole
    upstream = cotangent.astype(jnp.float32)
    d_branch_two, d_gain_three = second_back(upstream)
    d_branch_two_low = d_branch_two.astype(jnp.bfloat16)
    grad_down_part = jnp.einsum(
        "rf,rd->fd", active_low, d_branch_two_low, preferred_element_type=jnp.float32
    )
    d_active = jnp.einsum(
        "rd,fd->rf", d_branch_two_low, down_back, preferred_element_type=jnp.float32
    )
    d_gate, d_upward = active_back(d_active)
    d_gate_low = d_gate.astype(jnp.bfloat16)
    d_upward_low = d_upward.astype(jnp.bfloat16)
    grad_gate_part = jnp.einsum(
        "rd,rf->df", normed_two_low, d_gate_low, preferred_element_type=jnp.float32
    )
    grad_up_part = jnp.einsum(
        "rd,rf->df", normed_two_low, d_upward_low, preferred_element_type=jnp.float32
    )
    d_normed_two = jnp.einsum(
        "rf,df->rd", d_gate_low, gate_back, preferred_element_type=jnp.float32
    ) + jnp.einsum("rf,df->rd", d_upward_low, up_back, preferred_element_type=jnp.float32)
    d_hidden_norm, d_gain_two = norm_two_back(d_normed_two)
    d_hidden = upstream + d_hidden_norm
    d_branch_one, d_gain_one = first_back(d_hidden)
    d_branch_one_low = d_branch_one.astype(jnp.bfloat16)
    grad_out_part = jnp.einsum(
        "ra,rd->ad", attended, d_branch_one_low, preferred_element_type=jnp.float32
    )
    d_attended = jnp.einsum(
        "rd,ad->ra", d_branch_one_low, out_back, preferred_element_type=jnp.float32
    )
    d_attended = d_attended.astype(jnp.bfloat16).reshape(row_count, HEADS, HEAD_DIM)
    d_soft = jnp.einsum("rhd,kd->hrk", d_attended, all_values, preferred_element_type=jnp.float32)
    d_values_all = jnp.einsum(
        "hrk,rhd->kd", softmaxed_low, d_attended, preferred_element_type=jnp.float32
    )
    d_capped = softmaxed * (d_soft - jnp.sum(d_soft * softmaxed, axis=-1, keepdims=True))
    d_raw = (d_capped * (1.0 - bent_scores * bent_scores) * score_scale).astype(jnp.bfloat16)
    d_queries = jnp.einsum("hrk,kd->rhd", d_raw, all_keys, preferred_element_type=jnp.float32)
    d_keys_all = jnp.einsum("hrk,rhd->kd", d_raw, queries, preferred_element_type=jnp.float32)
    own_start = parity * row_count
    other_start = (1 - parity) * row_count
    returned_keys, returned_values = (
        swapped(
            lax.dynamic_slice_in_dim(d_keys_all, other_start, row_count, 0).astype(jnp.bfloat16),
            "fsdp",
            0,
        ).astype(jnp.float32),
        swapped(
            lax.dynamic_slice_in_dim(d_values_all, other_start, row_count, 0).astype(jnp.bfloat16),
            "fsdp",
            0,
        ).astype(jnp.float32),
    )
    d_keys = lax.dynamic_slice_in_dim(d_keys_all, own_start, row_count, 0) + returned_keys
    d_values = lax.dynamic_slice_in_dim(d_values_all, own_start, row_count, 0) + returned_values
    d_projected = jnp.concatenate(
        [
            rotary(d_queries, cosine[:, None, :], -sine[:, None, :]).reshape(row_count, attn_width),
            rotary(d_keys, cosine, -sine),
            d_values,
        ],
        axis=1,
    ).astype(jnp.bfloat16)
    grad_qkv_part = jnp.einsum(
        "rd,re->de", normed_one_low, d_projected, preferred_element_type=jnp.float32
    )
    d_normed_one = jnp.einsum(
        "re,de->rd", d_projected, qkv_back, preferred_element_type=jnp.float32
    )
    d_residual_norm, d_gain_zero = norm_one_back(d_normed_one)
    grad_tokens = d_hidden + d_residual_norm
    grad_gains_part = jnp.stack([d_gain_zero, d_gain_one, d_gain_two, d_gain_three], axis=1)
    reduced = (
        lax.psum_scatter(grad_qkv_part.astype(jnp.bfloat16), "fsdp", scatter_dimension=0, tiled=True),
        lax.psum_scatter(grad_out_part.astype(jnp.bfloat16), "fsdp", scatter_dimension=0, tiled=True),
        lax.psum_scatter(grad_gate_part.astype(jnp.bfloat16), "fsdp", scatter_dimension=0, tiled=True),
        lax.psum_scatter(grad_up_part.astype(jnp.bfloat16), "fsdp", scatter_dimension=0, tiled=True),
        lax.psum_scatter(grad_down_part.astype(jnp.bfloat16), "fsdp", scatter_dimension=0, tiled=True),
        lax.psum_scatter(grad_gains_part, "fsdp", scatter_dimension=0, tiled=True),
    )
    reduced = lax.psum(
        tuple(term.astype(jnp.float32) for term in reduced), "rep"
    )
    moments = (moment_qkv, moment_out, moment_gate, moment_up, moment_down)
    weight_shards = (w_qkv, w_out, w_gate, w_up, w_down)
    lanes = fsdp_size // GROUP
    if lanes > 1:
        teams = [[member * lanes + lane for lane in range(lanes)] for member in range(GROUP)]

        def joined(shard):
            return lax.all_gather(shard, "fsdp", axis=0, tiled=True, axis_index_groups=teams)

        def parted(block):
            size = block.shape[0] // lanes
            start = lax.rem(fsdp_place, lanes) * size
            return lax.dynamic_slice_in_dim(block, start, size, 0)
    else:

        def joined(shard):
            return shard

        def parted(block):
            return block

    new_moments, masters = muon(
        [joined(term) for term in reduced[:5]],
        [joined(term) for term in moments],
        [joined(term) for term in weight_shards],
    )
    new_moments = [parted(term) for term in new_moments]
    masters = [parted(term) for term in masters]
    gain_grad = reduced[5]
    gains_local = gains.astype(jnp.float32)
    first_new = first_decay * gain_first + (1.0 - first_decay) * gain_grad
    second_new = second_decay * gain_second + (1.0 - second_decay) * gain_grad * gain_grad
    first_hat = first_new / (1.0 - first_decay**ADAM_STEP)
    second_hat = second_new / (1.0 - second_decay**ADAM_STEP)
    master_gains = gains_local - adam_rate * (
        first_hat / (jnp.sqrt(second_hat) + adam_epsilon) + weight_decay * gains_local
    )
    return (
        final,
        grad_tokens,
        reduced[0],
        reduced[1],
        reduced[2],
        reduced[3],
        reduced[4],
        gain_grad,
        new_moments[0],
        new_moments[1],
        new_moments[2],
        new_moments[3],
        new_moments[4],
        masters[0],
        masters[1],
        masters[2],
        masters[3],
        masters[4],
        first_new,
        second_new,
        master_gains,
        statistics,
    )


def solution(mesh):
    in_specs = (
        P(("rep", "fsdp"), None),
        P(("rep", "fsdp"), None),
        P(),
        P("fsdp", None),
        P("fsdp", None),
        P("fsdp", None),
        P("fsdp", None),
        P("fsdp", None),
        P("fsdp", None),
        P("fsdp", None),
        P("fsdp", None),
        P("fsdp", None),
        P("fsdp", None),
        P("fsdp", None),
        P("fsdp", None),
        P("fsdp", None),
    )
    out_specs = (
        P(("rep", "fsdp"), None),
        P(("rep", "fsdp"), None),
        P("fsdp", None),
        P("fsdp", None),
        P("fsdp", None),
        P("fsdp", None),
        P("fsdp", None),
        P("fsdp", None),
        P("fsdp", None),
        P("fsdp", None),
        P("fsdp", None),
        P("fsdp", None),
        P("fsdp", None),
        P("fsdp", None),
        P("fsdp", None),
        P("fsdp", None),
        P("fsdp", None),
        P("fsdp", None),
        P("fsdp", None),
        P("fsdp", None),
        P("fsdp", None),
        P(),
    )
    return jax.shard_map(shards, mesh=mesh, in_specs=in_specs, out_specs=out_specs, check_vma=False)
```

```python
import jax
import jax.numpy as jnp
from jax import lax
from jax.experimental import pallas as pl
from jax.experimental.pallas import tpu as pltpu
from jax.sharding import PartitionSpec as P

HEADS = 4
HEAD_DIM = 256
NS_STEPS = 5
ADAM_STEP = 10


norm_epsilon = 1e-06
soft_cap = 50.0
rotary_base = 10000.0
newton_first = 3.4445
newton_second = -4.775
newton_third = 2.0315
momentum_decay = 0.95
muon_rate = 1.0
first_decay = 0.9
second_decay = 0.95
adam_rate = 1.0
weight_decay = 0.1
adam_epsilon = 1e-08
frobenius_epsilon = 1e-07

GROUP = 8
MESH = pl.DeviceIdType.MESH
f32 = jnp.float32
bf16 = jnp.bfloat16


def dot(a, b):
    return lax.dot_general(a, b, (((1,), (0,)), ((), ())), preferred_element_type=f32)


def dot_nt(a, b):
    return lax.dot_general(a, b, (((1,), (1,)), ((), ())), preferred_element_type=f32)


def dot_tn(a, b):
    return lax.dot_general(a, b, (((0,), (0,)), ((), ())), preferred_element_type=f32)


def place():
    size = lax.axis_size("fsdp")
    lanes = size // GROUP
    here = lax.axis_index("fsdp")
    return lax.axis_index("rep"), here // lanes, lax.rem(here, lanes), lanes


def rotary_tables(positions, head_dim):
    half_dim = head_dim // 2
    frequency = rotary_base ** (-(jnp.arange(half_dim, dtype=f32) * 2.0 / head_dim))
    angles = positions.astype(f32)[:, None] * frequency[None, :]
    return (jnp.cos(angles), jnp.sin(angles))


QKV, OUT, GATE, UP, DOWN = range(5)
CORE, ACROSS, ALONG = 1, 2, 4
PAIRS = (
    ((GATE, 0), (UP, 0)),
    ((DOWN, 0), (GATE, 1)),
    ((UP, 1), (DOWN, 1)),
    ((OUT, 0), (OUT, 1)),
    ((QKV, 0), (QKV, 1)),
)
CHUNK = 128
TILE = 256


def split_shape(number, shape):
    rows, cols = shape
    return (rows // 2, cols) if number in (OUT, DOWN) else (rows, cols // 2)


def layer_names(rows, keys, width, shapes, reps):
    halves = [split_shape(number, shape) for number, shape in enumerate(shapes)]
    feats = HEADS * HEAD_DIM
    inner = shapes[GATE][1]
    spaces = {}
    for number, (height, cols) in enumerate(shapes):
        spaces[f"whole{number}"] = pltpu.VMEM((height * GROUP, cols), bf16)
    spaces.update(
        gain_parts=pltpu.VMEM((GROUP, 8, width), f32),
        gains=pltpu.VMEM((8, width), f32),
        normed=pltpu.VMEM((rows, width), bf16),
        one_t=pltpu.VMEM((width, rows), bf16),
        two_t=pltpu.VMEM((width, rows), bf16),
        proj=pltpu.VMEM((rows, feats + 2 * HEAD_DIM), bf16),
        key=pltpu.VMEM((keys, HEAD_DIM), bf16),
        value=pltpu.VMEM((keys, HEAD_DIM), bf16),
        key_t=pltpu.VMEM((HEAD_DIM, keys), bf16),
        value_t=pltpu.VMEM((HEAD_DIM, keys), bf16),
        att=pltpu.VMEM((rows, feats), bf16),
        att_t=pltpu.VMEM((feats, rows), bf16),
        inverse=pltpu.VMEM((8, rows), f32),
        branch=pltpu.VMEM((rows, width), f32),
        hidden=pltpu.VMEM((rows, width), f32),
        slope=pltpu.VMEM((rows, inner), bf16),
        bend=pltpu.VMEM((rows, inner), bf16),
        active=pltpu.VMEM((rows, inner), bf16),
        d_key=pltpu.VMEM((keys, HEAD_DIM), f32),
        d_value=pltpu.VMEM((keys, HEAD_DIM), f32),
        swap_out=pltpu.VMEM((2, rows, HEAD_DIM), bf16),
        swap_in=pltpu.VMEM((2, rows, HEAD_DIM), bf16),
        squares=pltpu.VMEM((8, width), f32),
        d_gains=pltpu.VMEM((8, width), f32),
        small_parts=pltpu.VMEM((GROUP, 8, width), f32),
        small_reps=pltpu.VMEM((reps, 8, width), f32),
    )
    for number, half in enumerate(halves):
        spaces[f"stage{number}"] = pltpu.VMEM((2, 2, 2, 2) + half, bf16)
        spaces[f"chip{number}"] = pltpu.VMEM((2, 2, 2) + half, bf16)
        spaces[f"pair{number}"] = pltpu.VMEM((2, 2) + half, bf16)
        spaces[f"plane{number}"] = pltpu.VMEM((2,) + half, bf16)
        spaces[f"line{number}"] = pltpu.VMEM((2, 2) + half, bf16)
        spaces[f"total{number}"] = pltpu.VMEM((2,) + half, bf16)
    dma = pltpu.SemaphoreType.DMA
    spaces.update(
        own_sem=dma((5,)),
        result_sem=dma((5,)),
        weight_send=dma((5, 9)),
        weight_recv=dma((5, 9)),
        gain_send=dma((GROUP,)),
        gain_recv=dma((GROUP,)),
        key_send=dma((2,)),
        key_recv=dma((2,)),
        swap_send=dma((1,)),
        swap_recv=dma((1,)),
        chip_send=dma((5, 2)),
        chip_recv=dma((5, 2)),
        pair_send=dma((5, 2)),
        pair_recv=dma((5, 2)),
        plane_send=dma((5, 2)),
        plane_recv=dma((5, 2)),
        line_send=dma((5, 2)),
        line_recv=dma((5, 2, 2)),
        total_send=dma((5, 2, 2)),
        total_recv=dma((5, 2)),
        small_send=dma((GROUP,)),
        small_recv=dma((GROUP,)),
        reps_send=dma((reps,)),
        reps_recv=dma((reps,)),
    )
    return spaces


class Refs:
    def __init__(self, names, refs):
        self.__dict__.update(zip(names, refs))


def column_sum(x):
    return jnp.sum(x, axis=0, keepdims=True)


def row_mean(x):
    return jnp.mean(x, axis=-1, keepdims=True)


def layer_kernel(names, shapes, *refs):
    v = Refs(names, refs)
    rep, me, lane, lanes = place()
    reps = lax.axis_size("rep")
    here = lax.axis_index("fsdp")
    core, across, along = me % 2, (me // 2) % 2, me // 4
    rows, width = v.tokens.shape
    parity = here % 2
    weights = [v.w_qkv, v.w_out, v.w_gate, v.w_up, v.w_down]
    named = lambda name: [getattr(v, f"{name}{number}") for number in range(5)]
    whole, stage, chip, pair = named("whole"), named("stage"), named("chip"), named("pair")
    plane, line, total, result = named("plane"), named("line"), named("total"), named("grad")

    def device(member):
        return (rep, member * lanes + lane)

    def remote(src, dst, send, recv, where):
        return pltpu.make_async_remote_copy(
            src_ref=src,
            dst_ref=dst,
            send_sem=send,
            recv_sem=recv,
            device_id=where,
            device_id_type=MESH,
        )

    barrier = pltpu.get_barrier_semaphore()
    greeted = [device(me ^ step) for step in range(1, GROUP)]
    greeted += [(lax.rem(rep + step, reps), here) for step in range(1, reps)]
    if lanes > 1:
        greeted.append((rep, here ^ 1))
    for where in greeted:
        pl.semaphore_signal(barrier, inc=1, device_id=where, device_id_type=MESH)
    pl.semaphore_wait(barrier, len(greeted))

    def slot(number, member):
        height = shapes[number][0]
        return whole[number].at[pl.ds(pl.multiple_of(member * height, 16), height), :]

    def half_slot(number, member, half):
        height, cols = split_shape(number, shapes[number])
        start = pl.multiple_of(member * shapes[number][0], 16)
        if number in (OUT, DOWN):
            return whole[number].at[pl.ds(start + half * height, height), :]
        return whole[number].at[pl.ds(start, height), pl.ds(half * cols, cols)]

    def weight_copy(number, kind):
        beside, ahead = me ^ ACROSS, me ^ ALONG
        if kind < 3:
            where = me ^ (CORE, ACROSS, ALONG)[kind]
            src, dst = weights[number], slot(number, me)
        else:
            src = (
                half_slot(number, beside, 0),
                half_slot(number, ahead, 1),
                slot(number, beside),
                slot(number, ahead),
                half_slot(number, beside ^ ALONG, 0),
                half_slot(number, beside ^ ALONG, 1),
            )[kind - 3]
            dst = src
            where = (ahead, beside)[kind - 3] if kind < 5 else me ^ CORE
        return remote(
            src,
            dst,
            v.weight_send.at[number, kind],
            v.weight_recv.at[number, kind],
            device(where),
        )

    def own_copy(number):
        return pltpu.make_async_copy(weights[number], slot(number, me), v.own_sem.at[number])

    def weight_begin(number):
        for kind in (1, 2, 0):
            weight_copy(number, kind).start()
        own_copy(number).start()

    def weight_forward(number):
        weight_copy(number, 1).wait_recv()
        weight_copy(number, 3).start()
        weight_copy(number, 5).start()
        weight_copy(number, 2).wait_recv()
        weight_copy(number, 4).start()
        weight_copy(number, 6).start()

    def weight_corner(number):
        weight_copy(number, 3).wait_recv()
        weight_copy(number, 7).start()
        weight_copy(number, 4).wait_recv()
        weight_copy(number, 8).start()

    def weight_ready(number):
        own_copy(number).wait()
        for kind in (0, 5, 6, 7, 8):
            weight_copy(number, kind).wait_recv()

    weight_begin(QKV)
    weight_begin(OUT)

    def gain_copy(step):
        return remote(
            v.gain_parts.at[me],
            v.gain_parts.at[me],
            v.gain_send.at[step],
            v.gain_recv.at[step],
            device(me ^ step),
        )

    v.gain_parts[me] = v.gain_part[...]
    for step in range(1, GROUP):
        gain_copy(step).start()
    weight_begin(GATE)
    v.squares[...] = jnp.zeros_like(v.squares)
    v.d_gains[...] = jnp.zeros_like(v.d_gains)
    v.d_key[...] = jnp.zeros_like(v.d_key)
    v.d_value[...] = jnp.zeros_like(v.d_value)
    for step in range(1, GROUP):
        gain_copy(step).wait_recv()
    v.gains[...] = jnp.sum(v.gain_parts[...], axis=0)

    prefix = v.prefix[0]

    def valid_rows(start, count):
        spot = lax.broadcasted_iota(jnp.int32, (count, 1), 0) + (parity * rows + start)
        return jnp.where(spot >= prefix, 1.0, 0.0)

    def by_rows(body):
        @pl.loop(0, rows // CHUNK)
        def _(k):
            start = pl.multiple_of(k * CHUNK, CHUNK)
            body(pl.ds(start, CHUNK), start)

    def by_columns(count, body):
        @pl.loop(0, count // TILE)
        def _(k):
            body(pl.ds(pl.multiple_of(k * TILE, TILE), TILE), k)

    def inverse_root(x):
        return lax.rsqrt(row_mean(x * x) + norm_epsilon)

    def norm_back(x, scale, upstream, gain, row):
        v.d_gains[row : row + 1, :] += column_sum(upstream * x * scale)
        spread = upstream * gain
        return scale * spread - x * (scale * scale * scale * row_mean(x * spread))

    gain_row = lambda k: v.gains[k : k + 1, :]

    def first_norm(here_rows, start):
        x = v.tokens[here_rows, :].astype(f32)
        normed = x * inverse_root(x) * gain_row(0)
        v.normed[here_rows, :] = normed.astype(bf16)
        v.one_t[:, here_rows] = normed.T.astype(bf16)
        v.squares[0:1, :] += column_sum(valid_rows(start, CHUNK) * (x * x))

    by_rows(first_norm)
    weight_forward(QKV)
    weight_corner(QKV)
    weight_ready(QKV)

    feats = HEADS * HEAD_DIM
    half_dim = HEAD_DIM // 2
    own_rows = pl.ds(pl.multiple_of(parity * rows, rows), rows)
    other_rows = pl.ds(pl.multiple_of((1 - parity) * rows, rows), rows)

    def rotate(x, sign):
        first, second = x[:, :half_dim], x[:, half_dim:]
        cosine, sine = v.cosine[...], v.sine[...] * sign
        return first * cosine - second * sine, second * cosine + first * sine

    def key_copy(number):
        ref = (v.key, v.value)[number]
        return remote(
            ref.at[own_rows, :],
            ref.at[own_rows, :],
            v.key_send.at[number],
            v.key_recv.at[number],
            (rep, here ^ 1),
        )

    key_part = dot(v.normed[...], whole[QKV][:, feats : feats + HEAD_DIM])
    first, second = rotate(key_part, 1.0)
    v.key[own_rows, :half_dim] = first.astype(bf16)
    v.key[own_rows, half_dim:] = second.astype(bf16)
    key_copy(0).start()
    v.value[own_rows, :] = dot(v.normed[...], whole[QKV][:, feats + HEAD_DIM :]).astype(bf16)
    key_copy(1).start()

    @pl.loop(0, HEADS)
    def _(head):
        start = pl.multiple_of(head * HEAD_DIM, HEAD_DIM)
        part = dot(v.normed[...], whole[QKV][:, pl.ds(start, HEAD_DIM)])
        first, second = rotate(part, 1.0)
        v.proj[:, pl.ds(start, half_dim)] = first.astype(bf16)
        v.proj[:, pl.ds(start + half_dim, half_dim)] = second.astype(bf16)

    weight_forward(OUT)
    weight_begin(UP)
    for number in range(2):
        key_copy(number).wait_recv()
    v.key_t[...] = v.key[...].astype(f32).T.astype(bf16)
    v.value_t[...] = v.value[...].astype(f32).T.astype(bf16)

    keys = v.key.shape[0]
    bend_scale = HEAD_DIM ** (-0.5) / soft_cap

    def scores(head, start):
        here_rows = pl.ds(start, TILE)
        query = v.proj[here_rows, head * HEAD_DIM : (head + 1) * HEAD_DIM]
        bent = jnp.tanh(dot_nt(v.key[...], query) * bend_scale)
        spot = lax.broadcasted_iota(jnp.int32, (1, TILE), 1) + (parity * rows + start)
        last = jnp.maximum(spot, prefix - 1)
        allowed = lax.broadcasted_iota(jnp.int32, (keys, TILE), 0) <= last
        return bent, jnp.where(allowed, jnp.exp(soft_cap * bent), 0.0), query

    def attend(head):
        cols = slice(head * HEAD_DIM, (head + 1) * HEAD_DIM)

        @pl.loop(0, rows // TILE)
        def _(k):
            start = pl.multiple_of(k * TILE, TILE)
            here_rows = pl.ds(start, TILE)
            _, power, _ = scores(head, start)
            inverse = 1.0 / column_sum(power)
            v.inverse[head : head + 1, here_rows] = inverse
            mixed = dot(v.value_t[...], (power * inverse).astype(bf16))
            v.att_t[cols, here_rows] = mixed.astype(bf16)
            v.att[here_rows, cols] = mixed.T.astype(bf16)

    attend(0)
    weight_corner(OUT)
    weight_forward(GATE)
    weight_begin(DOWN)
    attend(1)
    attend(2)
    weight_corner(GATE)
    weight_forward(UP)
    attend(3)
    weight_ready(OUT)

    v.branch[...] = dot(v.att[...], whole[OUT][...])

    def second_norm(here_rows, start):
        x = v.branch[here_rows, :]
        first_out = x * inverse_root(x) * gain_row(1)
        hidden = v.tokens[here_rows, :].astype(f32) + first_out
        v.hidden[here_rows, :] = hidden
        normed = hidden * inverse_root(hidden) * gain_row(2)
        v.normed[here_rows, :] = normed.astype(bf16)
        v.two_t[:, here_rows] = normed.T.astype(bf16)
        v.squares[1:2, :] += column_sum(valid_rows(start, CHUNK) * (first_out * first_out))

    by_rows(second_norm)
    weight_ready(GATE)
    weight_corner(UP)
    weight_ready(UP)
    weight_forward(DOWN)
    inner = shapes[GATE][1]

    def feed(cols, k):
        gate = dot(v.normed[...], whole[GATE][:, cols])
        upward = dot(v.normed[...], whole[UP][:, cols])
        square = gate * gate
        bent = jnp.tanh(0.7978845608028654 * (gate + 0.044715 * gate * square))
        open_half = 0.5 * (1.0 + bent)
        smooth = gate * open_half
        steep = open_half + gate * (1.0 - bent * bent) * (
            0.3989422804014327 * (1.0 + 3.0 * 0.044715 * square)
        )
        v.active[:, cols] = (smooth * upward).astype(bf16)
        v.bend[:, cols] = smooth.astype(bf16)
        v.slope[:, cols] = (steep * upward).astype(bf16)

    by_columns(inner, feed)
    weight_corner(DOWN)
    weight_ready(DOWN)

    v.d_tokens[...] = dot(v.active[...], whole[DOWN][...])

    def last_norm(here_rows, start):
        x = v.d_tokens[here_rows, :]
        scale = inverse_root(x)
        second_out = x * scale * gain_row(3)
        final = v.hidden[here_rows, :] + second_out
        v.output[here_rows, :] = final
        valid = valid_rows(start, CHUNK)
        v.squares[2:3, :] += column_sum(valid * (second_out * second_out))
        v.squares[3:4, :] += column_sum(valid * (final * final))
        upstream = v.cotangent[here_rows, :].astype(f32)
        v.normed[here_rows, :] = norm_back(x, scale, upstream, gain_row(3), 3).astype(bf16)

    by_rows(last_norm)

    def first_across(number, half):
        return any(one == (number, half) for one, _ in PAIRS)

    def chip_copy(number, half):
        return remote(
            stage[number].at[half, :, :, 1 - core],
            chip[number].at[half],
            v.chip_send.at[number, half],
            v.chip_recv.at[number, half],
            device(me ^ CORE),
        )

    def pair_copy(number, half):
        if first_across(number, half):
            src, where = chip[number].at[half, :, 1 - across], me ^ ACROSS
        else:
            src, where = chip[number].at[half, 1 - along], me ^ ALONG
        return remote(
            src,
            pair[number].at[half],
            v.pair_send.at[number, half],
            v.pair_recv.at[number, half],
            device(where),
        )

    def plane_copy(number, half):
        if first_across(number, half):
            src, where = pair[number].at[half, 1 - along], me ^ ALONG
        else:
            src, where = pair[number].at[half, 1 - across], me ^ ACROSS
        return remote(
            src,
            plane[number].at[half],
            v.plane_send.at[number, half],
            v.plane_recv.at[number, half],
            device(where),
        )

    def added(one, two):
        return (one.astype(f32) + two.astype(f32)).astype(bf16)

    def chip_begin(number, half):
        chip_copy(number, half).start()

    def chip_end(number, half):
        chip_copy(number, half).wait_recv()

        @pl.loop(0, 4)
        def _(k):
            one, two = k // 2, k % 2
            chip[number][half, one, two] = added(
                chip[number][half, one, two], stage[number][half, one, two, core]
            )

        pair_copy(number, half).start()

    def pair_end(number, half):
        pair_copy(number, half).wait_recv()

        @pl.loop(0, 2)
        def _(k):
            if first_across(number, half):
                mine = chip[number][half, k, across]
            else:
                mine = chip[number][half, along, k]
            pair[number][half, k] = added(pair[number][half, k], mine)

        plane_copy(number, half).start()

    def plane_end(number, half):
        plane_copy(number, half).wait_recv()
        kept = along if first_across(number, half) else across
        plane[number][half] = added(plane[number][half], pair[number][half, kept])

    order = [half for both in PAIRS for half in both]

    def sum_owner(number, half):
        return order.index((number, half)) % reps

    def line_copy(number, half):
        owner = sum_owner(number, half)
        side = jnp.where(rep < owner, 0, 1)
        return remote(
            plane[number].at[half],
            line[number].at[half, side],
            v.line_send.at[number, half],
            v.line_recv.at[number, half, side],
            (rep + 1 - 2 * side, here),
        )

    def line_wait(number, half, side):
        remote(
            plane[number].at[half],
            line[number].at[half, side],
            v.line_send.at[number, half],
            v.line_recv.at[number, half, side],
            (lax.rem(rep + 1, reps), here),
        ).wait_recv()

    inside = (rep > 0) & (rep < reps - 1)

    def line_begin(number, half):
        owner = sum_owner(number, half)

        @pl.when(rep != owner)
        def _():
            side = jnp.where(rep < owner, 0, 1)

            @pl.when(inside)
            def _():
                line_wait(number, half, side)
                plane[number][half] = added(plane[number][half], line[number][half, side])

            line_copy(number, half).start()

    def total_copy(number, half, way, step):
        return remote(
            total[number].at[half],
            total[number].at[half],
            v.total_send.at[number, half, way],
            v.total_recv.at[number, half],
            (rep + step, here),
        )

    def owner_ways(owner):
        return [w for w, there in ((0, owner > 0), (1, owner < reps - 1)) if there]

    def line_end(number, half):
        owner = sum_owner(number, half)

        @pl.when(rep == owner)
        def _():
            summed = plane[number][half].astype(f32)
            for side in owner_ways(owner):
                line_wait(number, half, side)
                summed = summed + line[number][half, side].astype(f32)
            total[number][half] = summed.astype(bf16)
            for way in owner_ways(owner):
                total_copy(number, half, way, 2 * way - 1).start()

    def total_end(number, half):
        owner = sum_owner(number, half)

        @pl.when(rep != owner)
        def _():
            away = jnp.where(rep < owner, -1, 1)
            total_copy(number, half, 0, away).wait_recv()

            @pl.when(inside)
            def _():
                total_copy(number, half, 0, away).start()

    def for_pair(action, index):
        for number, half in PAIRS[index]:
            action(number, half)

    def keep_columns(number, col_half, col, found):
        height = shapes[number][0]
        for member in range(GROUP):
            stage[number][
                col_half, member // 4, (member // 2) % 2, member % 2, :, pl.ds(col, TILE)
            ] = found[member * height : (member + 1) * height].astype(bf16)

    down_rows = shapes[DOWN][0]
    halved = inner // 2 // TILE

    def feed_back(side):
        @pl.loop(0, halved)
        def _(k):
            col = pl.multiple_of(k * TILE, TILE)
            start = pl.multiple_of(side * (inner // 2) + k * TILE, TILE)
            cols = pl.ds(start, TILE)
            d_active = dot_nt(v.normed[...], whole[DOWN][cols, :])
            d_gate = (d_active * v.slope[:, cols].astype(f32)).astype(bf16)
            d_upward = (d_active * v.bend[:, cols].astype(f32)).astype(bf16)
            v.slope[:, cols] = d_gate
            v.bend[:, cols] = d_upward
            keep_columns(GATE, side, col, dot(v.two_t[...], d_gate))
            keep_columns(UP, side, col, dot(v.two_t[...], d_upward))
            found = dot_tn(v.active[:, cols], v.normed[...]).astype(bf16)
            per = TILE // down_rows
            for part in range(per):
                member = (side * halved + k) * per + part
                y, x, c = member // 4, (member // 2) % 2, member % 2
                base = part * down_rows
                stage[DOWN][0, y, x, c] = found[base : base + down_rows // 2]
                stage[DOWN][1, y, x, c] = found[base + down_rows // 2 : base + down_rows]

    feed_back(0)
    for_pair(chip_begin, 0)
    feed_back(1)
    for_pair(chip_begin, 1)
    for_pair(chip_begin, 2)
    for_pair(chip_end, 0)
    v.d_tokens[...] = dot_nt(v.slope[...], whole[GATE][...]) + dot_nt(
        v.bend[...], whole[UP][...]
    )
    for_pair(chip_end, 1)

    def middle_norms(here_rows, start):
        x = v.hidden[here_rows, :]
        flow = norm_back(x, inverse_root(x), v.d_tokens[here_rows, :], gain_row(2), 2)
        d_hidden = v.cotangent[here_rows, :].astype(f32) + flow
        v.d_tokens[here_rows, :] = d_hidden
        x = v.branch[here_rows, :]
        flow = norm_back(x, inverse_root(x), d_hidden, gain_row(1), 1)
        v.normed[here_rows, :] = flow.astype(bf16)

    by_rows(middle_norms)
    for_pair(chip_end, 2)
    out_rows = shapes[OUT][0]
    v.att[...] = dot_nt(v.normed[...], whole[OUT][...]).astype(bf16)

    @pl.loop(0, GROUP // 2)
    def _(k):
        start = pl.multiple_of(k * 2 * out_rows, 2 * out_rows)
        found = dot(v.att_t[pl.ds(start, 2 * out_rows), :], v.normed[...]).astype(bf16)
        for part in range(4):
            stage[OUT][part % 2, k // 2, k % 2, part // 2] = found[
                part * (out_rows // 2) : (part + 1) * (out_rows // 2)
            ]

    for_pair(chip_begin, 3)

    def attend_back(head):
        cols = slice(head * HEAD_DIM, (head + 1) * HEAD_DIM)

        @pl.loop(0, rows // TILE)
        def _(k):
            start = pl.multiple_of(k * TILE, TILE)
            here_rows = pl.ds(start, TILE)
            bent, power, query = scores(head, start)
            soft = power * v.inverse[head : head + 1, here_rows]
            flow = v.att[here_rows, cols]
            d_soft = dot_nt(v.value[...], flow)
            v.d_value[...] += dot(soft.astype(bf16), flow)
            level = column_sum(d_soft * soft)
            d_raw = soft * (d_soft - level) * ((1.0 - bent * bent) * HEAD_DIM ** (-0.5))
            d_raw = d_raw.astype(bf16)
            v.d_key[...] += dot(d_raw, query)
            d_query = dot(v.key_t[...], d_raw).T
            first, second = d_query[:, :half_dim], d_query[:, half_dim:]
            cosine, sine = v.cosine[here_rows, :], v.sine[here_rows, :]
            base = head * HEAD_DIM
            v.proj[here_rows, base : base + half_dim] = (first * cosine + second * sine).astype(
                bf16
            )
            v.proj[here_rows, base + half_dim : base + HEAD_DIM] = (
                second * cosine - first * sine
            ).astype(bf16)

    swap = remote(
        v.swap_out,
        v.swap_in,
        v.swap_send.at[0],
        v.swap_recv.at[0],
        (rep, here ^ 1),
    )

    attend_back(0)
    for_pair(chip_end, 3)
    for_pair(pair_end, 0)
    attend_back(1)
    for_pair(pair_end, 1)
    for_pair(plane_end, 0)
    for_pair(line_begin, 0)
    attend_back(2)
    for_pair(pair_end, 2)
    for_pair(plane_end, 1)
    for_pair(line_begin, 1)
    for_pair(line_end, 0)
    attend_back(3)
    v.swap_out[0] = v.d_key[other_rows, :].astype(bf16)
    v.swap_out[1] = v.d_value[other_rows, :].astype(bf16)
    swap.start()
    for_pair(pair_end, 3)
    for_pair(plane_end, 2)
    for_pair(line_begin, 2)
    for_pair(line_end, 1)
    for_pair(total_end, 0)

    qkv_half = split_shape(QKV, shapes[QKV])[1] // TILE

    def projection_grad(tile):
        found = dot(v.one_t[...], v.proj[:, tile * TILE : (tile + 1) * TILE])
        keep_columns(QKV, tile // qkv_half, (tile % qkv_half) * TILE, found)

    for tile in range(qkv_half):
        projection_grad(tile)
    chip_begin(QKV, 0)
    swap.wait_recv()
    d_key = v.d_key[own_rows, :] + v.swap_in[0].astype(f32)
    first, second = rotate(d_key, -1.0)
    v.proj[:, feats : feats + half_dim] = first.astype(bf16)
    v.proj[:, feats + half_dim : feats + HEAD_DIM] = second.astype(bf16)
    v.proj[:, feats + HEAD_DIM :] = (
        v.d_value[own_rows, :] + v.swap_in[1].astype(f32)
    ).astype(bf16)
    for tile in range(qkv_half, 2 * qkv_half):
        projection_grad(tile)
    chip_begin(QKV, 1)
    for_pair(chip_end, 4)
    v.branch[...] = dot_nt(v.proj[...], whole[QKV][...])

    def first_norm_back(here_rows, start):
        x = v.tokens[here_rows, :].astype(f32)
        flow = norm_back(x, inverse_root(x), v.branch[here_rows, :], gain_row(0), 0)
        v.d_tokens[here_rows, :] += flow

    by_rows(first_norm_back)

    def small_copy(step):
        return remote(
            v.small_parts.at[me],
            v.small_parts.at[me],
            v.small_send.at[step],
            v.small_recv.at[step],
            device(me ^ step),
        )

    def reps_copy(step):
        return remote(
            v.small_reps.at[rep],
            v.small_reps.at[rep],
            v.reps_send.at[step],
            v.reps_recv.at[step],
            (lax.rem(rep + step, reps), here),
        )

    spot = lax.broadcasted_iota(jnp.int32, (1, width), 1)
    numbers = jnp.where(spot == 4, column_sum(valid_rows(0, rows)), 0.0)
    for k in range(4):
        summed = jnp.sum(v.squares[k : k + 1, :], axis=1, keepdims=True)
        numbers = numbers + jnp.where(spot == k, summed, 0.0)
    v.d_gains[4:5, :] = numbers
    v.small_parts[me] = v.d_gains[...]
    for step in range(1, GROUP):
        small_copy(step).start()
    for_pair(pair_end, 4)
    for_pair(plane_end, 3)
    for_pair(line_begin, 3)
    for_pair(line_end, 2)
    for_pair(total_end, 1)
    for step in range(1, GROUP):
        small_copy(step).wait_recv()
    v.small_reps[rep] = jnp.sum(v.small_parts[...], axis=0)
    for step in range(1, reps):
        reps_copy(step).start()
    for_pair(plane_end, 4)
    for_pair(line_begin, 4)
    for_pair(line_end, 3)
    for_pair(total_end, 2)
    for_pair(line_end, 4)
    for_pair(total_end, 3)
    for_pair(total_end, 4)
    for step in range(1, reps):
        reps_copy(step).wait_recv()
    v.small[...] = jnp.sum(v.small_reps[...], axis=0)
    results = [
        pltpu.make_async_copy(total[number], result[number], v.result_sem.at[number])
        for number in range(5)
    ]
    for copy in results:
        copy.start()

    for number in range(5):
        for kind in range(9):
            weight_copy(number, kind).wait_send()
    for number in range(2):
        key_copy(number).wait_send()
    swap.wait_send()
    for step in range(1, GROUP):
        gain_copy(step).wait_send()
        small_copy(step).wait_send()
    for step in range(1, reps):
        reps_copy(step).wait_send()
    for number, half in order:
        chip_copy(number, half).wait_send()
        pair_copy(number, half).wait_send()
        plane_copy(number, half).wait_send()
        owner = sum_owner(number, half)

        @pl.when(rep != owner)
        def _():
            line_copy(number, half).wait_send()

            @pl.when(inside)
            def _():
                total_copy(number, half, 0, jnp.where(rep < owner, -1, 1)).wait_send()

        @pl.when(rep == owner)
        def _():
            for way in owner_ways(owner):
                total_copy(number, half, way, 2 * way - 1).wait_send()

    for copy in results:
        copy.wait()


def layer(prefix, tokens, cotangent, cosine, sine, gain_part, weights, reps):
    shapes = tuple(w.shape for w in weights)
    rows, width = tokens.shape
    spaces = layer_names(rows, 2 * rows, width, shapes, reps)
    halves = [split_shape(number, shape) for number, shape in enumerate(shapes)]
    inputs = ["prefix", "tokens", "cotangent", "cosine", "sine", "gain_part"]
    inputs += ["w_qkv", "w_out", "w_gate", "w_up", "w_down"]
    outputs = ["output", "d_tokens", "small"] + [f"grad{number}" for number in range(5)]
    vmem = pl.BlockSpec(memory_space=pltpu.VMEM)
    names = inputs + outputs + list(spaces)
    out = pl.pallas_call(
        lambda *refs: layer_kernel(names, shapes, *refs),
        out_shape=[
            jax.ShapeDtypeStruct((rows, width), f32),
            jax.ShapeDtypeStruct((rows, width), f32),
            jax.ShapeDtypeStruct((8, width), f32),
        ]
        + [jax.ShapeDtypeStruct((2,) + half, bf16) for half in halves],
        in_specs=[pl.BlockSpec(memory_space=pltpu.SMEM)]
        + [vmem] * 5
        + [pl.BlockSpec(memory_space=pl.ANY)] * 5,
        out_specs=[vmem] * 3 + [pl.BlockSpec(memory_space=pl.ANY)] * 5,
        scratch_shapes=list(spaces.values()),
        compiler_params=pltpu.CompilerParams(
            collective_id=2, has_side_effects=True, vmem_limit_bytes=64 * 2**20
        ),
        name="layer",
    )(prefix, tokens, cotangent, cosine, sine, gain_part, *weights)
    return out[0], out[1], out[2], out[3:]


OWNERS = (6, 7, 0, 2, 4)
FLIPPED = (False, True, False, False, True)


def gram_into(x_ref, gram):
    rows = gram.shape[0]
    starts = list(range(0, rows, 256))
    for j in starts:
        n = min(256, rows - j)
        gram[j:rows, j : j + n] = dot_nt(x_ref[j:rows, :], x_ref[j : j + n, :])
    for j in starts:
        n = min(256, rows - j)
        if j + n < rows:
            gram[j : j + n, j + n : rows] = gram[j + n : rows, j : j + n].T


def newton_step(x_ref, gram, mixer, high, low, first, refined):
    gram_into(x_ref, gram)
    rows = gram.shape[0]
    same = lax.broadcasted_iota(jnp.int32, (rows, rows), 0) == lax.broadcasted_iota(
        jnp.int32, (rows, rows), 1
    )
    whole = gram[...]
    scale = None
    if first:
        scale = 1.0 / (jnp.sqrt(jnp.sum(jnp.where(same, whole, 0.0))) + frobenius_epsilon)
        whole = whole * (scale * scale)
        gram[...] = whole
    high[...] = whole.astype(bf16)
    squared = dot(high[...], high[...])
    if refined:
        low[...] = (gram[...] - high[...].astype(f32)).astype(bf16)
        squared = squared + dot(high[...], low[...]) + dot(low[...], high[...])
    mix = (
        jnp.where(same, newton_first, 0.0) + newton_second * gram[...] + newton_third * squared
    )
    if first:
        mix = mix * scale
    mixer[...] = mix.astype(bf16)
    width = x_ref.shape[1]
    tile = 1024 if width % 1024 == 0 else width

    @pl.loop(0, width // tile)
    def _(t):
        cols = pl.ds(pl.multiple_of(t * tile, tile), tile)
        x_ref[:, cols] = dot(mixer[...], x_ref[:, cols]).astype(bf16)


def muon_kernel(shapes, *refs):
    grads, moments, results = refs[0:5], refs[5:10], refs[10:15]
    outgoing, arrived = refs[15:20], refs[20:25]
    x_all, gram, mixer, high, low = refs[25:30]
    gather_send, gather_recv, scatter_send, scatter_recv = refs[30:34]
    rep, me, lane, lanes = place()

    def device(member):
        return (rep, member * lanes + lane)

    owner_here = me == OWNERS[0]
    for owner in OWNERS[1:]:
        owner_here = owner_here | (me == owner)

    @pl.when(owner_here)
    def _():
        x_all[...] = jnp.zeros_like(x_all)

    barrier = pltpu.get_barrier_semaphore()
    for step in range(1, GROUP):
        pl.semaphore_signal(
            barrier, inc=1, device_id=device(me ^ step), device_id_type=MESH
        )

    def block(number, member):
        rows, cols = shapes[number]
        if FLIPPED[number]:
            return x_all.at[:, pl.ds(member * rows, rows)]
        return x_all.at[pl.ds(member * rows, rows), pl.ds(0, cols)]

    for number in range(5):
        grad = jnp.concatenate(
            [grads[number][0], grads[number][1]], axis=0 if number in (OUT, DOWN) else 1
        ).astype(f32)
        new = momentum_decay * moments[number][...] + (1.0 - momentum_decay) * grad
        nesterov = (1.0 - momentum_decay) * grad + momentum_decay * new
        if FLIPPED[number]:
            nesterov = nesterov.T
        outgoing[number][...] = nesterov.astype(bf16)
    pl.semaphore_wait(barrier, GROUP - 1)

    def gather_copy(number, member, sender):
        rows, _ = shapes[number]
        if FLIPPED[number]:
            start = pl.multiple_of(sender * rows, rows)
            target = x_all.at[:, pl.ds(start, rows)]
        else:
            start = pl.multiple_of(sender * rows, 16)
            target = x_all.at[pl.ds(start, rows), pl.ds(0, shapes[number][1])]
        return pltpu.make_async_remote_copy(
            src_ref=outgoing[number],
            dst_ref=target,
            send_sem=gather_send.at[number],
            recv_sem=gather_recv.at[sender],
            device_id=device(member),
            device_id_type=MESH,
        )

    for number in (2, 3, 4, 0, 1):

        @pl.when(me != OWNERS[number])
        def _():
            gather_copy(number, OWNERS[number], me).start()

    for number in range(5):
        owner = OWNERS[number]

        @pl.when(me == owner)
        def _():
            rows, cols = shapes[number]
            if FLIPPED[number]:
                x_all[:, owner * rows : (owner + 1) * rows] = outgoing[number][...]
            else:
                x_all[owner * rows : (owner + 1) * rows, 0:cols] = outgoing[number][...]
            for step in range(1, GROUP):
                gather_copy(number, owner, owner ^ step).wait_recv()

    @pl.when(owner_here)
    def _():
        newton_step(x_all, gram, mixer, high, low, True, False)

        @pl.loop(0, NS_STEPS - 3)
        def _(k):
            newton_step(x_all, gram, mixer, high, low, False, False)

        @pl.loop(0, 2)
        def _(k):
            newton_step(x_all, gram, mixer, high, low, False, True)

    def scatter_copy(number, member):
        rows, cols = shapes[number]
        return pltpu.make_async_remote_copy(
            src_ref=block(number, member),
            dst_ref=arrived[number],
            send_sem=scatter_send.at[member],
            recv_sem=scatter_recv.at[number],
            device_id=device(member),
            device_id_type=MESH,
        )

    for number in range(5):
        owner = OWNERS[number]

        @pl.when(me == owner)
        def _():
            for step in range(1, GROUP):
                scatter_copy(number, owner ^ step).start()
            arrived[number][...] = block(number, owner)[...]

    for number in range(5):
        owner = OWNERS[number]

        @pl.when(me != owner)
        def _():
            scatter_copy(number, owner).wait_recv()

        update = arrived[number][...]
        if FLIPPED[number]:
            update = update.astype(f32).T.astype(bf16)
        results[number][...] = update

    for number in range(5):
        owner = OWNERS[number]

        @pl.when(me == owner)
        def _():
            for step in range(1, GROUP):
                scatter_copy(number, owner ^ step).wait_send()

        @pl.when(me != owner)
        def _():
            gather_copy(number, owner, me).wait_send()


def muon(grads, moments):
    shapes = tuple(moment.shape for moment in moments)
    flipped = [s[::-1] if flip else s for s, flip in zip(shapes, FLIPPED)]
    side = shapes[0][0] * GROUP
    width = max(s[0] * GROUP if flip else s[1] for s, flip in zip(shapes, FLIPPED))
    vmem = pl.BlockSpec(memory_space=pltpu.VMEM)
    return pl.pallas_call(
        lambda *refs: muon_kernel(shapes, *refs),
        out_shape=[jax.ShapeDtypeStruct(s, bf16) for s in shapes],
        in_specs=[vmem] * 10,
        out_specs=[vmem] * 5,
        scratch_shapes=[pltpu.VMEM(s, bf16) for s in flipped]
        + [pltpu.VMEM(s, bf16) for s in flipped]
        + [
            pltpu.VMEM((side, width), bf16),
            pltpu.VMEM((side, side), f32),
            pltpu.VMEM((side, side), bf16),
            pltpu.VMEM((side, side), bf16),
            pltpu.VMEM((side, side), bf16),
            pltpu.SemaphoreType.DMA((5,)),
            pltpu.SemaphoreType.DMA((GROUP,)),
            pltpu.SemaphoreType.DMA((GROUP,)),
            pltpu.SemaphoreType.DMA((5,)),
        ],
        compiler_params=pltpu.CompilerParams(
            collective_id=1, has_side_effects=True, vmem_limit_bytes=48 * 2**20
        ),
        name="muon",
    )(*grads, *moments)


def finish_kernel(factors, *refs):
    grads, updates, moments, weights = refs[0:5], refs[5:10], refs[10:15], refs[15:20]
    streams = refs[20:22]
    wide, news, masters = refs[22:27], refs[27:32], refs[32:37]
    for number in range(5):
        grad = grads[number][0].astype(f32)
        wide[number][...] = grad
        news[number][...] = (
            momentum_decay * moments[number][...] + (1.0 - momentum_decay) * grad
        )
        masters[number][...] = weights[number][...].astype(f32) - factors[number] * updates[
            number
        ][...].astype(f32)
    for source, target in zip(streams, refs[37:39]):
        target[...] = source[...]


def finish(grads, updates, moments, weights, streams):
    steps = 4
    shapes = tuple(moment.shape for moment in moments)
    factors = [max(1.0, s[0] * GROUP / s[1]) ** 0.5 * muon_rate for s in shapes]
    halves, wholes = [], []
    for number, (rows, cols) in enumerate(shapes):
        if number in (OUT, DOWN):
            halves.append(pl.BlockSpec((1, rows // steps, cols), lambda j: (j // 2, j % 2, 0)))
            wholes.append(pl.BlockSpec((rows // steps, cols), lambda j: (j, 0)))
        else:
            halves.append(pl.BlockSpec((1, rows, cols // steps), lambda j: (j // 2, 0, j % 2)))
            wholes.append(pl.BlockSpec((rows, cols // steps), lambda j: (0, j)))
    lines = [
        pl.BlockSpec((s.shape[0] // steps, s.shape[1]), lambda j: (j, 0)) for s in streams
    ]
    out = pl.pallas_call(
        lambda *refs: finish_kernel(factors, *refs),
        grid=(steps,),
        out_shape=[jax.ShapeDtypeStruct(s, f32) for s in shapes * 3]
        + [jax.ShapeDtypeStruct(s.shape, f32) for s in streams],
        in_specs=halves + wholes * 3 + lines,
        out_specs=wholes * 3 + lines,
        compiler_params=pltpu.CompilerParams(vmem_limit_bytes=48 * 2**20),
        name="finish",
    )(*grads, *updates, *moments, *weights, *streams)
    return out[0:5], out[5:10], out[10:15], out[15:17]


def shards(
    tokens,
    cotangent,
    prefix,
    w_qkv,
    w_out,
    w_gate,
    w_up,
    w_down,
    gains,
    moment_qkv,
    moment_out,
    moment_gate,
    moment_up,
    moment_down,
    gain_first,
    gain_second,
):
    rows, width = tokens.shape
    reps = lax.axis_size("rep")
    here = lax.axis_index("fsdp")
    rep, me, lane, lanes = place()
    teams = [[member * lanes + k for k in range(lanes)] for member in range(GROUP)]

    def joined(shard):
        if lanes == 1:
            return shard
        return lax.all_gather(shard, "fsdp", axis=0, tiled=True, axis_index_groups=teams)

    def summed(term):
        if lanes == 1:
            return term
        parts = lax.all_gather(term, "fsdp", axis_index_groups=teams)
        return jnp.sum(parts.astype(f32), axis=0).astype(term.dtype)

    def parted(block):
        if lanes == 1:
            return block
        size = block.shape[0] // lanes
        return lax.dynamic_slice_in_dim(block, lane * size, size, 0)

    sequence_id = (rep * lax.axis_size("fsdp") + here) // 2
    prefix_len = lax.dynamic_slice_in_dim(prefix, sequence_id, 1, 0)
    positions = here % 2 * rows + jnp.arange(rows, dtype=jnp.int32)
    cosine, sine = rotary_tables(positions, HEAD_DIM)
    gain_block = joined(gains).astype(f32).T
    gain_part = lax.dynamic_update_slice(
        jnp.zeros((8, width), f32), gain_block, (0, me * gain_block.shape[1])
    )
    weights = [joined(term) for term in (w_qkv, w_out, w_gate, w_up, w_down)]
    moments = [
        joined(term)
        for term in (moment_qkv, moment_out, moment_gate, moment_up, moment_down)
    ]
    output, d_tokens, small, halves = layer(
        prefix_len, tokens, cotangent, cosine, sine, gain_part, weights, reps
    )
    halves = [summed(term) for term in halves]
    small = summed(small)
    updates = muon(halves, moments)
    grads, news, masters, streams = finish(
        halves, updates, moments, weights, (output, d_tokens)
    )
    grads, news, masters = (
        [parted(term) for term in group] for group in (grads, news, masters)
    )
    statistics = jnp.sqrt(small[4, 0:4] / (small[4, 4] * width))
    count = gains.shape[0]
    gain_grad = lax.dynamic_slice(small, (0, here * count), (4, count)).T
    gains_local = gains.astype(f32)
    first_new = first_decay * gain_first + (1.0 - first_decay) * gain_grad
    second_new = second_decay * gain_second + (1.0 - second_decay) * gain_grad * gain_grad
    first_hat = first_new / (1.0 - first_decay**ADAM_STEP)
    second_hat = second_new / (1.0 - second_decay**ADAM_STEP)
    master_gains = gains_local - adam_rate * (
        first_hat / (jnp.sqrt(second_hat) + adam_epsilon) + weight_decay * gains_local
    )
    return (
        *streams,
        *grads,
        gain_grad,
        *news,
        *masters,
        first_new,
        second_new,
        master_gains,
        statistics,
    )


def solution(mesh):
    in_specs = (
        P(("rep", "fsdp"), None),
        P(("rep", "fsdp"), None),
        P(),
        P("fsdp", None),
        P("fsdp", None),
        P("fsdp", None),
        P("fsdp", None),
        P("fsdp", None),
        P("fsdp", None),
        P("fsdp", None),
        P("fsdp", None),
        P("fsdp", None),
        P("fsdp", None),
        P("fsdp", None),
        P("fsdp", None),
        P("fsdp", None),
    )
    out_specs = (
        P(("rep", "fsdp"), None),
        P(("rep", "fsdp"), None),
        P("fsdp", None),
        P("fsdp", None),
        P("fsdp", None),
        P("fsdp", None),
        P("fsdp", None),
        P("fsdp", None),
        P("fsdp", None),
        P("fsdp", None),
        P("fsdp", None),
        P("fsdp", None),
        P("fsdp", None),
        P("fsdp", None),
        P("fsdp", None),
        P("fsdp", None),
        P("fsdp", None),
        P("fsdp", None),
        P("fsdp", None),
        P("fsdp", None),
        P("fsdp", None),
        P(),
    )
    return jax.shard_map(shards, mesh=mesh, in_specs=in_specs, out_specs=out_specs, check_vma=False)
```

```python
import jax
import jax.numpy as jnp
from jax import lax
from jax.experimental import pallas as pl
from jax.experimental.pallas import tpu as pltpu
from jax.sharding import PartitionSpec as P

HEADS = 4
HEAD_DIM = 256
NS_STEPS = 5
ADAM_STEP = 10


norm_epsilon = 1e-06
soft_cap = 50.0
rotary_base = 10000.0
newton_first = 3.4445
newton_second = -4.775
newton_third = 2.0315
momentum_decay = 0.95
muon_rate = 1.0
first_decay = 0.9
second_decay = 0.95
adam_rate = 1.0
weight_decay = 0.1
adam_epsilon = 1e-08
frobenius_epsilon = 1e-07

GROUP = 8
MESH = pl.DeviceIdType.MESH
f32 = jnp.float32
bf16 = jnp.bfloat16


def dot(a, b):
    return lax.dot_general(a, b, (((1,), (0,)), ((), ())), preferred_element_type=f32)


def dot_nt(a, b):
    return lax.dot_general(a, b, (((1,), (1,)), ((), ())), preferred_element_type=f32)


def dot_tn(a, b):
    return lax.dot_general(a, b, (((0,), (0,)), ((), ())), preferred_element_type=f32)


def place():
    size = lax.axis_size("fsdp")
    lanes = size // GROUP
    here = lax.axis_index("fsdp")
    return lax.axis_index("rep"), here // lanes, lax.rem(here, lanes), lanes


QKV, OUT, GATE, UP, DOWN = range(5)
CORE, ACROSS, ALONG = 1, 2, 4
PAIRS = (
    ((GATE, 0), (UP, 0)),
    ((DOWN, 0), (GATE, 1)),
    ((UP, 1), (DOWN, 1)),
    ((OUT, 0), (OUT, 1)),
    ((QKV, 0), (QKV, 1)),
)
CHUNK = 128
TILE = 256


def split_shape(number, shape):
    rows, cols = shape
    return (rows // 2, cols) if number in (OUT, DOWN) else (rows, cols // 2)


def layer_names(rows, keys, width, shapes, reps):
    halves = [split_shape(number, shape) for number, shape in enumerate(shapes)]
    feats = HEADS * HEAD_DIM
    inner = shapes[GATE][1]
    spaces = {}
    for number, (height, cols) in enumerate(shapes):
        spaces[f"whole{number}"] = pltpu.VMEM((height * GROUP, cols), bf16)
    spaces.update(
        cosine=pltpu.VMEM((rows, HEAD_DIM // 2), f32),
        sine=pltpu.VMEM((rows, HEAD_DIM // 2), f32),
        gain_parts=pltpu.VMEM((GROUP, 8, 128), f32),
        gains=pltpu.VMEM((8, width), f32),
        normed=pltpu.VMEM((rows, width), bf16),
        one_t=pltpu.VMEM((width, rows), bf16),
        two_t=pltpu.VMEM((width, rows), bf16),
        proj=pltpu.VMEM((rows, feats + 2 * HEAD_DIM), bf16),
        key=pltpu.VMEM((keys, HEAD_DIM), bf16),
        value=pltpu.VMEM((keys, HEAD_DIM), bf16),
        key_t=pltpu.VMEM((HEAD_DIM, keys), bf16),
        value_t=pltpu.VMEM((HEAD_DIM, keys), bf16),
        att=pltpu.VMEM((rows, feats), bf16),
        att_t=pltpu.VMEM((feats, rows), bf16),
        inverse=pltpu.VMEM((8, rows), f32),
        branch=pltpu.VMEM((rows, width), f32),
        hidden=pltpu.VMEM((rows, width), f32),
        slope=pltpu.VMEM((rows, inner), bf16),
        bend=pltpu.VMEM((rows, inner), bf16),
        active=pltpu.VMEM((rows, inner), bf16),
        d_key=pltpu.VMEM((keys, HEAD_DIM), f32),
        d_value=pltpu.VMEM((keys, HEAD_DIM), f32),
        swap_out=pltpu.VMEM((2, rows, HEAD_DIM), bf16),
        swap_in=pltpu.VMEM((2, rows, HEAD_DIM), bf16),
        squares=pltpu.VMEM((8, width), f32),
        d_gains=pltpu.VMEM((8, width), f32),
        small_parts=pltpu.VMEM((GROUP, 8, width), f32),
        small_reps=pltpu.VMEM((reps, 8, width), f32),
    )
    for number, half in enumerate(halves):
        spaces[f"stage{number}"] = pltpu.VMEM((2, 2, 2, 2) + half, bf16)
        spaces[f"chip{number}"] = pltpu.VMEM((2, 2, 2) + half, bf16)
        spaces[f"pair{number}"] = pltpu.VMEM((2, 2) + half, bf16)
        spaces[f"plane{number}"] = pltpu.VMEM((2,) + half, bf16)
        spaces[f"line{number}"] = pltpu.VMEM((2, 2) + half, bf16)
        spaces[f"total{number}"] = pltpu.VMEM((2,) + half, bf16)
    dma = pltpu.SemaphoreType.DMA
    spaces.update(
        own_sem=dma((5,)),
        result_sem=dma((5,)),
        weight_send=dma((5, 9)),
        weight_recv=dma((5, 9)),
        gain_send=dma((GROUP,)),
        gain_recv=dma((GROUP,)),
        key_send=dma((2,)),
        key_recv=dma((2,)),
        swap_send=dma((1,)),
        swap_recv=dma((1,)),
        chip_send=dma((5, 2)),
        chip_recv=dma((5, 2)),
        pair_send=dma((5, 2)),
        pair_recv=dma((5, 2)),
        plane_send=dma((5, 2)),
        plane_recv=dma((5, 2)),
        line_send=dma((5, 2)),
        line_recv=dma((5, 2, 2)),
        total_send=dma((5, 2)),
        total_recv=dma((5, 2)),
        small_send=dma((GROUP,)),
        small_recv=dma((GROUP,)),
        reps_send=dma((reps,)),
        reps_recv=dma((reps,)),
    )
    return spaces


class Refs:
    def __init__(self, names, refs):
        self.__dict__.update(zip(names, refs))


def column_sum(x):
    return jnp.sum(x, axis=0, keepdims=True)


def row_mean(x):
    return jnp.mean(x, axis=-1, keepdims=True)


def layer_kernel(names, shapes, *refs):
    v = Refs(names, refs)
    rep, me, lane, lanes = place()
    reps = lax.axis_size("rep")
    here = lax.axis_index("fsdp")
    core, across, along = me % 2, (me // 2) % 2, me // 4
    rows, width = v.tokens.shape
    parity = here % 2
    weights = [v.w_qkv, v.w_out, v.w_gate, v.w_up, v.w_down]
    named = lambda name: [getattr(v, f"{name}{number}") for number in range(5)]
    whole, stage, chip, pair = named("whole"), named("stage"), named("chip"), named("pair")
    plane, line, total, result = named("plane"), named("line"), named("total"), named("grad")

    def device(member):
        return (rep, member * lanes + lane)

    def remote(src, dst, send, recv, where):
        return pltpu.make_async_remote_copy(
            src_ref=src,
            dst_ref=dst,
            send_sem=send,
            recv_sem=recv,
            device_id=where,
            device_id_type=MESH,
        )

    barrier = pltpu.get_barrier_semaphore()
    greeted = [device(me ^ step) for step in range(1, GROUP)]
    greeted += [(lax.rem(rep + step, reps), here) for step in range(1, reps)]
    if lanes > 1:
        greeted.append((rep, here ^ 1))
    for where in greeted:
        pl.semaphore_signal(barrier, inc=1, device_id=where, device_id_type=MESH)
    pl.semaphore_wait(barrier, len(greeted))

    def slot(number, member):
        height = shapes[number][0]
        return whole[number].at[pl.ds(pl.multiple_of(member * height, 16), height), :]

    def half_slot(number, member, half):
        height, cols = split_shape(number, shapes[number])
        start = pl.multiple_of(member * shapes[number][0], 16)
        if number in (OUT, DOWN):
            return whole[number].at[pl.ds(start + half * height, height), :]
        return whole[number].at[pl.ds(start, height), pl.ds(half * cols, cols)]

    def weight_copy(number, kind):
        beside, ahead = me ^ ACROSS, me ^ ALONG
        if kind < 3:
            where = me ^ (CORE, ACROSS, ALONG)[kind]
            src, dst = weights[number], slot(number, me)
        else:
            src = (
                half_slot(number, beside, 0),
                half_slot(number, ahead, 1),
                slot(number, beside),
                slot(number, ahead),
                half_slot(number, beside ^ ALONG, 0),
                half_slot(number, beside ^ ALONG, 1),
            )[kind - 3]
            dst = src
            where = (ahead, beside)[kind - 3] if kind < 5 else me ^ CORE
        return remote(
            src,
            dst,
            v.weight_send.at[number, kind],
            v.weight_recv.at[number, kind],
            device(where),
        )

    def own_copy(number):
        return pltpu.make_async_copy(weights[number], slot(number, me), v.own_sem.at[number])

    def weight_begin(number):
        for kind in (1, 2, 0):
            weight_copy(number, kind).start()
        own_copy(number).start()

    def weight_forward(number):
        weight_copy(number, 1).wait_recv()
        weight_copy(number, 3).start()
        weight_copy(number, 5).start()
        weight_copy(number, 2).wait_recv()
        weight_copy(number, 4).start()
        weight_copy(number, 6).start()

    def weight_corner(number):
        weight_copy(number, 3).wait_recv()
        weight_copy(number, 7).start()
        weight_copy(number, 4).wait_recv()
        weight_copy(number, 8).start()

    def weight_ready(number):
        own_copy(number).wait()
        for kind in (0, 5, 6, 7, 8):
            weight_copy(number, kind).wait_recv()

    weight_begin(QKV)
    weight_begin(OUT)

    def gain_copy(step):
        return remote(
            v.gain_parts.at[me],
            v.gain_parts.at[me],
            v.gain_send.at[step],
            v.gain_recv.at[step],
            device(me ^ step),
        )

    gain_count, gain_rows = v.gain_block.shape
    v.gain_parts[me] = jnp.zeros_like(v.gain_parts[me])
    v.gain_parts[me, 0:gain_count, 0:gain_rows] = v.gain_block[...].astype(f32)
    for step in range(1, GROUP):
        gain_copy(step).start()
    weight_begin(GATE)
    v.squares[...] = jnp.zeros_like(v.squares)
    v.d_gains[...] = jnp.zeros_like(v.d_gains)
    v.d_key[...] = jnp.zeros_like(v.d_key)
    v.d_value[...] = jnp.zeros_like(v.d_value)
    spot = lax.broadcasted_iota(jnp.int32, (rows, HEAD_DIM // 2), 0) + parity * rows
    angles = spot.astype(f32) * v.frequency[...]
    v.cosine[...] = jnp.cos(angles)
    v.sine[...] = jnp.sin(angles)
    for step in range(1, GROUP):
        gain_copy(step).wait_recv()
    for member in range(GROUP):
        v.gains[:, member * gain_rows : (member + 1) * gain_rows] = v.gain_parts[
            member, :, 0:gain_rows
        ]

    prefix = v.prefix[(rep * lax.axis_size("fsdp") + here) // 2]

    def valid_rows(start, count):
        spot = lax.broadcasted_iota(jnp.int32, (count, 1), 0) + (parity * rows + start)
        return jnp.where(spot >= prefix, 1.0, 0.0)

    def by_rows(body):
        @pl.loop(0, rows // CHUNK)
        def _(k):
            start = pl.multiple_of(k * CHUNK, CHUNK)
            body(pl.ds(start, CHUNK), start)

    def by_columns(count, body):
        @pl.loop(0, count // TILE)
        def _(k):
            body(pl.ds(pl.multiple_of(k * TILE, TILE), TILE), k)

    def inverse_root(x):
        return lax.rsqrt(row_mean(x * x) + norm_epsilon)

    def norm_back(x, scale, upstream, gain, row):
        v.d_gains[row : row + 1, :] += column_sum(upstream * x * scale)
        spread = upstream * gain
        return scale * spread - x * (scale * scale * scale * row_mean(x * spread))

    gain_row = lambda k: v.gains[k : k + 1, :]

    def first_norm(here_rows, start):
        x = v.tokens[here_rows, :].astype(f32)
        normed = x * inverse_root(x) * gain_row(0)
        v.normed[here_rows, :] = normed.astype(bf16)
        v.one_t[:, here_rows] = normed.T.astype(bf16)
        v.squares[0:1, :] += column_sum(valid_rows(start, CHUNK) * (x * x))

    by_rows(first_norm)
    weight_forward(QKV)
    weight_corner(QKV)
    weight_ready(QKV)

    feats = HEADS * HEAD_DIM
    half_dim = HEAD_DIM // 2
    own_rows = pl.ds(pl.multiple_of(parity * rows, rows), rows)
    other_rows = pl.ds(pl.multiple_of((1 - parity) * rows, rows), rows)

    def rotate(x, sign):
        first, second = x[:, :half_dim], x[:, half_dim:]
        cosine, sine = v.cosine[...], v.sine[...] * sign
        return first * cosine - second * sine, second * cosine + first * sine

    def key_copy(number):
        ref = (v.key, v.value)[number]
        return remote(
            ref.at[own_rows, :],
            ref.at[own_rows, :],
            v.key_send.at[number],
            v.key_recv.at[number],
            (rep, here ^ 1),
        )

    key_part = dot(v.normed[...], whole[QKV][:, feats : feats + HEAD_DIM])
    first, second = rotate(key_part, 1.0)
    v.key[own_rows, :half_dim] = first.astype(bf16)
    v.key[own_rows, half_dim:] = second.astype(bf16)
    key_copy(0).start()
    v.value[own_rows, :] = dot(v.normed[...], whole[QKV][:, feats + HEAD_DIM :]).astype(bf16)
    key_copy(1).start()

    @pl.loop(0, HEADS)
    def _(head):
        start = pl.multiple_of(head * HEAD_DIM, HEAD_DIM)
        part = dot(v.normed[...], whole[QKV][:, pl.ds(start, HEAD_DIM)])
        first, second = rotate(part, 1.0)
        v.proj[:, pl.ds(start, half_dim)] = first.astype(bf16)
        v.proj[:, pl.ds(start + half_dim, half_dim)] = second.astype(bf16)

    weight_forward(OUT)
    weight_begin(UP)
    for number in range(2):
        key_copy(number).wait_recv()
    v.key_t[...] = v.key[...].astype(f32).T.astype(bf16)
    v.value_t[...] = v.value[...].astype(f32).T.astype(bf16)

    keys = v.key.shape[0]
    bend_scale = HEAD_DIM ** (-0.5) / soft_cap

    def scores(head, start):
        here_rows = pl.ds(start, TILE)
        query = v.proj[here_rows, head * HEAD_DIM : (head + 1) * HEAD_DIM]
        bent = jnp.tanh(dot_nt(v.key[...], query) * bend_scale)
        spot = lax.broadcasted_iota(jnp.int32, (1, TILE), 1) + (parity * rows + start)
        last = jnp.maximum(spot, prefix - 1)
        allowed = lax.broadcasted_iota(jnp.int32, (keys, TILE), 0) <= last
        return bent, jnp.where(allowed, jnp.exp(soft_cap * bent), 0.0), query

    def attend(head):
        cols = slice(head * HEAD_DIM, (head + 1) * HEAD_DIM)

        @pl.loop(0, rows // TILE)
        def _(k):
            start = pl.multiple_of(k * TILE, TILE)
            here_rows = pl.ds(start, TILE)
            _, power, _ = scores(head, start)
            inverse = 1.0 / column_sum(power)
            v.inverse[head : head + 1, here_rows] = inverse
            mixed = dot(v.value_t[...], (power * inverse).astype(bf16))
            v.att_t[cols, here_rows] = mixed.astype(bf16)
            v.att[here_rows, cols] = mixed.T.astype(bf16)

    attend(0)
    weight_corner(OUT)
    weight_forward(GATE)
    weight_begin(DOWN)
    attend(1)
    attend(2)
    weight_corner(GATE)
    weight_forward(UP)
    attend(3)
    weight_ready(OUT)

    v.branch[...] = dot(v.att[...], whole[OUT][...])

    def second_norm(here_rows, start):
        x = v.branch[here_rows, :]
        first_out = x * inverse_root(x) * gain_row(1)
        hidden = v.tokens[here_rows, :].astype(f32) + first_out
        v.hidden[here_rows, :] = hidden
        normed = hidden * inverse_root(hidden) * gain_row(2)
        v.normed[here_rows, :] = normed.astype(bf16)
        v.two_t[:, here_rows] = normed.T.astype(bf16)
        v.squares[1:2, :] += column_sum(valid_rows(start, CHUNK) * (first_out * first_out))

    by_rows(second_norm)
    weight_ready(GATE)
    weight_corner(UP)
    weight_ready(UP)
    weight_forward(DOWN)
    inner = shapes[GATE][1]

    def feed(cols, k):
        gate = dot(v.normed[...], whole[GATE][:, cols])
        upward = dot(v.normed[...], whole[UP][:, cols])
        square = gate * gate
        bent = jnp.tanh(0.7978845608028654 * (gate + 0.044715 * gate * square))
        open_half = 0.5 * (1.0 + bent)
        smooth = gate * open_half
        steep = open_half + gate * (1.0 - bent * bent) * (
            0.3989422804014327 * (1.0 + 3.0 * 0.044715 * square)
        )
        v.active[:, cols] = (smooth * upward).astype(bf16)
        v.bend[:, cols] = smooth.astype(bf16)
        v.slope[:, cols] = (steep * upward).astype(bf16)

    by_columns(inner, feed)
    weight_corner(DOWN)
    weight_ready(DOWN)

    v.d_tokens[...] = dot(v.active[...], whole[DOWN][...])

    def last_norm(here_rows, start):
        x = v.d_tokens[here_rows, :]
        scale = inverse_root(x)
        second_out = x * scale * gain_row(3)
        final = v.hidden[here_rows, :] + second_out
        v.output[here_rows, :] = final
        valid = valid_rows(start, CHUNK)
        v.squares[2:3, :] += column_sum(valid * (second_out * second_out))
        v.squares[3:4, :] += column_sum(valid * (final * final))
        upstream = v.cotangent[here_rows, :].astype(f32)
        v.normed[here_rows, :] = norm_back(x, scale, upstream, gain_row(3), 3).astype(bf16)

    by_rows(last_norm)

    def first_across(number, half):
        return any(one == (number, half) for one, _ in PAIRS)

    def chip_copy(number, half):
        return remote(
            stage[number].at[half, :, :, 1 - core],
            chip[number].at[half],
            v.chip_send.at[number, half],
            v.chip_recv.at[number, half],
            device(me ^ CORE),
        )

    def pair_copy(number, half):
        if first_across(number, half):
            src, where = chip[number].at[half, :, 1 - across], me ^ ACROSS
        else:
            src, where = chip[number].at[half, 1 - along], me ^ ALONG
        return remote(
            src,
            pair[number].at[half],
            v.pair_send.at[number, half],
            v.pair_recv.at[number, half],
            device(where),
        )

    def plane_copy(number, half):
        if first_across(number, half):
            src, where = pair[number].at[half, 1 - along], me ^ ALONG
        else:
            src, where = pair[number].at[half, 1 - across], me ^ ACROSS
        return remote(
            src,
            plane[number].at[half],
            v.plane_send.at[number, half],
            v.plane_recv.at[number, half],
            device(where),
        )

    def added(one, two):
        return (one.astype(f32) + two.astype(f32)).astype(bf16)

    def chip_begin(number, half):
        chip_copy(number, half).start()

    def chip_end(number, half):
        chip_copy(number, half).wait_recv()

        @pl.loop(0, 4)
        def _(k):
            one, two = k // 2, k % 2
            chip[number][half, one, two] = added(
                chip[number][half, one, two], stage[number][half, one, two, core]
            )

        pair_copy(number, half).start()

    def pair_end(number, half):
        pair_copy(number, half).wait_recv()

        @pl.loop(0, 2)
        def _(k):
            if first_across(number, half):
                mine = chip[number][half, k, across]
            else:
                mine = chip[number][half, along, k]
            pair[number][half, k] = added(pair[number][half, k], mine)

        plane_copy(number, half).start()

    def plane_end(number, half):
        plane_copy(number, half).wait_recv()
        kept = along if first_across(number, half) else across
        plane[number][half] = added(plane[number][half], pair[number][half, kept])

    order = [half for both in PAIRS for half in both]

    on_left = rep < reps // 2
    inward = jnp.where(on_left, 1, -1)
    at_end = (rep == 0) | (rep == reps - 1)
    at_middle = (rep == reps // 2 - 1) | (rep == reps // 2)

    def line_copy(number, half, way):
        return remote(
            plane[number].at[half],
            line[number].at[half, way],
            v.line_send.at[number, half],
            v.line_recv.at[number, half, way],
            (rep + inward, here),
        )

    def total_copy(number, half):
        return remote(
            total[number].at[half],
            total[number].at[half],
            v.total_send.at[number, half],
            v.total_recv.at[number, half],
            (rep - inward, here),
        )

    def line_begin(number, half):
        @pl.when(jnp.logical_not(at_end))
        def _():
            line_copy(number, half, 0).wait_recv()
            plane[number][half] = added(plane[number][half], line[number][half, 0])

        @pl.when(jnp.logical_not(at_middle))
        def _():
            line_copy(number, half, 0).start()

        @pl.when(at_middle)
        def _():
            line_copy(number, half, 1).start()

    def line_end(number, half):
        @pl.when(at_middle)
        def _():
            line_copy(number, half, 1).wait_recv()
            total[number][half] = added(plane[number][half], line[number][half, 1])

            @pl.when(jnp.logical_not(at_end))
            def _():
                total_copy(number, half).start()

    def total_end(number, half):
        @pl.when(jnp.logical_not(at_middle))
        def _():
            total_copy(number, half).wait_recv()

            @pl.when(jnp.logical_not(at_end))
            def _():
                total_copy(number, half).start()

    def for_pair(action, index):
        for number, half in PAIRS[index]:
            action(number, half)

    def keep_columns(number, col_half, col, found):
        height = shapes[number][0]
        for member in range(GROUP):
            stage[number][
                col_half, member // 4, (member // 2) % 2, member % 2, :, pl.ds(col, TILE)
            ] = found[member * height : (member + 1) * height].astype(bf16)

    down_rows = shapes[DOWN][0]
    halved = inner // 2 // TILE

    def feed_back(side, begin, end):
        @pl.loop(begin, end)
        def _(k):
            col = pl.multiple_of(k * TILE, TILE)
            start = pl.multiple_of(side * (inner // 2) + k * TILE, TILE)
            cols = pl.ds(start, TILE)
            d_active = dot_nt(v.normed[...], whole[DOWN][cols, :])
            d_gate = (d_active * v.slope[:, cols].astype(f32)).astype(bf16)
            d_upward = (d_active * v.bend[:, cols].astype(f32)).astype(bf16)
            v.slope[:, cols] = d_gate
            v.bend[:, cols] = d_upward
            keep_columns(GATE, side, col, dot(v.two_t[...], d_gate))
            keep_columns(UP, side, col, dot(v.two_t[...], d_upward))
            found = dot_tn(v.active[:, cols], v.normed[...]).astype(bf16)
            per = TILE // down_rows
            for part in range(per):
                member = (side * halved + k) * per + part
                y, x, c = member // 4, (member // 2) % 2, member % 2
                base = part * down_rows
                stage[DOWN][0, y, x, c] = found[base : base + down_rows // 2]
                stage[DOWN][1, y, x, c] = found[base + down_rows // 2 : base + down_rows]

    feed_back(0, 0, halved)
    for_pair(chip_begin, 0)
    feed_back(1, 0, halved // 2)
    for_pair(chip_end, 0)
    feed_back(1, halved // 2, halved)
    for_pair(chip_begin, 1)
    for_pair(chip_begin, 2)
    v.d_tokens[...] = dot_nt(v.slope[...], whole[GATE][...])
    for_pair(chip_end, 1)
    v.d_tokens[...] += dot_nt(v.bend[...], whole[UP][...])
    for_pair(chip_end, 2)

    def middle_norms(here_rows, start):
        x = v.hidden[here_rows, :]
        flow = norm_back(x, inverse_root(x), v.d_tokens[here_rows, :], gain_row(2), 2)
        d_hidden = v.cotangent[here_rows, :].astype(f32) + flow
        v.d_tokens[here_rows, :] = d_hidden
        x = v.branch[here_rows, :]
        flow = norm_back(x, inverse_root(x), d_hidden, gain_row(1), 1)
        v.normed[here_rows, :] = flow.astype(bf16)

    by_rows(middle_norms)
    for_pair(pair_end, 0)
    out_rows = shapes[OUT][0]
    v.att[...] = dot_nt(v.normed[...], whole[OUT][...]).astype(bf16)

    @pl.loop(0, GROUP // 2)
    def _(k):
        start = pl.multiple_of(k * 2 * out_rows, 2 * out_rows)
        found = dot(v.att_t[pl.ds(start, 2 * out_rows), :], v.normed[...]).astype(bf16)
        for part in range(4):
            stage[OUT][part % 2, k // 2, k % 2, part // 2] = found[
                part * (out_rows // 2) : (part + 1) * (out_rows // 2)
            ]

    for_pair(chip_begin, 3)
    for_pair(pair_end, 1)
    for_pair(plane_end, 0)
    for_pair(line_begin, 0)

    def attend_back(head):
        cols = slice(head * HEAD_DIM, (head + 1) * HEAD_DIM)

        @pl.loop(0, rows // TILE)
        def _(k):
            start = pl.multiple_of(k * TILE, TILE)
            here_rows = pl.ds(start, TILE)
            bent, power, query = scores(head, start)
            soft = power * v.inverse[head : head + 1, here_rows]
            flow = v.att[here_rows, cols]
            d_soft = dot_nt(v.value[...], flow)
            v.d_value[...] += dot(soft.astype(bf16), flow)
            level = column_sum(d_soft * soft)
            d_raw = soft * (d_soft - level) * ((1.0 - bent * bent) * HEAD_DIM ** (-0.5))
            d_raw = d_raw.astype(bf16)
            v.d_key[...] += dot(d_raw, query)
            d_query = dot(v.key_t[...], d_raw).T
            first, second = d_query[:, :half_dim], d_query[:, half_dim:]
            cosine, sine = v.cosine[here_rows, :], v.sine[here_rows, :]
            base = head * HEAD_DIM
            v.proj[here_rows, base : base + half_dim] = (first * cosine + second * sine).astype(
                bf16
            )
            v.proj[here_rows, base + half_dim : base + HEAD_DIM] = (
                second * cosine - first * sine
            ).astype(bf16)

    swap = remote(
        v.swap_out,
        v.swap_in,
        v.swap_send.at[0],
        v.swap_recv.at[0],
        (rep, here ^ 1),
    )

    attend_back(0)
    for_pair(chip_end, 3)
    attend_back(1)
    for_pair(line_end, 0)
    for_pair(pair_end, 2)
    attend_back(2)
    for_pair(plane_end, 1)
    for_pair(line_begin, 1)
    for_pair(total_end, 0)
    attend_back(3)
    v.swap_out[0] = v.d_key[other_rows, :].astype(bf16)
    v.swap_out[1] = v.d_value[other_rows, :].astype(bf16)
    swap.start()
    for_pair(line_end, 1)
    for_pair(pair_end, 3)

    qkv_half = split_shape(QKV, shapes[QKV])[1] // TILE

    def projection_grad(tile):
        found = dot(v.one_t[...], v.proj[:, tile * TILE : (tile + 1) * TILE])
        keep_columns(QKV, tile // qkv_half, (tile % qkv_half) * TILE, found)

    for tile in range(qkv_half):
        projection_grad(tile)
    chip_begin(QKV, 0)
    swap.wait_recv()
    d_key = v.d_key[own_rows, :] + v.swap_in[0].astype(f32)
    first, second = rotate(d_key, -1.0)
    v.proj[:, feats : feats + half_dim] = first.astype(bf16)
    v.proj[:, feats + half_dim : feats + HEAD_DIM] = second.astype(bf16)
    v.proj[:, feats + HEAD_DIM :] = (
        v.d_value[own_rows, :] + v.swap_in[1].astype(f32)
    ).astype(bf16)
    for tile in range(qkv_half, 2 * qkv_half):
        projection_grad(tile)
    chip_begin(QKV, 1)
    for_pair(plane_end, 2)
    for_pair(line_begin, 2)
    for_pair(chip_end, 4)
    v.branch[...] = dot_nt(v.proj[...], whole[QKV][...])
    for_pair(total_end, 1)
    for_pair(plane_end, 3)
    for_pair(line_begin, 3)

    def first_norm_back(here_rows, start):
        x = v.tokens[here_rows, :].astype(f32)
        flow = norm_back(x, inverse_root(x), v.branch[here_rows, :], gain_row(0), 0)
        v.d_tokens[here_rows, :] += flow

    by_rows(first_norm_back)

    def small_copy(step):
        return remote(
            v.small_parts.at[me],
            v.small_parts.at[me],
            v.small_send.at[step],
            v.small_recv.at[step],
            device(me ^ step),
        )

    def reps_copy(step):
        return remote(
            v.small_reps.at[rep],
            v.small_reps.at[rep],
            v.reps_send.at[step],
            v.reps_recv.at[step],
            (lax.rem(rep + step, reps), here),
        )

    spot = lax.broadcasted_iota(jnp.int32, (1, width), 1)
    numbers = jnp.where(spot == 4, column_sum(valid_rows(0, rows)), 0.0)
    for k in range(4):
        summed = jnp.sum(v.squares[k : k + 1, :], axis=1, keepdims=True)
        numbers = numbers + jnp.where(spot == k, summed, 0.0)
    v.d_gains[4:5, :] = numbers
    v.small_parts[me] = v.d_gains[...]
    for step in range(1, GROUP):
        small_copy(step).start()
    for_pair(line_end, 2)
    for_pair(pair_end, 4)
    for_pair(line_end, 3)
    for_pair(total_end, 2)
    for step in range(1, GROUP):
        small_copy(step).wait_recv()
    v.small_reps[rep] = jnp.sum(v.small_parts[...], axis=0)
    for step in range(1, reps):
        reps_copy(step).start()
    for number, half in PAIRS[4]:
        plane_end(number, half)
        line_begin(number, half)
    for_pair(total_end, 3)
    for_pair(line_end, 4)
    for_pair(total_end, 4)
    for step in range(1, reps):
        reps_copy(step).wait_recv()
    v.small[...] = jnp.sum(v.small_reps[...], axis=0)
    results = [
        pltpu.make_async_copy(total[number], result[number], v.result_sem.at[number])
        for number in range(5)
    ]
    for copy in results:
        copy.start()

    for number in range(5):
        for kind in range(9):
            weight_copy(number, kind).wait_send()
    for number in range(2):
        key_copy(number).wait_send()
    swap.wait_send()
    for step in range(1, GROUP):
        gain_copy(step).wait_send()
        small_copy(step).wait_send()
    for step in range(1, reps):
        reps_copy(step).wait_send()
    for number, half in order:
        chip_copy(number, half).wait_send()
        pair_copy(number, half).wait_send()
        plane_copy(number, half).wait_send()
        line_copy(number, half, 0).wait_send()

        @pl.when(jnp.logical_not(at_end))
        def _():
            total_copy(number, half).wait_send()

    for copy in results:
        copy.wait()


def layer(prefix, tokens, cotangent, frequency, gain_block, weights, reps):
    shapes = tuple(w.shape for w in weights)
    rows, width = tokens.shape
    spaces = layer_names(rows, 2 * rows, width, shapes, reps)
    halves = [split_shape(number, shape) for number, shape in enumerate(shapes)]
    inputs = ["prefix", "tokens", "cotangent", "frequency", "gain_block"]
    inputs += ["w_qkv", "w_out", "w_gate", "w_up", "w_down"]
    outputs = ["output", "d_tokens", "small"] + [f"grad{number}" for number in range(5)]
    vmem = pl.BlockSpec(memory_space=pltpu.VMEM)
    names = inputs + outputs + list(spaces)
    out = pl.pallas_call(
        lambda *refs: layer_kernel(names, shapes, *refs),
        out_shape=[
            jax.ShapeDtypeStruct((rows, width), f32),
            jax.ShapeDtypeStruct((rows, width), f32),
            jax.ShapeDtypeStruct((8, width), f32),
        ]
        + [jax.ShapeDtypeStruct((2,) + half, bf16) for half in halves],
        in_specs=[pl.BlockSpec(memory_space=pltpu.SMEM)]
        + [vmem] * 4
        + [pl.BlockSpec(memory_space=pl.ANY)] * 5,
        out_specs=[vmem] * 3 + [pl.BlockSpec(memory_space=pl.ANY)] * 5,
        scratch_shapes=list(spaces.values()),
        compiler_params=pltpu.CompilerParams(
            collective_id=2, has_side_effects=True, vmem_limit_bytes=64 * 2**20
        ),
        name="layer",
    )(prefix, tokens, cotangent, frequency, gain_block, *weights)
    return out[0], out[1], out[2], out[3:]


OWNERS = (6, 7, 0, 2, 4)
FLIPPED = (False, True, False, False, True)


def gram_into(x_ref, gram):
    rows = gram.shape[0]
    starts = list(range(0, rows, 256))
    for j in starts:
        n = min(256, rows - j)
        gram[j:rows, j : j + n] = dot_nt(x_ref[j:rows, :], x_ref[j : j + n, :])
    for j in starts:
        n = min(256, rows - j)
        if j + n < rows:
            gram[j : j + n, j + n : rows] = gram[j + n : rows, j : j + n].T


def newton_step(x_ref, gram, mixer, high, low, first, refined):
    gram_into(x_ref, gram)
    rows = gram.shape[0]
    same = lax.broadcasted_iota(jnp.int32, (rows, rows), 0) == lax.broadcasted_iota(
        jnp.int32, (rows, rows), 1
    )
    whole = gram[...]
    scale = None
    if first:
        scale = 1.0 / (jnp.sqrt(jnp.sum(jnp.where(same, whole, 0.0))) + frobenius_epsilon)
        whole = whole * (scale * scale)
        gram[...] = whole
    high[...] = whole.astype(bf16)
    squared = dot(high[...], high[...])
    if refined:
        low[...] = (gram[...] - high[...].astype(f32)).astype(bf16)
        squared = squared + dot(high[...], low[...]) + dot(low[...], high[...])
    mix = (
        jnp.where(same, newton_first, 0.0) + newton_second * gram[...] + newton_third * squared
    )
    if first:
        mix = mix * scale
    mixer[...] = mix.astype(bf16)
    width = x_ref.shape[1]
    tile = 1024 if width % 1024 == 0 else width

    @pl.loop(0, width // tile)
    def _(t):
        cols = pl.ds(pl.multiple_of(t * tile, tile), tile)
        x_ref[:, cols] = dot(mixer[...], x_ref[:, cols]).astype(bf16)


def muon_kernel(shapes, *refs):
    sources, results = refs[0:10], refs[10:15]
    outgoing, arrived = refs[15:20], refs[20:25]
    x_all, gram, mixer, high, low = refs[25:30]
    gather_send, gather_recv, scatter_send, scatter_recv, load_sem = refs[30:35]
    loaded = refs[35:45]
    grads, moments = loaded[0:5], loaded[5:10]
    loads = [
        pltpu.make_async_copy(source, target, load_sem.at[k])
        for k, (source, target) in enumerate(zip(sources, loaded))
    ]
    for load in loads:
        load.start()
    rep, me, lane, lanes = place()

    def device(member):
        return (rep, member * lanes + lane)

    owner_here = me == OWNERS[0]
    for owner in OWNERS[1:]:
        owner_here = owner_here | (me == owner)

    @pl.when(owner_here)
    def _():
        x_all[...] = jnp.zeros_like(x_all)

    barrier = pltpu.get_barrier_semaphore()
    for step in range(1, GROUP):
        pl.semaphore_signal(
            barrier, inc=1, device_id=device(me ^ step), device_id_type=MESH
        )

    def block(number, member):
        rows, cols = shapes[number]
        if FLIPPED[number]:
            return x_all.at[:, pl.ds(member * rows, rows)]
        return x_all.at[pl.ds(member * rows, rows), pl.ds(0, cols)]

    for number in (2, 3, 4, 0, 1):
        loads[number].wait()
        loads[5 + number].wait()
        grad = jnp.concatenate(
            [grads[number][0], grads[number][1]], axis=0 if number in (OUT, DOWN) else 1
        ).astype(f32)
        new = momentum_decay * moments[number][...] + (1.0 - momentum_decay) * grad
        nesterov = (1.0 - momentum_decay) * grad + momentum_decay * new
        if FLIPPED[number]:
            nesterov = nesterov.T
        outgoing[number][...] = nesterov.astype(bf16)
    pl.semaphore_wait(barrier, GROUP - 1)

    def gather_copy(number, member, sender):
        rows, _ = shapes[number]
        if FLIPPED[number]:
            start = pl.multiple_of(sender * rows, rows)
            target = x_all.at[:, pl.ds(start, rows)]
        else:
            start = pl.multiple_of(sender * rows, 16)
            target = x_all.at[pl.ds(start, rows), pl.ds(0, shapes[number][1])]
        return pltpu.make_async_remote_copy(
            src_ref=outgoing[number],
            dst_ref=target,
            send_sem=gather_send.at[number],
            recv_sem=gather_recv.at[sender],
            device_id=device(member),
            device_id_type=MESH,
        )

    for number in (2, 3, 4, 0, 1):

        @pl.when(me != OWNERS[number])
        def _():
            gather_copy(number, OWNERS[number], me).start()

    for number in range(5):
        owner = OWNERS[number]

        @pl.when(me == owner)
        def _():
            rows, cols = shapes[number]
            if FLIPPED[number]:
                x_all[:, owner * rows : (owner + 1) * rows] = outgoing[number][...]
            else:
                x_all[owner * rows : (owner + 1) * rows, 0:cols] = outgoing[number][...]
            for step in range(1, GROUP):
                gather_copy(number, owner, owner ^ step).wait_recv()

    @pl.when(owner_here)
    def _():
        newton_step(x_all, gram, mixer, high, low, True, False)

        @pl.loop(0, NS_STEPS - 3)
        def _(k):
            newton_step(x_all, gram, mixer, high, low, False, False)

        @pl.loop(0, 2)
        def _(k):
            newton_step(x_all, gram, mixer, high, low, False, True)

    def scatter_copy(number, member):
        rows, cols = shapes[number]
        return pltpu.make_async_remote_copy(
            src_ref=block(number, member),
            dst_ref=arrived[number],
            send_sem=scatter_send.at[member],
            recv_sem=scatter_recv.at[number],
            device_id=device(member),
            device_id_type=MESH,
        )

    for number in range(5):
        owner = OWNERS[number]

        @pl.when(me == owner)
        def _():
            for step in range(1, GROUP):
                scatter_copy(number, owner ^ step).start()
            arrived[number][...] = block(number, owner)[...]

    for number in range(5):
        owner = OWNERS[number]

        @pl.when(me != owner)
        def _():
            scatter_copy(number, owner).wait_recv()

        update = arrived[number][...]
        if FLIPPED[number]:
            update = update.astype(f32).T.astype(bf16)
        results[number][...] = update

    for number in range(5):
        owner = OWNERS[number]

        @pl.when(me == owner)
        def _():
            for step in range(1, GROUP):
                scatter_copy(number, owner ^ step).wait_send()

        @pl.when(me != owner)
        def _():
            gather_copy(number, owner, me).wait_send()


def muon(grads, moments):
    shapes = tuple(moment.shape for moment in moments)
    flipped = [s[::-1] if flip else s for s, flip in zip(shapes, FLIPPED)]
    side = shapes[0][0] * GROUP
    width = max(s[0] * GROUP if flip else s[1] for s, flip in zip(shapes, FLIPPED))
    vmem = pl.BlockSpec(memory_space=pltpu.VMEM)
    return pl.pallas_call(
        lambda *refs: muon_kernel(shapes, *refs),
        out_shape=[jax.ShapeDtypeStruct(s, bf16) for s in shapes],
        in_specs=[pl.BlockSpec(memory_space=pl.ANY)] * 10,
        out_specs=[vmem] * 5,
        scratch_shapes=[pltpu.VMEM(s, bf16) for s in flipped]
        + [pltpu.VMEM(s, bf16) for s in flipped]
        + [
            pltpu.VMEM((side, width), bf16),
            pltpu.VMEM((side, side), f32),
            pltpu.VMEM((side, side), bf16),
            pltpu.VMEM((side, side), bf16),
            pltpu.VMEM((side, side), bf16),
            pltpu.SemaphoreType.DMA((5,)),
            pltpu.SemaphoreType.DMA((GROUP,)),
            pltpu.SemaphoreType.DMA((GROUP,)),
            pltpu.SemaphoreType.DMA((5,)),
            pltpu.SemaphoreType.DMA((10,)),
        ]
        + [pltpu.VMEM(term.shape, term.dtype) for term in (*grads, *moments)],
        compiler_params=pltpu.CompilerParams(
            collective_id=1, has_side_effects=True, vmem_limit_bytes=63 * 2**20
        ),
        name="muon",
    )(*grads, *moments)


def finish_kernel(factors, *refs):
    grads, updates, moments, weights = refs[0:5], refs[5:10], refs[10:15], refs[15:20]
    streams, (small, gains, first, second) = refs[20:22], refs[22:26]
    wide, news, masters = refs[26:31], refs[31:36], refs[36:41]
    stream_out = refs[41:43]
    gain_grad, first_new, second_new, master_gains, statistics = refs[43:48]
    here = lax.axis_index("fsdp")
    for number in range(5):
        grad = grads[number][0].astype(f32)
        wide[number][...] = grad
        news[number][...] = (
            momentum_decay * moments[number][...] + (1.0 - momentum_decay) * grad
        )
        masters[number][...] = weights[number][...].astype(f32) - factors[number] * updates[
            number
        ][...].astype(f32)
    for source, target in zip(streams, stream_out):
        target[...] = source[...]

    @pl.when(pl.program_id(0) == 0)
    def _():
        kinds, count = gains.shape
        width = small.shape[1]
        shift = lax.rem(width - here * count, width)
        grad = pltpu.roll(small[...], shift, 1)[0:kinds, 0:count]
        gain_grad[...] = grad
        gains_local = gains[...].astype(f32)
        first_next = first_decay * first[...] + (1.0 - first_decay) * grad
        second_next = second_decay * second[...] + (1.0 - second_decay) * grad * grad
        first_new[...] = first_next
        second_new[...] = second_next
        first_hat = first_next / (1.0 - first_decay**ADAM_STEP)
        second_hat = second_next / (1.0 - second_decay**ADAM_STEP)
        master_gains[...] = gains_local - adam_rate * (
            first_hat / (jnp.sqrt(second_hat) + adam_epsilon) + weight_decay * gains_local
        )
        statistics[...] = jnp.sqrt(small[4:5, 0:4] / (small[4:5, 4:5] * width))


def finish(grads, updates, moments, weights, streams, small, gains, first, second):
    steps = 4
    shapes = tuple(moment.shape for moment in moments)
    factors = [max(1.0, s[0] * GROUP / s[1]) ** 0.5 * muon_rate for s in shapes]
    halves, wholes = [], []
    for number, (rows, cols) in enumerate(shapes):
        if number in (OUT, DOWN):
            halves.append(pl.BlockSpec((1, rows // steps, cols), lambda j: (j // 2, j % 2, 0)))
            wholes.append(pl.BlockSpec((rows // steps, cols), lambda j: (j, 0)))
        else:
            halves.append(pl.BlockSpec((1, rows, cols // steps), lambda j: (j // 2, 0, j % 2)))
            wholes.append(pl.BlockSpec((rows, cols // steps), lambda j: (0, j)))
    lines = [
        pl.BlockSpec((s.shape[0] // steps, s.shape[1]), lambda j: (j, 0)) for s in streams
    ]
    single = lambda shape: pl.BlockSpec(shape, lambda j: (0, 0))
    table = single(gains.shape)
    out = pl.pallas_call(
        lambda *refs: finish_kernel(factors, *refs),
        grid=(steps,),
        out_shape=[jax.ShapeDtypeStruct(s, f32) for s in shapes * 3]
        + [jax.ShapeDtypeStruct(s.shape, f32) for s in streams]
        + [jax.ShapeDtypeStruct(gains.shape, f32)] * 4
        + [jax.ShapeDtypeStruct((1, 4), f32)],
        in_specs=halves + wholes * 3 + lines + [single(small.shape)] + [table] * 3,
        out_specs=wholes * 3 + lines + [table] * 4 + [single((1, 4))],
        compiler_params=pltpu.CompilerParams(vmem_limit_bytes=63 * 2**20),
        name="finish",
    )(*grads, *updates, *moments, *weights, *streams, small, gains, first, second)
    return out[0:5], out[5:10], out[10:15], out[15:17], out[17:21], out[21]


def shards(
    tokens,
    cotangent,
    prefix,
    w_qkv,
    w_out,
    w_gate,
    w_up,
    w_down,
    gains,
    moment_qkv,
    moment_out,
    moment_gate,
    moment_up,
    moment_down,
    gain_first,
    gain_second,
):
    reps = lax.axis_size("rep")
    _, _, lane, lanes = place()
    teams = [[member * lanes + k for k in range(lanes)] for member in range(GROUP)]

    def joined(shard):
        if lanes == 1:
            return shard
        return lax.all_gather(shard, "fsdp", axis=0, tiled=True, axis_index_groups=teams)

    def summed(term):
        if lanes == 1:
            return term
        parts = lax.all_gather(term, "fsdp", axis_index_groups=teams)
        return jnp.sum(parts.astype(f32), axis=0).astype(term.dtype)

    def parted(block):
        if lanes == 1:
            return block
        size = block.shape[0] // lanes
        return lax.dynamic_slice_in_dim(block, lane * size, size, 0)

    half_dim = jnp.arange(HEAD_DIM // 2, dtype=f32)
    frequency = (rotary_base ** (-(half_dim * 2.0 / HEAD_DIM)))[None, :]
    weights = [joined(term) for term in (w_qkv, w_out, w_gate, w_up, w_down)]
    moments = [
        joined(term)
        for term in (moment_qkv, moment_out, moment_gate, moment_up, moment_down)
    ]
    output, d_tokens, small, halves = layer(
        prefix, tokens, cotangent, frequency, joined(gains).T, weights, reps
    )
    halves = [summed(term) for term in halves]
    small = summed(small)
    updates = muon(halves, moments)
    grads, news, masters, streams, gain_terms, statistics = finish(
        halves,
        updates,
        moments,
        weights,
        (output, d_tokens),
        small,
        gains.T,
        gain_first.T,
        gain_second.T,
    )
    gain_terms = [term.T for term in gain_terms]
    grads, news, masters = (
        [parted(term) for term in group] for group in (grads, news, masters)
    )
    return (
        *streams,
        *grads,
        gain_terms[0],
        *news,
        *masters,
        *gain_terms[1:],
        statistics.reshape(4),
    )


def solution(mesh):
    in_specs = (
        P(("rep", "fsdp"), None),
        P(("rep", "fsdp"), None),
        P(),
        P("fsdp", None),
        P("fsdp", None),
        P("fsdp", None),
        P("fsdp", None),
        P("fsdp", None),
        P("fsdp", None),
        P("fsdp", None),
        P("fsdp", None),
        P("fsdp", None),
        P("fsdp", None),
        P("fsdp", None),
        P("fsdp", None),
        P("fsdp", None),
    )
    out_specs = (
        P(("rep", "fsdp"), None),
        P(("rep", "fsdp"), None),
        P("fsdp", None),
        P("fsdp", None),
        P("fsdp", None),
        P("fsdp", None),
        P("fsdp", None),
        P("fsdp", None),
        P("fsdp", None),
        P("fsdp", None),
        P("fsdp", None),
        P("fsdp", None),
        P("fsdp", None),
        P("fsdp", None),
        P("fsdp", None),
        P("fsdp", None),
        P("fsdp", None),
        P("fsdp", None),
        P("fsdp", None),
        P("fsdp", None),
        P("fsdp", None),
        P(),
    )
    return jax.shard_map(shards, mesh=mesh, in_specs=in_specs, out_specs=out_specs, check_vma=False)
```

```python
import jax
import jax.numpy as jnp
from jax import lax
from jax.experimental import pallas as pl
from jax.experimental.pallas import tpu as pltpu
from jax.sharding import PartitionSpec as P

HEADS = 4
HEAD_DIM = 256
NS_STEPS = 5
ADAM_STEP = 10


norm_epsilon = 1e-06
soft_cap = 50.0
rotary_base = 10000.0
newton_first = 3.4445
newton_second = -4.775
newton_third = 2.0315
momentum_decay = 0.95
muon_rate = 1.0
first_decay = 0.9
second_decay = 0.95
adam_rate = 1.0
weight_decay = 0.1
adam_epsilon = 1e-08
frobenius_epsilon = 1e-07

GROUP = 8
MESH = pl.DeviceIdType.MESH
f32 = jnp.float32
bf16 = jnp.bfloat16


def dot(a, b):
    return lax.dot_general(a, b, (((1,), (0,)), ((), ())), preferred_element_type=f32)


def dot_nt(a, b):
    return lax.dot_general(a, b, (((1,), (1,)), ((), ())), preferred_element_type=f32)


def dot_tn(a, b):
    return lax.dot_general(a, b, (((0,), (0,)), ((), ())), preferred_element_type=f32)


def place():
    size = lax.axis_size("fsdp")
    lanes = size // GROUP
    here = lax.axis_index("fsdp")
    return lax.axis_index("rep"), here // lanes, lax.rem(here, lanes), lanes


QKV, OUT, GATE, UP, DOWN = range(5)
CORE, ACROSS, ALONG = 1, 2, 4
PAIRS = (
    ((GATE, 0), (UP, 0)),
    ((DOWN, 0), (GATE, 1)),
    ((UP, 1), (DOWN, 1)),
    ((OUT, 0), (OUT, 1)),
    ((QKV, 0), (QKV, 1)),
)
CHUNK = 128
TILE = 256


def split_shape(number, shape):
    rows, cols = shape
    return (rows // 2, cols) if number in (OUT, DOWN) else (rows, cols // 2)


def layer_names(rows, keys, width, shapes, reps):
    halves = [split_shape(number, shape) for number, shape in enumerate(shapes)]
    feats = HEADS * HEAD_DIM
    inner = shapes[GATE][1]
    spaces = {}
    for number, (height, cols) in enumerate(shapes):
        spaces[f"whole{number}"] = pltpu.VMEM((height * GROUP, cols), bf16)
    spaces.update(
        cosine=pltpu.VMEM((rows, HEAD_DIM // 2), f32),
        sine=pltpu.VMEM((rows, HEAD_DIM // 2), f32),
        gain_parts=pltpu.VMEM((GROUP, 8, 128), f32),
        gains=pltpu.VMEM((8, width), f32),
        normed=pltpu.VMEM((rows, width), bf16),
        one_t=pltpu.VMEM((width, rows), bf16),
        two_t=pltpu.VMEM((width, rows), bf16),
        proj=pltpu.VMEM((rows, feats + 2 * HEAD_DIM), bf16),
        key=pltpu.VMEM((keys, HEAD_DIM), bf16),
        value=pltpu.VMEM((keys, HEAD_DIM), bf16),
        key_t=pltpu.VMEM((HEAD_DIM, keys), bf16),
        value_t=pltpu.VMEM((HEAD_DIM, keys), bf16),
        att=pltpu.VMEM((rows, feats), bf16),
        att_t=pltpu.VMEM((feats, rows), bf16),
        inverse=pltpu.VMEM((8, rows), f32),
        branch=pltpu.VMEM((rows, width), f32),
        hidden=pltpu.VMEM((rows, width), f32),
        slope=pltpu.VMEM((rows, inner), bf16),
        bend=pltpu.VMEM((rows, inner), bf16),
        active=pltpu.VMEM((rows, inner), bf16),
        d_key=pltpu.VMEM((keys, HEAD_DIM), f32),
        d_value=pltpu.VMEM((keys, HEAD_DIM), f32),
        swap_in=pltpu.VMEM((rows, 2 * HEAD_DIM), bf16),
        squares=pltpu.VMEM((8, width), f32),
        d_gains=pltpu.VMEM((8, width), f32),
        small_parts=pltpu.VMEM((GROUP, 8, width), f32),
        small_reps=pltpu.VMEM((reps, 8, width), f32),
    )
    for number, half in enumerate(halves):
        spaces[f"stage{number}"] = pltpu.VMEM((2, 2, 2, 2) + half, bf16)
        spaces[f"chip{number}"] = pltpu.VMEM((2, 2, 2) + half, bf16)
        spaces[f"pair{number}"] = pltpu.VMEM((2, 2) + half, bf16)
        spaces[f"plane{number}"] = pltpu.VMEM((2,) + half, bf16)
        spaces[f"line{number}"] = pltpu.VMEM((2, 2) + half, bf16)
        spaces[f"total{number}"] = pltpu.VMEM((2,) + half, bf16)
    dma = pltpu.SemaphoreType.DMA
    spaces.update(
        own_sem=dma((5,)),
        result_sem=dma((5,)),
        weight_send=dma((5, 11)),
        weight_recv=dma((5, 11)),
        gain_send=dma((GROUP,)),
        gain_recv=dma((GROUP,)),
        key_send=dma((2,)),
        key_recv=dma((2,)),
        swap_send=dma((1,)),
        swap_recv=dma((1,)),
        chip_send=dma((5, 2)),
        chip_recv=dma((5, 2)),
        pair_send=dma((5, 2)),
        pair_recv=dma((5, 2)),
        plane_send=dma((5, 2)),
        plane_recv=dma((5, 2)),
        line_send=dma((5, 2)),
        line_recv=dma((5, 2, 2)),
        total_send=dma((5, 2)),
        total_recv=dma((5, 2)),
        small_send=dma((GROUP,)),
        small_recv=dma((GROUP,)),
        reps_send=dma((reps,)),
        reps_recv=dma((reps,)),
    )
    return spaces


class Refs:
    def __init__(self, names, refs):
        self.__dict__.update(zip(names, refs))


def column_sum(x):
    return jnp.sum(x, axis=0, keepdims=True)


def row_mean(x):
    return jnp.mean(x, axis=-1, keepdims=True)


def layer_kernel(names, shapes, *refs):
    v = Refs(names, refs)
    rep, me, lane, lanes = place()
    reps = lax.axis_size("rep")
    here = lax.axis_index("fsdp")
    core, across, along = me % 2, (me // 2) % 2, me // 4
    rows, width = v.tokens.shape
    parity = here % 2
    weights = [v.w_qkv, v.w_out, v.w_gate, v.w_up, v.w_down]
    named = lambda name: [getattr(v, f"{name}{number}") for number in range(5)]
    whole, stage, chip, pair = named("whole"), named("stage"), named("chip"), named("pair")
    plane, line, total, result = named("plane"), named("line"), named("total"), named("grad")

    def device(member):
        return (rep, member * lanes + lane)

    def remote(src, dst, send, recv, where):
        return pltpu.make_async_remote_copy(
            src_ref=src,
            dst_ref=dst,
            send_sem=send,
            recv_sem=recv,
            device_id=where,
            device_id_type=MESH,
        )

    barrier = pltpu.get_barrier_semaphore()
    greeted = [device(me ^ step) for step in range(1, GROUP)]
    greeted += [(lax.rem(rep + step, reps), here) for step in range(1, reps)]
    if lanes > 1:
        greeted.append((rep, here ^ 1))
    for where in greeted:
        pl.semaphore_signal(barrier, inc=1, device_id=where, device_id_type=MESH)
    pl.semaphore_wait(barrier, len(greeted))

    odd = rep % 2

    def parts(number):
        rows_or_cols, tile = shapes[number][1], 128
        if number in (OUT, DOWN):
            rows_or_cols, tile = shapes[number][0], 16
        outer = (rows_or_cols // tile + 1) // 3 * tile
        return outer, rows_or_cols - 2 * outer, tile

    def window(number, member, start, size, tile):
        height = shapes[number][0]
        base = pl.multiple_of(member * height, 16)
        if number in (OUT, DOWN):
            return whole[number].at[pl.ds(pl.multiple_of(base + start, 16), size), :]
        return whole[number].at[pl.ds(base, height), pl.ds(pl.multiple_of(start, 128), size)]

    def slot(number, member):
        height = shapes[number][0]
        return whole[number].at[pl.ds(pl.multiple_of(member * height, 16), height), :]

    def outer_part(number, member):
        outer, middle, tile = parts(number)
        return window(number, member, odd * (outer + middle), outer, tile)

    def middle_part(number, member):
        outer, middle, tile = parts(number)
        return window(number, member, outer, middle, tile)

    def own_parts(number):
        outer, middle, tile = parts(number)
        start = pl.multiple_of(odd * outer, tile)
        if number in (OUT, DOWN):
            return weights[number].at[pl.ds(start, outer + middle), :]
        return weights[number].at[:, pl.ds(start, outer + middle)]

    def both_parts(number, member):
        outer, middle, tile = parts(number)
        return window(number, member, odd * outer, outer + middle, tile)

    def weight_copy(number, kind):
        beside, ahead = me ^ ACROSS, me ^ ALONG
        corner = beside ^ ALONG
        if kind == 0:
            src, dst, where = weights[number], slot(number, me), device(me ^ CORE)
        elif kind < 3:
            src, dst = own_parts(number), both_parts(number, me)
            where = device((beside, ahead)[kind - 1])
        elif kind < 5:
            src = outer_part(number, beside) if kind == 3 else middle_part(number, ahead)
            dst, where = src, device((ahead, beside)[kind - 3])
        elif kind < 8:
            src = outer_part(number, (beside, ahead, corner)[kind - 5])
            dst, where = src, (rep + 1 - 2 * odd, here)
        else:
            src = slot(number, (beside, ahead, corner)[kind - 8])
            dst, where = src, device(me ^ CORE)
        return remote(
            src, dst, v.weight_send.at[number, kind], v.weight_recv.at[number, kind], where
        )

    def own_copy(number):
        return pltpu.make_async_copy(weights[number], slot(number, me), v.own_sem.at[number])

    def weight_begin(number):
        for kind in (1, 2, 0):
            weight_copy(number, kind).start()
        own_copy(number).start()

    def weight_forward(number):
        weight_copy(number, 1).wait_recv()
        weight_copy(number, 3).start()
        weight_copy(number, 5).start()
        weight_copy(number, 2).wait_recv()
        weight_copy(number, 4).start()
        weight_copy(number, 6).start()

    def weight_corner(number):
        weight_copy(number, 3).wait_recv()
        weight_copy(number, 7).start()

    def weight_cross(number):
        weight_copy(number, 5).wait_recv()
        weight_copy(number, 8).start()
        weight_copy(number, 6).wait_recv()
        weight_copy(number, 9).start()
        weight_copy(number, 4).wait_recv()
        weight_copy(number, 7).wait_recv()
        weight_copy(number, 10).start()

    def weight_ready(number):
        own_copy(number).wait()
        for kind in (0, 8, 9, 10):
            weight_copy(number, kind).wait_recv()

    weight_begin(QKV)

    def gain_copy(step):
        return remote(
            v.gain_parts.at[me],
            v.gain_parts.at[me],
            v.gain_send.at[step],
            v.gain_recv.at[step],
            device(me ^ step),
        )

    gain_count, gain_rows = v.gain_block.shape
    v.gain_parts[me] = jnp.zeros_like(v.gain_parts[me])
    v.gain_parts[me, 0:gain_count, 0:gain_rows] = v.gain_block[...].astype(f32)
    for step in range(1, GROUP):
        gain_copy(step).start()
    weight_begin(OUT)
    weight_begin(GATE)
    v.squares[...] = jnp.zeros_like(v.squares)
    v.d_gains[...] = jnp.zeros_like(v.d_gains)
    v.d_key[...] = jnp.zeros_like(v.d_key)
    v.d_value[...] = jnp.zeros_like(v.d_value)
    spot = lax.broadcasted_iota(jnp.int32, (rows, HEAD_DIM // 2), 0) + parity * rows
    angles = spot.astype(f32) * v.frequency[...]
    v.cosine[...] = jnp.cos(angles)
    v.sine[...] = jnp.sin(angles)
    for step in range(1, GROUP):
        gain_copy(step).wait_recv()
    for member in range(GROUP):
        v.gains[:, member * gain_rows : (member + 1) * gain_rows] = v.gain_parts[
            member, :, 0:gain_rows
        ]

    prefix = v.prefix[(rep * lax.axis_size("fsdp") + here) // 2]

    def valid_rows(start, count):
        spot = lax.broadcasted_iota(jnp.int32, (count, 1), 0) + (parity * rows + start)
        return jnp.where(spot >= prefix, 1.0, 0.0)

    def by_rows(body):
        @pl.loop(0, rows // CHUNK)
        def _(k):
            start = pl.multiple_of(k * CHUNK, CHUNK)
            body(pl.ds(start, CHUNK), start)

    def by_columns(count, body):
        @pl.loop(0, count // TILE)
        def _(k):
            body(pl.ds(pl.multiple_of(k * TILE, TILE), TILE), k)

    def inverse_root(x):
        return lax.rsqrt(row_mean(x * x) + norm_epsilon)

    def norm_back(x, scale, upstream, gain, row):
        v.d_gains[row : row + 1, :] += column_sum(upstream * x * scale)
        spread = upstream * gain
        return scale * spread - x * (scale * scale * scale * row_mean(x * spread))

    gain_row = lambda k: v.gains[k : k + 1, :]

    def first_norm(here_rows, start):
        x = v.tokens[here_rows, :].astype(f32)
        normed = x * inverse_root(x) * gain_row(0)
        v.normed[here_rows, :] = normed.astype(bf16)
        v.one_t[:, here_rows] = normed.T.astype(bf16)
        v.squares[0:1, :] += column_sum(valid_rows(start, CHUNK) * (x * x))

    by_rows(first_norm)
    weight_forward(QKV)
    weight_corner(QKV)
    weight_forward(OUT)
    weight_begin(UP)
    weight_cross(QKV)
    weight_corner(OUT)
    weight_ready(QKV)

    feats = HEADS * HEAD_DIM
    half_dim = HEAD_DIM // 2
    own_rows = pl.ds(pl.multiple_of(parity * rows, rows), rows)
    other_rows = pl.ds(pl.multiple_of((1 - parity) * rows, rows), rows)

    def rotate(x, sign):
        first, second = x[:, :half_dim], x[:, half_dim:]
        cosine, sine = v.cosine[...], v.sine[...] * sign
        return first * cosine - second * sine, second * cosine + first * sine

    def key_copy(number):
        ref = (v.key, v.value)[number]
        return remote(
            ref.at[own_rows, :],
            ref.at[own_rows, :],
            v.key_send.at[number],
            v.key_recv.at[number],
            (rep, here ^ 1),
        )

    key_part = dot(v.normed[...], whole[QKV][:, feats : feats + HEAD_DIM])
    first, second = rotate(key_part, 1.0)
    v.key[own_rows, :half_dim] = first.astype(bf16)
    v.key[own_rows, half_dim:] = second.astype(bf16)
    key_copy(0).start()
    v.value[own_rows, :] = dot(v.normed[...], whole[QKV][:, feats + HEAD_DIM :]).astype(bf16)
    key_copy(1).start()

    @pl.loop(0, HEADS)
    def _(head):
        start = pl.multiple_of(head * HEAD_DIM, HEAD_DIM)
        part = dot(v.normed[...], whole[QKV][:, pl.ds(start, HEAD_DIM)])
        first, second = rotate(part, 1.0)
        v.proj[:, pl.ds(start, half_dim)] = first.astype(bf16)
        v.proj[:, pl.ds(start + half_dim, half_dim)] = second.astype(bf16)

    weight_forward(GATE)
    weight_begin(DOWN)
    for number in range(2):
        key_copy(number).wait_recv()
    v.key_t[...] = v.key[...].astype(f32).T.astype(bf16)
    v.value_t[...] = v.value[...].astype(f32).T.astype(bf16)

    keys = v.key.shape[0]
    bend_scale = HEAD_DIM ** (-0.5) / soft_cap

    def scores(head, start):
        here_rows = pl.ds(start, TILE)
        query = v.proj[here_rows, head * HEAD_DIM : (head + 1) * HEAD_DIM]
        bent = jnp.tanh(dot_nt(v.key[...], query) * bend_scale)
        spot = lax.broadcasted_iota(jnp.int32, (1, TILE), 1) + (parity * rows + start)
        last = jnp.maximum(spot, prefix - 1)
        allowed = lax.broadcasted_iota(jnp.int32, (keys, TILE), 0) <= last
        return bent, jnp.where(allowed, jnp.exp(soft_cap * bent), 0.0), query

    def attend(head, start):
        cols = slice(head * HEAD_DIM, (head + 1) * HEAD_DIM)
        here_rows = pl.ds(start, TILE)
        _, power, _ = scores(head, start)
        inverse = 1.0 / column_sum(power)
        v.inverse[head : head + 1, here_rows] = inverse
        mixed = dot(v.value_t[...], (power * inverse).astype(bf16))
        v.att_t[cols, here_rows] = mixed.astype(bf16)
        v.att[here_rows, cols] = mixed.T.astype(bf16)

    weight_cross(OUT)
    attend(0, 0 * TILE)
    weight_corner(GATE)
    attend(0, 1 * TILE)
    weight_forward(UP)
    attend(1, 0 * TILE)
    weight_cross(GATE)
    attend(1, 1 * TILE)
    weight_corner(UP)
    attend(2, 0 * TILE)
    weight_forward(DOWN)
    attend(2, 1 * TILE)
    weight_cross(UP)
    attend(3, 0 * TILE)
    weight_corner(DOWN)
    attend(3, 1 * TILE)
    weight_ready(OUT)

    v.branch[...] = dot(v.att[...], whole[OUT][...])

    def second_norm(here_rows, start):
        x = v.branch[here_rows, :]
        first_out = x * inverse_root(x) * gain_row(1)
        hidden = v.tokens[here_rows, :].astype(f32) + first_out
        v.hidden[here_rows, :] = hidden
        normed = hidden * inverse_root(hidden) * gain_row(2)
        v.normed[here_rows, :] = normed.astype(bf16)
        v.two_t[:, here_rows] = normed.T.astype(bf16)
        v.squares[1:2, :] += column_sum(valid_rows(start, CHUNK) * (first_out * first_out))

    by_rows(second_norm)
    weight_ready(GATE)
    weight_ready(UP)
    inner = shapes[GATE][1]

    def feed(cols, k):
        gate = dot(v.normed[...], whole[GATE][:, cols])
        upward = dot(v.normed[...], whole[UP][:, cols])
        square = gate * gate
        bent = jnp.tanh(0.7978845608028654 * (gate + 0.044715 * gate * square))
        open_half = 0.5 * (1.0 + bent)
        smooth = gate * open_half
        steep = open_half + gate * (1.0 - bent * bent) * (
            0.3989422804014327 * (1.0 + 3.0 * 0.044715 * square)
        )
        v.active[:, cols] = (smooth * upward).astype(bf16)
        v.bend[:, cols] = smooth.astype(bf16)
        v.slope[:, cols] = (steep * upward).astype(bf16)

    by_columns(inner, feed)
    weight_cross(DOWN)
    weight_ready(DOWN)

    v.d_tokens[...] = dot(v.active[...], whole[DOWN][...])

    def last_norm(here_rows, start):
        x = v.d_tokens[here_rows, :]
        scale = inverse_root(x)
        second_out = x * scale * gain_row(3)
        final = v.hidden[here_rows, :] + second_out
        v.output[here_rows, :] = final
        valid = valid_rows(start, CHUNK)
        v.squares[2:3, :] += column_sum(valid * (second_out * second_out))
        v.squares[3:4, :] += column_sum(valid * (final * final))
        upstream = v.cotangent[here_rows, :].astype(f32)
        v.normed[here_rows, :] = norm_back(x, scale, upstream, gain_row(3), 3).astype(bf16)

    by_rows(last_norm)

    def first_across(number, half):
        return any(one == (number, half) for one, _ in PAIRS)

    def chip_copy(number, half):
        return remote(
            stage[number].at[half, :, :, 1 - core],
            chip[number].at[half],
            v.chip_send.at[number, half],
            v.chip_recv.at[number, half],
            device(me ^ CORE),
        )

    def pair_copy(number, half):
        if first_across(number, half):
            src, where = chip[number].at[half, :, 1 - across], me ^ ACROSS
        else:
            src, where = chip[number].at[half, 1 - along], me ^ ALONG
        return remote(
            src,
            pair[number].at[half],
            v.pair_send.at[number, half],
            v.pair_recv.at[number, half],
            device(where),
        )

    def plane_copy(number, half):
        if first_across(number, half):
            src, where = pair[number].at[half, 1 - along], me ^ ALONG
        else:
            src, where = pair[number].at[half, 1 - across], me ^ ACROSS
        return remote(
            src,
            plane[number].at[half],
            v.plane_send.at[number, half],
            v.plane_recv.at[number, half],
            device(where),
        )

    def added(one, two):
        return (one.astype(f32) + two.astype(f32)).astype(bf16)

    def chip_begin(number, half):
        chip_copy(number, half).start()

    def chip_end(number, half):
        chip_copy(number, half).wait_recv()

        @pl.loop(0, 4)
        def _(k):
            one, two = k // 2, k % 2
            chip[number][half, one, two] = added(
                chip[number][half, one, two], stage[number][half, one, two, core]
            )

        pair_copy(number, half).start()

    def pair_end(number, half):
        pair_copy(number, half).wait_recv()

        @pl.loop(0, 2)
        def _(k):
            if first_across(number, half):
                mine = chip[number][half, k, across]
            else:
                mine = chip[number][half, along, k]
            pair[number][half, k] = added(pair[number][half, k], mine)

        plane_copy(number, half).start()

    def plane_end(number, half):
        plane_copy(number, half).wait_recv()
        kept = along if first_across(number, half) else across
        plane[number][half] = added(plane[number][half], pair[number][half, kept])

        @pl.when(at_end)
        def _():
            line_send(number, half)

    order = [half for both in PAIRS for half in both]

    on_left = rep < reps // 2
    inward = jnp.where(on_left, 1, -1)
    at_end = (rep == 0) | (rep == reps - 1)
    at_middle = (rep == reps // 2 - 1) | (rep == reps // 2)

    def line_copy(number, half, way):
        return remote(
            plane[number].at[half],
            line[number].at[half, way],
            v.line_send.at[number, half],
            v.line_recv.at[number, half, way],
            (rep + inward, here),
        )

    def total_copy(number, half):
        return remote(
            total[number].at[half],
            total[number].at[half],
            v.total_send.at[number, half],
            v.total_recv.at[number, half],
            (rep - inward, here),
        )

    def line_send(number, half):
        @pl.when(jnp.logical_not(at_middle))
        def _():
            line_copy(number, half, 0).start()

        @pl.when(at_middle)
        def _():
            line_copy(number, half, 1).start()

    def line_begin(number, half):
        @pl.when(jnp.logical_not(at_end))
        def _():
            line_copy(number, half, 0).wait_recv()
            plane[number][half] = added(plane[number][half], line[number][half, 0])
            line_send(number, half)

    def line_end(number, half):
        @pl.when(at_middle)
        def _():
            line_copy(number, half, 1).wait_recv()
            total[number][half] = added(plane[number][half], line[number][half, 1])

            @pl.when(jnp.logical_not(at_end))
            def _():
                total_copy(number, half).start()

    def total_end(number, half):
        @pl.when(jnp.logical_not(at_middle))
        def _():
            total_copy(number, half).wait_recv()

            @pl.when(jnp.logical_not(at_end))
            def _():
                total_copy(number, half).start()

    def for_pair(action, index):
        for number, half in PAIRS[index]:
            action(number, half)

    def keep_columns(number, col_half, col, found):
        height = shapes[number][0]
        for member in range(GROUP):
            stage[number][
                col_half, member // 4, (member // 2) % 2, member % 2, :, pl.ds(col, TILE)
            ] = found[member * height : (member + 1) * height].astype(bf16)

    down_rows = shapes[DOWN][0]
    halved = inner // 2 // TILE

    def feed_back(side, begin, end):
        @pl.loop(begin, end)
        def _(k):
            col = pl.multiple_of(k * TILE, TILE)
            start = pl.multiple_of(side * (inner // 2) + k * TILE, TILE)
            cols = pl.ds(start, TILE)
            d_active = dot_nt(v.normed[...], whole[DOWN][cols, :])
            d_gate = (d_active * v.slope[:, cols].astype(f32)).astype(bf16)
            d_upward = (d_active * v.bend[:, cols].astype(f32)).astype(bf16)
            v.slope[:, cols] = d_gate
            v.bend[:, cols] = d_upward
            keep_columns(GATE, side, col, dot(v.two_t[...], d_gate))
            keep_columns(UP, side, col, dot(v.two_t[...], d_upward))
            found = dot_tn(v.active[:, cols], v.normed[...]).astype(bf16)
            per = TILE // down_rows
            for part in range(per):
                member = (side * halved + k) * per + part
                y, x, c = member // 4, (member // 2) % 2, member % 2
                base = part * down_rows
                stage[DOWN][0, y, x, c] = found[base : base + down_rows // 2]
                stage[DOWN][1, y, x, c] = found[base + down_rows // 2 : base + down_rows]

    feed_back(0, 0, halved)
    for_pair(chip_begin, 0)
    feed_back(1, 0, halved // 2)
    for_pair(chip_end, 0)
    feed_back(1, halved // 2, halved)
    for_pair(chip_begin, 1)
    for_pair(chip_begin, 2)
    v.d_tokens[...] = dot_nt(v.slope[...], whole[GATE][...])
    for_pair(chip_end, 1)
    v.d_tokens[...] += dot_nt(v.bend[...], whole[UP][...])
    for_pair(chip_end, 2)

    def middle_norms(here_rows, start):
        x = v.hidden[here_rows, :]
        flow = norm_back(x, inverse_root(x), v.d_tokens[here_rows, :], gain_row(2), 2)
        d_hidden = v.cotangent[here_rows, :].astype(f32) + flow
        v.d_tokens[here_rows, :] = d_hidden
        x = v.branch[here_rows, :]
        flow = norm_back(x, inverse_root(x), d_hidden, gain_row(1), 1)
        v.normed[here_rows, :] = flow.astype(bf16)

    by_rows(middle_norms)
    for_pair(pair_end, 0)
    out_rows = shapes[OUT][0]
    v.att[...] = dot_nt(v.normed[...], whole[OUT][...]).astype(bf16)

    @pl.loop(0, GROUP // 2)
    def _(k):
        start = pl.multiple_of(k * 2 * out_rows, 2 * out_rows)
        found = dot(v.att_t[pl.ds(start, 2 * out_rows), :], v.normed[...]).astype(bf16)
        for part in range(4):
            stage[OUT][part % 2, k // 2, k % 2, part // 2] = found[
                part * (out_rows // 2) : (part + 1) * (out_rows // 2)
            ]

    for_pair(chip_begin, 3)
    for_pair(pair_end, 1)
    for_pair(plane_end, 0)

    def attend_back(head):
        cols = slice(head * HEAD_DIM, (head + 1) * HEAD_DIM)

        @pl.loop(0, rows // TILE)
        def _(k):
            start = pl.multiple_of(k * TILE, TILE)
            here_rows = pl.ds(start, TILE)
            bent, power, query = scores(head, start)
            soft = power * v.inverse[head : head + 1, here_rows]
            flow = v.att[here_rows, cols]
            d_soft = dot_nt(v.value[...], flow)
            v.d_value[...] += dot(soft.astype(bf16), flow)
            level = column_sum(d_soft * soft)
            d_raw = soft * (d_soft - level) * ((1.0 - bent * bent) * HEAD_DIM ** (-0.5))
            d_raw = d_raw.astype(bf16)
            v.d_key[...] += dot(d_raw, query)
            d_query = dot(v.key_t[...], d_raw).T
            first, second = d_query[:, :half_dim], d_query[:, half_dim:]
            cosine, sine = v.cosine[here_rows, :], v.sine[here_rows, :]
            base = head * HEAD_DIM
            v.proj[here_rows, base : base + half_dim] = (first * cosine + second * sine).astype(
                bf16
            )
            v.proj[here_rows, base + half_dim : base + HEAD_DIM] = (
                second * cosine - first * sine
            ).astype(bf16)

    swap = remote(
        v.att.at[:, 0 : 2 * HEAD_DIM],
        v.swap_in,
        v.swap_send.at[0],
        v.swap_recv.at[0],
        (rep, here ^ 1),
    )

    attend_back(0)
    for_pair(chip_end, 3)
    attend_back(1)
    for_pair(pair_end, 2)
    attend_back(2)
    for_pair(line_begin, 0)
    for_pair(plane_end, 1)
    attend_back(3)
    v.att[:, 0:HEAD_DIM] = v.d_key[other_rows, :].astype(bf16)
    v.att[:, HEAD_DIM : 2 * HEAD_DIM] = v.d_value[other_rows, :].astype(bf16)
    swap.start()
    for_pair(pair_end, 3)

    qkv_half = split_shape(QKV, shapes[QKV])[1] // TILE

    def projection_grad(tile):
        found = dot(v.one_t[...], v.proj[:, tile * TILE : (tile + 1) * TILE])
        keep_columns(QKV, tile // qkv_half, (tile % qkv_half) * TILE, found)

    for tile in range(qkv_half):
        projection_grad(tile)
    chip_begin(QKV, 0)
    swap.wait_recv()
    d_key = v.d_key[own_rows, :] + v.swap_in[:, 0:HEAD_DIM].astype(f32)
    first, second = rotate(d_key, -1.0)
    v.proj[:, feats : feats + half_dim] = first.astype(bf16)
    v.proj[:, feats + half_dim : feats + HEAD_DIM] = second.astype(bf16)
    v.proj[:, feats + HEAD_DIM :] = (
        v.d_value[own_rows, :] + v.swap_in[:, HEAD_DIM:].astype(f32)
    ).astype(bf16)
    for tile in range(qkv_half, 2 * qkv_half):
        projection_grad(tile)
    chip_begin(QKV, 1)
    for_pair(chip_end, 4)
    for_pair(line_begin, 1)
    for_pair(plane_end, 2)
    for_pair(line_end, 0)
    v.branch[...] = dot_nt(v.proj[...], whole[QKV][...])
    for_pair(plane_end, 3)

    def first_norm_back(here_rows, start):
        x = v.tokens[here_rows, :].astype(f32)
        flow = norm_back(x, inverse_root(x), v.branch[here_rows, :], gain_row(0), 0)
        v.d_tokens[here_rows, :] += flow

    by_rows(first_norm_back)

    def small_copy(step):
        return remote(
            v.small_parts.at[me],
            v.small_parts.at[me],
            v.small_send.at[step],
            v.small_recv.at[step],
            device(me ^ step),
        )

    def reps_copy(step):
        return remote(
            v.small_reps.at[rep],
            v.small_reps.at[rep],
            v.reps_send.at[step],
            v.reps_recv.at[step],
            (lax.rem(rep + step, reps), here),
        )

    spot = lax.broadcasted_iota(jnp.int32, (1, width), 1)
    numbers = jnp.where(spot == 4, column_sum(valid_rows(0, rows)), 0.0)
    for k in range(4):
        summed = jnp.sum(v.squares[k : k + 1, :], axis=1, keepdims=True)
        numbers = numbers + jnp.where(spot == k, summed, 0.0)
    v.d_gains[4:5, :] = numbers
    v.small_parts[me] = v.d_gains[...]
    for step in range(1, GROUP):
        small_copy(step).start()
    for_pair(line_end, 1)
    for_pair(total_end, 0)
    for_pair(pair_end, 4)
    for_pair(line_begin, 2)
    for_pair(line_begin, 3)
    for_pair(total_end, 1)
    for step in range(1, GROUP):
        small_copy(step).wait_recv()
    v.small_reps[rep] = jnp.sum(v.small_parts[...], axis=0)
    for step in range(1, reps):
        reps_copy(step).start()
    for_pair(line_end, 2)
    for_pair(plane_end, 4)
    for_pair(line_end, 3)
    for_pair(total_end, 2)
    for_pair(line_begin, 4)
    for_pair(total_end, 3)
    for_pair(line_end, 4)
    for_pair(total_end, 4)
    for step in range(1, reps):
        reps_copy(step).wait_recv()
    v.small[...] = jnp.sum(v.small_reps[...], axis=0)
    results = [
        pltpu.make_async_copy(total[number], result[number], v.result_sem.at[number])
        for number in range(5)
    ]
    for copy in results:
        copy.start()

    for number in range(5):
        for kind in range(11):
            weight_copy(number, kind).wait_send()
    for number in range(2):
        key_copy(number).wait_send()
    swap.wait_send()
    for step in range(1, GROUP):
        gain_copy(step).wait_send()
        small_copy(step).wait_send()
    for step in range(1, reps):
        reps_copy(step).wait_send()
    for number, half in order:
        chip_copy(number, half).wait_send()
        pair_copy(number, half).wait_send()
        plane_copy(number, half).wait_send()
        line_copy(number, half, 0).wait_send()

        @pl.when(jnp.logical_not(at_end))
        def _():
            total_copy(number, half).wait_send()

    for copy in results:
        copy.wait()


def layer(prefix, tokens, cotangent, frequency, gain_block, weights, reps):
    shapes = tuple(w.shape for w in weights)
    rows, width = tokens.shape
    spaces = layer_names(rows, 2 * rows, width, shapes, reps)
    halves = [split_shape(number, shape) for number, shape in enumerate(shapes)]
    inputs = ["prefix", "tokens", "cotangent", "frequency", "gain_block"]
    inputs += ["w_qkv", "w_out", "w_gate", "w_up", "w_down"]
    outputs = ["output", "d_tokens", "small"] + [f"grad{number}" for number in range(5)]
    vmem = pl.BlockSpec(memory_space=pltpu.VMEM)
    names = inputs + outputs + list(spaces)
    out = pl.pallas_call(
        lambda *refs: layer_kernel(names, shapes, *refs),
        out_shape=[
            jax.ShapeDtypeStruct((rows, width), f32),
            jax.ShapeDtypeStruct((rows, width), f32),
            jax.ShapeDtypeStruct((8, width), f32),
        ]
        + [jax.ShapeDtypeStruct((2,) + half, bf16) for half in halves],
        in_specs=[pl.BlockSpec(memory_space=pltpu.SMEM)]
        + [vmem] * 4
        + [pl.BlockSpec(memory_space=pl.ANY)] * 5,
        out_specs=[vmem] * 3 + [pl.BlockSpec(memory_space=pl.ANY)] * 5,
        scratch_shapes=list(spaces.values()),
        compiler_params=pltpu.CompilerParams(
            collective_id=2, has_side_effects=True, vmem_limit_bytes=64 * 2**20
        ),
        name="layer",
    )(prefix, tokens, cotangent, frequency, gain_block, *weights)
    return out[0], out[1], out[2], out[3:]


OWNERS = (6, 7, 0, 2, 4)
FLIPPED = (False, True, False, False, True)


def gram_into(x_ref, gram):
    rows = gram.shape[0]
    starts = list(range(0, rows, 256))
    for j in starts:
        n = min(256, rows - j)
        gram[j:rows, j : j + n] = dot_nt(x_ref[j:rows, :], x_ref[j : j + n, :])
    for j in starts:
        n = min(256, rows - j)
        if j + n < rows:
            gram[j : j + n, j + n : rows] = gram[j + n : rows, j : j + n].T


def newton_step(x_ref, gram, mixer, high, low, first, refined):
    gram_into(x_ref, gram)
    rows = gram.shape[0]
    same = lax.broadcasted_iota(jnp.int32, (rows, rows), 0) == lax.broadcasted_iota(
        jnp.int32, (rows, rows), 1
    )
    whole = gram[...]
    scale = None
    if first:
        scale = 1.0 / (jnp.sqrt(jnp.sum(jnp.where(same, whole, 0.0))) + frobenius_epsilon)
        whole = whole * (scale * scale)
        gram[...] = whole
    high[...] = whole.astype(bf16)
    squared = dot(high[...], high[...])
    if refined:
        low[...] = (gram[...] - high[...].astype(f32)).astype(bf16)
        squared = squared + dot(high[...], low[...]) + dot(low[...], high[...])
    mix = (
        jnp.where(same, newton_first, 0.0) + newton_second * gram[...] + newton_third * squared
    )
    if first:
        mix = mix * scale
    mixer[...] = mix.astype(bf16)
    width = x_ref.shape[1]
    tile = 1024 if width % 1024 == 0 else width

    @pl.loop(0, width // tile)
    def _(t):
        cols = pl.ds(pl.multiple_of(t * tile, tile), tile)
        x_ref[:, cols] = dot(mixer[...], x_ref[:, cols]).astype(bf16)


def muon_kernel(shapes, *refs):
    sources, results = refs[0:10], refs[10:15]
    outgoing, arrived = refs[15:20], refs[20:25]
    x_all, gram, mixer, high, low = refs[25:30]
    gather_send, gather_recv, scatter_send, scatter_recv, load_sem = refs[30:35]
    loaded = refs[35:45]
    grads, moments = loaded[0:5], loaded[5:10]
    loads = [
        pltpu.make_async_copy(source, target, load_sem.at[k])
        for k, (source, target) in enumerate(zip(sources, loaded))
    ]
    for load in loads:
        load.start()
    rep, me, lane, lanes = place()

    def device(member):
        return (rep, member * lanes + lane)

    owner_here = me == OWNERS[0]
    for owner in OWNERS[1:]:
        owner_here = owner_here | (me == owner)

    @pl.when(owner_here)
    def _():
        x_all[...] = jnp.zeros_like(x_all)

    barrier = pltpu.get_barrier_semaphore()
    for step in range(1, GROUP):
        pl.semaphore_signal(
            barrier, inc=1, device_id=device(me ^ step), device_id_type=MESH
        )

    def block(number, member):
        rows, cols = shapes[number]
        if FLIPPED[number]:
            return x_all.at[:, pl.ds(member * rows, rows)]
        return x_all.at[pl.ds(member * rows, rows), pl.ds(0, cols)]

    for number in (2, 3, 4, 0, 1):
        loads[number].wait()
        loads[5 + number].wait()
        grad = jnp.concatenate(
            [grads[number][0], grads[number][1]], axis=0 if number in (OUT, DOWN) else 1
        ).astype(f32)
        new = momentum_decay * moments[number][...] + (1.0 - momentum_decay) * grad
        nesterov = (1.0 - momentum_decay) * grad + momentum_decay * new
        if FLIPPED[number]:
            nesterov = nesterov.T
        outgoing[number][...] = nesterov.astype(bf16)
    pl.semaphore_wait(barrier, GROUP - 1)

    def gather_copy(number, member, sender):
        rows, _ = shapes[number]
        if FLIPPED[number]:
            start = pl.multiple_of(sender * rows, rows)
            target = x_all.at[:, pl.ds(start, rows)]
        else:
            start = pl.multiple_of(sender * rows, 16)
            target = x_all.at[pl.ds(start, rows), pl.ds(0, shapes[number][1])]
        return pltpu.make_async_remote_copy(
            src_ref=outgoing[number],
            dst_ref=target,
            send_sem=gather_send.at[number],
            recv_sem=gather_recv.at[sender],
            device_id=device(member),
            device_id_type=MESH,
        )

    for number in (2, 3, 4, 0, 1):

        @pl.when(me != OWNERS[number])
        def _():
            gather_copy(number, OWNERS[number], me).start()

    for number in range(5):
        owner = OWNERS[number]

        @pl.when(me == owner)
        def _():
            rows, cols = shapes[number]
            if FLIPPED[number]:
                x_all[:, owner * rows : (owner + 1) * rows] = outgoing[number][...]
            else:
                x_all[owner * rows : (owner + 1) * rows, 0:cols] = outgoing[number][...]
            for step in range(1, GROUP):
                gather_copy(number, owner, owner ^ step).wait_recv()

    @pl.when(owner_here)
    def _():
        newton_step(x_all, gram, mixer, high, low, True, False)

        @pl.loop(0, NS_STEPS - 3)
        def _(k):
            newton_step(x_all, gram, mixer, high, low, False, False)

        @pl.loop(0, 2)
        def _(k):
            newton_step(x_all, gram, mixer, high, low, False, True)

    def scatter_copy(number, member):
        rows, cols = shapes[number]
        return pltpu.make_async_remote_copy(
            src_ref=block(number, member),
            dst_ref=arrived[number],
            send_sem=scatter_send.at[member],
            recv_sem=scatter_recv.at[number],
            device_id=device(member),
            device_id_type=MESH,
        )

    for number in range(5):
        owner = OWNERS[number]

        @pl.when(me == owner)
        def _():
            for step in range(1, GROUP):
                scatter_copy(number, owner ^ step).start()
            arrived[number][...] = block(number, owner)[...]

    for number in range(5):
        owner = OWNERS[number]

        @pl.when(me != owner)
        def _():
            scatter_copy(number, owner).wait_recv()

        update = arrived[number][...]
        if FLIPPED[number]:
            update = update.astype(f32).T.astype(bf16)
        results[number][...] = update

    for number in range(5):
        owner = OWNERS[number]

        @pl.when(me == owner)
        def _():
            for step in range(1, GROUP):
                scatter_copy(number, owner ^ step).wait_send()

        @pl.when(me != owner)
        def _():
            gather_copy(number, owner, me).wait_send()


def muon(grads, moments):
    shapes = tuple(moment.shape for moment in moments)
    flipped = [s[::-1] if flip else s for s, flip in zip(shapes, FLIPPED)]
    side = shapes[0][0] * GROUP
    width = max(s[0] * GROUP if flip else s[1] for s, flip in zip(shapes, FLIPPED))
    vmem = pl.BlockSpec(memory_space=pltpu.VMEM)
    return pl.pallas_call(
        lambda *refs: muon_kernel(shapes, *refs),
        out_shape=[jax.ShapeDtypeStruct(s, bf16) for s in shapes],
        in_specs=[pl.BlockSpec(memory_space=pl.ANY)] * 10,
        out_specs=[vmem] * 5,
        scratch_shapes=[pltpu.VMEM(s, bf16) for s in flipped]
        + [pltpu.VMEM(s, bf16) for s in flipped]
        + [
            pltpu.VMEM((side, width), bf16),
            pltpu.VMEM((side, side), f32),
            pltpu.VMEM((side, side), bf16),
            pltpu.VMEM((side, side), bf16),
            pltpu.VMEM((side, side), bf16),
            pltpu.SemaphoreType.DMA((5,)),
            pltpu.SemaphoreType.DMA((GROUP,)),
            pltpu.SemaphoreType.DMA((GROUP,)),
            pltpu.SemaphoreType.DMA((5,)),
            pltpu.SemaphoreType.DMA((10,)),
        ]
        + [pltpu.VMEM(term.shape, term.dtype) for term in (*grads, *moments)],
        compiler_params=pltpu.CompilerParams(
            collective_id=1, has_side_effects=True, vmem_limit_bytes=63 * 2**20
        ),
        name="muon",
    )(*grads, *moments)


def finish_kernel(factors, *refs):
    grads, updates, moments, weights = refs[0:5], refs[5:10], refs[10:15], refs[15:20]
    streams, (small, gains, first, second) = refs[20:22], refs[22:26]
    wide, news, masters = refs[26:31], refs[31:36], refs[36:41]
    stream_out = refs[41:43]
    gain_grad, first_new, second_new, master_gains, statistics = refs[43:48]
    here = lax.axis_index("fsdp")
    for number in range(5):
        grad = grads[number][0].astype(f32)
        wide[number][...] = grad
        news[number][...] = (
            momentum_decay * moments[number][...] + (1.0 - momentum_decay) * grad
        )
        masters[number][...] = weights[number][...].astype(f32) - factors[number] * updates[
            number
        ][...].astype(f32)
    for source, target in zip(streams, stream_out):
        target[...] = source[...]

    @pl.when(pl.program_id(0) == 0)
    def _():
        kinds, count = gains.shape
        width = small.shape[1]
        shift = lax.rem(width - here * count, width)
        grad = pltpu.roll(small[...], shift, 1)[0:kinds, 0:count]
        gain_grad[...] = grad
        gains_local = gains[...].astype(f32)
        first_next = first_decay * first[...] + (1.0 - first_decay) * grad
        second_next = second_decay * second[...] + (1.0 - second_decay) * grad * grad
        first_new[...] = first_next
        second_new[...] = second_next
        first_hat = first_next / (1.0 - first_decay**ADAM_STEP)
        second_hat = second_next / (1.0 - second_decay**ADAM_STEP)
        master_gains[...] = gains_local - adam_rate * (
            first_hat / (jnp.sqrt(second_hat) + adam_epsilon) + weight_decay * gains_local
        )
        statistics[...] = jnp.sqrt(small[4:5, 0:4] / (small[4:5, 4:5] * width))


def finish(grads, updates, moments, weights, streams, small, gains, first, second):
    steps = 4
    shapes = tuple(moment.shape for moment in moments)
    factors = [max(1.0, s[0] * GROUP / s[1]) ** 0.5 * muon_rate for s in shapes]
    halves, wholes = [], []
    for number, (rows, cols) in enumerate(shapes):
        if number in (OUT, DOWN):
            halves.append(pl.BlockSpec((1, rows // steps, cols), lambda j: (j // 2, j % 2, 0)))
            wholes.append(pl.BlockSpec((rows // steps, cols), lambda j: (j, 0)))
        else:
            halves.append(pl.BlockSpec((1, rows, cols // steps), lambda j: (j // 2, 0, j % 2)))
            wholes.append(pl.BlockSpec((rows, cols // steps), lambda j: (0, j)))
    lines = [
        pl.BlockSpec((s.shape[0] // steps, s.shape[1]), lambda j: (j, 0)) for s in streams
    ]
    single = lambda shape: pl.BlockSpec(shape, lambda j: (0, 0))
    table = single(gains.shape)
    out = pl.pallas_call(
        lambda *refs: finish_kernel(factors, *refs),
        grid=(steps,),
        out_shape=[jax.ShapeDtypeStruct(s, f32) for s in shapes * 3]
        + [jax.ShapeDtypeStruct(s.shape, f32) for s in streams]
        + [jax.ShapeDtypeStruct(gains.shape, f32)] * 4
        + [jax.ShapeDtypeStruct((1, 4), f32)],
        in_specs=halves + wholes * 3 + lines + [single(small.shape)] + [table] * 3,
        out_specs=wholes * 3 + lines + [table] * 4 + [single((1, 4))],
        compiler_params=pltpu.CompilerParams(vmem_limit_bytes=63 * 2**20),
        name="finish",
    )(*grads, *updates, *moments, *weights, *streams, small, gains, first, second)
    return out[0:5], out[5:10], out[10:15], out[15:17], out[17:21], out[21]


def shards(
    tokens,
    cotangent,
    prefix,
    w_qkv,
    w_out,
    w_gate,
    w_up,
    w_down,
    gains,
    moment_qkv,
    moment_out,
    moment_gate,
    moment_up,
    moment_down,
    gain_first,
    gain_second,
):
    reps = lax.axis_size("rep")
    _, _, lane, lanes = place()
    teams = [[member * lanes + k for k in range(lanes)] for member in range(GROUP)]

    def joined(shard):
        if lanes == 1:
            return shard
        return lax.all_gather(shard, "fsdp", axis=0, tiled=True, axis_index_groups=teams)

    def summed(term):
        if lanes == 1:
            return term
        parts = lax.all_gather(term, "fsdp", axis_index_groups=teams)
        return jnp.sum(parts.astype(f32), axis=0).astype(term.dtype)

    def parted(block):
        if lanes == 1:
            return block
        size = block.shape[0] // lanes
        return lax.dynamic_slice_in_dim(block, lane * size, size, 0)

    half_dim = jnp.arange(HEAD_DIM // 2, dtype=f32)
    frequency = (rotary_base ** (-(half_dim * 2.0 / HEAD_DIM)))[None, :]
    weights = [joined(term) for term in (w_qkv, w_out, w_gate, w_up, w_down)]
    moments = [
        joined(term)
        for term in (moment_qkv, moment_out, moment_gate, moment_up, moment_down)
    ]
    output, d_tokens, small, halves = layer(
        prefix, tokens, cotangent, frequency, joined(gains).T, weights, reps
    )
    halves = [summed(term) for term in halves]
    small = summed(small)
    updates = muon(halves, moments)
    grads, news, masters, streams, gain_terms, statistics = finish(
        halves,
        updates,
        moments,
        weights,
        (output, d_tokens),
        small,
        gains.T,
        gain_first.T,
        gain_second.T,
    )
    gain_terms = [term.T for term in gain_terms]
    grads, news, masters = (
        [parted(term) for term in group] for group in (grads, news, masters)
    )
    return (
        *streams,
        *grads,
        gain_terms[0],
        *news,
        *masters,
        *gain_terms[1:],
        statistics.reshape(4),
    )


def solution(mesh):
    in_specs = (
        P(("rep", "fsdp"), None),
        P(("rep", "fsdp"), None),
        P(),
        P("fsdp", None),
        P("fsdp", None),
        P("fsdp", None),
        P("fsdp", None),
        P("fsdp", None),
        P("fsdp", None),
        P("fsdp", None),
        P("fsdp", None),
        P("fsdp", None),
        P("fsdp", None),
        P("fsdp", None),
        P("fsdp", None),
        P("fsdp", None),
    )
    out_specs = (
        P(("rep", "fsdp"), None),
        P(("rep", "fsdp"), None),
        P("fsdp", None),
        P("fsdp", None),
        P("fsdp", None),
        P("fsdp", None),
        P("fsdp", None),
        P("fsdp", None),
        P("fsdp", None),
        P("fsdp", None),
        P("fsdp", None),
        P("fsdp", None),
        P("fsdp", None),
        P("fsdp", None),
        P("fsdp", None),
        P("fsdp", None),
        P("fsdp", None),
        P("fsdp", None),
        P("fsdp", None),
        P("fsdp", None),
        P("fsdp", None),
        P(),
    )
    return jax.shard_map(shards, mesh=mesh, in_specs=in_specs, out_specs=out_specs, check_vma=False)
```

```python
import jax
import jax.numpy as jnp
from jax import lax
from jax.experimental import pallas as pl
from jax.experimental.pallas import tpu as pltpu
from jax.sharding import PartitionSpec as P

HEADS = 4
HEAD_DIM = 256
NS_STEPS = 5
ADAM_STEP = 10


norm_epsilon = 1e-06
soft_cap = 50.0
rotary_base = 10000.0
newton_first = 3.4445
newton_second = -4.775
newton_third = 2.0315
momentum_decay = 0.95
muon_rate = 1.0
first_decay = 0.9
second_decay = 0.95
adam_rate = 1.0
weight_decay = 0.1
adam_epsilon = 1e-08
frobenius_epsilon = 1e-07

GROUP = 8
MESH = pl.DeviceIdType.MESH
f32 = jnp.float32
bf16 = jnp.bfloat16


def dot(a, b):
    return lax.dot_general(a, b, (((1,), (0,)), ((), ())), preferred_element_type=f32)


def dot_nt(a, b):
    return lax.dot_general(a, b, (((1,), (1,)), ((), ())), preferred_element_type=f32)


def dot_tn(a, b):
    return lax.dot_general(a, b, (((0,), (0,)), ((), ())), preferred_element_type=f32)


def place():
    size = lax.axis_size("fsdp")
    lanes = size // GROUP
    here = lax.axis_index("fsdp")
    return lax.axis_index("rep"), here // lanes, lax.rem(here, lanes), lanes


QKV, OUT, GATE, UP, DOWN = range(5)
CORE, ACROSS, ALONG = 1, 2, 4
PAIRS = (
    ((GATE, 0), (UP, 0)),
    ((DOWN, 0), (GATE, 1)),
    ((UP, 1), (DOWN, 1)),
    ((OUT, 0), (OUT, 1)),
    ((QKV, 0), (QKV, 1)),
)
CHUNK = 128
TILE = 256


def split_shape(number, shape):
    rows, cols = shape
    return (rows // 2, cols) if number in (OUT, DOWN) else (rows, cols // 2)


def layer_names(rows, keys, width, shapes, reps):
    halves = [split_shape(number, shape) for number, shape in enumerate(shapes)]
    feats = HEADS * HEAD_DIM
    inner = shapes[GATE][1]
    spaces = {}
    for number, (height, cols) in enumerate(shapes):
        spaces[f"whole{number}"] = pltpu.VMEM((height * GROUP, cols), bf16)
    spaces.update(
        cosine=pltpu.VMEM((rows, HEAD_DIM // 2), f32),
        sine=pltpu.VMEM((rows, HEAD_DIM // 2), f32),
        gain_parts=pltpu.VMEM((GROUP, 8, 128), f32),
        gains=pltpu.VMEM((8, width), f32),
        normed=pltpu.VMEM((rows, width), bf16),
        one_t=pltpu.VMEM((width, rows), bf16),
        two_t=pltpu.VMEM((width, rows), bf16),
        proj=pltpu.VMEM((rows, feats + 2 * HEAD_DIM), bf16),
        key=pltpu.VMEM((keys, HEAD_DIM), bf16),
        value=pltpu.VMEM((keys, HEAD_DIM), bf16),
        key_t=pltpu.VMEM((HEAD_DIM, keys), bf16),
        value_t=pltpu.VMEM((HEAD_DIM, keys), bf16),
        att=pltpu.VMEM((rows, feats), bf16),
        att_t=pltpu.VMEM((feats, rows), bf16),
        inverse=pltpu.VMEM((8, rows), f32),
        branch=pltpu.VMEM((rows, width), f32),
        hidden=pltpu.VMEM((rows, width), f32),
        slope=pltpu.VMEM((rows, inner), bf16),
        bend=pltpu.VMEM((rows, inner), bf16),
        active=pltpu.VMEM((rows, inner), bf16),
        d_key=pltpu.VMEM((keys, HEAD_DIM), f32),
        d_value=pltpu.VMEM((keys, HEAD_DIM), f32),
        swap_in=pltpu.VMEM((rows, 2 * HEAD_DIM), bf16),
        squares=pltpu.VMEM((8, width), f32),
        d_gains=pltpu.VMEM((8, width), f32),
        small_parts=pltpu.VMEM((GROUP, 8, width), f32),
        small_reps=pltpu.VMEM((reps, 8, width), f32),
    )
    for number, half in enumerate(halves):
        spaces[f"stage{number}"] = pltpu.VMEM((2, 2, 2, 2) + half, bf16)
        spaces[f"chip{number}"] = pltpu.VMEM((2, 2, 2) + half, bf16)
        spaces[f"pair{number}"] = pltpu.VMEM((2, 2) + half, bf16)
        spaces[f"plane{number}"] = pltpu.VMEM((2,) + half, bf16)
        spaces[f"line{number}"] = pltpu.VMEM((2, 2) + half, bf16)
        spaces[f"total{number}"] = pltpu.VMEM((2,) + half, bf16)
    dma = pltpu.SemaphoreType.DMA
    spaces.update(
        own_sem=dma((5,)),
        result_sem=dma((5,)),
        weight_send=dma((5, 11)),
        weight_recv=dma((5, 11)),
        gain_send=dma((GROUP,)),
        gain_recv=dma((GROUP,)),
        key_send=dma((2,)),
        key_recv=dma((2,)),
        swap_send=dma((1,)),
        swap_recv=dma((1,)),
        chip_send=dma((5, 2)),
        chip_recv=dma((5, 2)),
        pair_send=dma((5, 2)),
        pair_recv=dma((5, 2)),
        plane_send=dma((5, 2)),
        plane_recv=dma((5, 2)),
        line_send=dma((5, 2)),
        line_recv=dma((5, 2, 2)),
        total_send=dma((5, 2)),
        total_recv=dma((5, 2)),
        small_send=dma((GROUP,)),
        small_recv=dma((GROUP,)),
        reps_send=dma((reps,)),
        reps_recv=dma((reps,)),
    )
    return spaces


class Refs:
    def __init__(self, names, refs):
        self.__dict__.update(zip(names, refs))


def column_sum(x):
    return jnp.sum(x, axis=0, keepdims=True)


def row_mean(x):
    return jnp.mean(x, axis=-1, keepdims=True)


def layer_kernel(names, shapes, *refs):
    v = Refs(names, refs)
    rep, me, lane, lanes = place()
    reps = lax.axis_size("rep")
    here = lax.axis_index("fsdp")
    core, across, along = me % 2, (me // 2) % 2, me // 4
    rows, width = v.tokens.shape
    parity = here % 2
    weights = [v.w_qkv, v.w_out, v.w_gate, v.w_up, v.w_down]
    named = lambda name: [getattr(v, f"{name}{number}") for number in range(5)]
    whole, stage, chip, pair = named("whole"), named("stage"), named("chip"), named("pair")
    plane, line, total, result = named("plane"), named("line"), named("total"), named("grad")

    def device(member):
        return (rep, member * lanes + lane)

    def remote(src, dst, send, recv, where):
        return pltpu.make_async_remote_copy(
            src_ref=src,
            dst_ref=dst,
            send_sem=send,
            recv_sem=recv,
            device_id=where,
            device_id_type=MESH,
        )

    barrier = pltpu.get_barrier_semaphore()
    greeted = [device(me ^ step) for step in range(1, GROUP)]
    greeted += [(lax.rem(rep + step, reps), here) for step in range(1, reps)]
    if lanes > 1:
        greeted.append((rep, here ^ 1))
    for where in greeted:
        pl.semaphore_signal(barrier, inc=1, device_id=where, device_id_type=MESH)
    pl.semaphore_wait(barrier, len(greeted))

    odd = rep % 2

    def parts(number):
        rows_or_cols, tile = shapes[number][1], 128
        if number in (OUT, DOWN):
            rows_or_cols, tile = shapes[number][0], 16
        outer = (rows_or_cols // tile + 1) // 3 * tile
        return outer, rows_or_cols - 2 * outer, tile

    def window(number, member, start, size, tile):
        height = shapes[number][0]
        base = pl.multiple_of(member * height, 16)
        if number in (OUT, DOWN):
            return whole[number].at[pl.ds(pl.multiple_of(base + start, 16), size), :]
        return whole[number].at[pl.ds(base, height), pl.ds(pl.multiple_of(start, 128), size)]

    def slot(number, member):
        height = shapes[number][0]
        return whole[number].at[pl.ds(pl.multiple_of(member * height, 16), height), :]

    def outer_part(number, member):
        outer, middle, tile = parts(number)
        return window(number, member, odd * (outer + middle), outer, tile)

    def middle_part(number, member):
        outer, middle, tile = parts(number)
        return window(number, member, outer, middle, tile)

    def own_parts(number):
        outer, middle, tile = parts(number)
        start = pl.multiple_of(odd * outer, tile)
        if number in (OUT, DOWN):
            return weights[number].at[pl.ds(start, outer + middle), :]
        return weights[number].at[:, pl.ds(start, outer + middle)]

    def both_parts(number, member):
        outer, middle, tile = parts(number)
        return window(number, member, odd * outer, outer + middle, tile)

    def weight_copy(number, kind):
        beside, ahead = me ^ ACROSS, me ^ ALONG
        corner = beside ^ ALONG
        if kind == 0:
            src, dst, where = weights[number], slot(number, me), device(me ^ CORE)
        elif kind < 3:
            src, dst = own_parts(number), both_parts(number, me)
            where = device((beside, ahead)[kind - 1])
        elif kind < 5:
            src = outer_part(number, beside) if kind == 3 else middle_part(number, ahead)
            dst, where = src, device((ahead, beside)[kind - 3])
        elif kind < 8:
            src = outer_part(number, (beside, ahead, corner)[kind - 5])
            dst, where = src, (rep + 1 - 2 * odd, here)
        else:
            src = slot(number, (beside, ahead, corner)[kind - 8])
            dst, where = src, device(me ^ CORE)
        return remote(
            src, dst, v.weight_send.at[number, kind], v.weight_recv.at[number, kind], where
        )

    def own_copy(number):
        return pltpu.make_async_copy(weights[number], slot(number, me), v.own_sem.at[number])

    def weight_begin(number):
        for kind in (1, 2, 0):
            weight_copy(number, kind).start()
        own_copy(number).start()

    def weight_forward(number):
        weight_copy(number, 1).wait_recv()
        weight_copy(number, 3).start()
        weight_copy(number, 5).start()
        weight_copy(number, 2).wait_recv()
        weight_copy(number, 4).start()
        weight_copy(number, 6).start()

    def weight_corner(number):
        weight_copy(number, 3).wait_recv()
        weight_copy(number, 7).start()

    def weight_cross(number):
        weight_copy(number, 5).wait_recv()
        weight_copy(number, 8).start()
        weight_copy(number, 6).wait_recv()
        weight_copy(number, 9).start()
        weight_copy(number, 4).wait_recv()
        weight_copy(number, 7).wait_recv()
        weight_copy(number, 10).start()

    def weight_ready(number):
        own_copy(number).wait()
        for kind in (0, 8, 9, 10):
            weight_copy(number, kind).wait_recv()

    weight_begin(QKV)

    def gain_copy(step):
        return remote(
            v.gain_parts.at[me],
            v.gain_parts.at[me],
            v.gain_send.at[step],
            v.gain_recv.at[step],
            device(me ^ step),
        )

    gain_count, gain_rows = v.gain_block.shape
    v.gain_parts[me] = jnp.zeros_like(v.gain_parts[me])
    v.gain_parts[me, 0:gain_count, 0:gain_rows] = v.gain_block[...].astype(f32)
    for step in range(1, GROUP):
        gain_copy(step).start()
    weight_begin(OUT)
    weight_begin(GATE)
    v.squares[...] = jnp.zeros_like(v.squares)
    v.d_gains[...] = jnp.zeros_like(v.d_gains)
    v.d_key[...] = jnp.zeros_like(v.d_key)
    v.d_value[...] = jnp.zeros_like(v.d_value)
    spot = lax.broadcasted_iota(jnp.int32, (rows, HEAD_DIM // 2), 0) + parity * rows
    angles = spot.astype(f32) * v.frequency[...]
    v.cosine[...] = jnp.cos(angles)
    v.sine[...] = jnp.sin(angles)
    for step in range(1, GROUP):
        gain_copy(step).wait_recv()
    for member in range(GROUP):
        v.gains[:, member * gain_rows : (member + 1) * gain_rows] = v.gain_parts[
            member, :, 0:gain_rows
        ]

    prefix = v.prefix[(rep * lax.axis_size("fsdp") + here) // 2]

    def valid_rows(start, count):
        spot = lax.broadcasted_iota(jnp.int32, (count, 1), 0) + (parity * rows + start)
        return jnp.where(spot >= prefix, 1.0, 0.0)

    def by_rows(body):
        @pl.loop(0, rows // CHUNK)
        def _(k):
            start = pl.multiple_of(k * CHUNK, CHUNK)
            body(pl.ds(start, CHUNK), start)

    def by_columns(count, body):
        @pl.loop(0, count // TILE)
        def _(k):
            body(pl.ds(pl.multiple_of(k * TILE, TILE), TILE), k)

    def inverse_root(x):
        return lax.rsqrt(row_mean(x * x) + norm_epsilon)

    def norm_back(x, scale, upstream, gain, row):
        v.d_gains[row : row + 1, :] += column_sum(upstream * x * scale)
        spread = upstream * gain
        return scale * spread - x * (scale * scale * scale * row_mean(x * spread))

    gain_row = lambda k: v.gains[k : k + 1, :]

    def first_norm(here_rows, start):
        x = v.tokens[here_rows, :].astype(f32)
        normed = x * inverse_root(x) * gain_row(0)
        v.normed[here_rows, :] = normed.astype(bf16)
        v.one_t[:, here_rows] = normed.T.astype(bf16)
        v.squares[0:1, :] += column_sum(valid_rows(start, CHUNK) * (x * x))

    by_rows(first_norm)
    weight_forward(QKV)
    weight_corner(QKV)
    weight_forward(OUT)
    weight_begin(UP)
    weight_cross(QKV)
    weight_corner(OUT)
    weight_ready(QKV)

    feats = HEADS * HEAD_DIM
    half_dim = HEAD_DIM // 2
    own_rows = pl.ds(pl.multiple_of(parity * rows, rows), rows)
    other_rows = pl.ds(pl.multiple_of((1 - parity) * rows, rows), rows)

    def rotate(x, sign):
        first, second = x[:, :half_dim], x[:, half_dim:]
        cosine, sine = v.cosine[...], v.sine[...] * sign
        return first * cosine - second * sine, second * cosine + first * sine

    def key_copy(number):
        ref = (v.key, v.value)[number]
        return remote(
            ref.at[own_rows, :],
            ref.at[own_rows, :],
            v.key_send.at[number],
            v.key_recv.at[number],
            (rep, here ^ 1),
        )

    key_part = dot(v.normed[...], whole[QKV][:, feats : feats + HEAD_DIM])
    first, second = rotate(key_part, 1.0)
    v.key[own_rows, :half_dim] = first.astype(bf16)
    v.key[own_rows, half_dim:] = second.astype(bf16)
    key_copy(0).start()
    v.value[own_rows, :] = dot(v.normed[...], whole[QKV][:, feats + HEAD_DIM :]).astype(bf16)
    key_copy(1).start()

    @pl.loop(0, HEADS)
    def _(head):
        start = pl.multiple_of(head * HEAD_DIM, HEAD_DIM)
        part = dot(v.normed[...], whole[QKV][:, pl.ds(start, HEAD_DIM)])
        first, second = rotate(part, 1.0)
        v.proj[:, pl.ds(start, half_dim)] = first.astype(bf16)
        v.proj[:, pl.ds(start + half_dim, half_dim)] = second.astype(bf16)

    weight_forward(GATE)
    weight_begin(DOWN)
    for number in range(2):
        key_copy(number).wait_recv()
    v.key_t[...] = v.key[...].astype(f32).T.astype(bf16)
    v.value_t[...] = v.value[...].astype(f32).T.astype(bf16)

    keys = v.key.shape[0]
    bend_scale = HEAD_DIM ** (-0.5) / soft_cap

    def head_columns(head):
        return pl.ds(pl.multiple_of(head * HEAD_DIM, HEAD_DIM), HEAD_DIM)

    def scores(head, start):
        here_rows = pl.ds(start, TILE)
        query = v.proj[here_rows, head_columns(head)]
        bent = jnp.tanh(dot_nt(v.key[...], query) * bend_scale)
        spot = lax.broadcasted_iota(jnp.int32, (1, TILE), 1) + (parity * rows + start)
        last = jnp.maximum(spot, prefix - 1)
        allowed = lax.broadcasted_iota(jnp.int32, (keys, TILE), 0) <= last
        return bent, jnp.where(allowed, jnp.exp(soft_cap * bent), 0.0), query

    blocks = rows // TILE

    def attend(begin, end):
        @pl.loop(begin, end)
        def _(k):
            head = k // blocks
            start = pl.multiple_of(lax.rem(k, blocks) * TILE, TILE)
            cols, here_rows = head_columns(head), pl.ds(start, TILE)
            _, power, _ = scores(head, start)
            inverse = 1.0 / column_sum(power)
            v.inverse[pl.ds(head, 1), here_rows] = inverse
            mixed = dot(v.value_t[...], (power * inverse).astype(bf16))
            v.att_t[cols, here_rows] = mixed.astype(bf16)
            v.att[here_rows, cols] = mixed.T.astype(bf16)

    weight_cross(OUT)
    weight_corner(GATE)
    attend(0, 2)
    weight_forward(UP)
    attend(2, 4)
    weight_cross(GATE)
    weight_corner(UP)
    attend(4, 6)
    weight_forward(DOWN)
    weight_corner(DOWN)
    attend(6, 8)
    weight_ready(OUT)

    v.branch[...] = dot(v.att[...], whole[OUT][...])

    def second_norm(here_rows, start):
        x = v.branch[here_rows, :]
        first_out = x * inverse_root(x) * gain_row(1)
        hidden = v.tokens[here_rows, :].astype(f32) + first_out
        v.hidden[here_rows, :] = hidden
        normed = hidden * inverse_root(hidden) * gain_row(2)
        v.normed[here_rows, :] = normed.astype(bf16)
        v.two_t[:, here_rows] = normed.T.astype(bf16)
        v.squares[1:2, :] += column_sum(valid_rows(start, CHUNK) * (first_out * first_out))

    by_rows(second_norm)
    weight_cross(UP)
    weight_ready(GATE)
    weight_ready(UP)
    inner = shapes[GATE][1]

    def feed(cols, k):
        gate = dot(v.normed[...], whole[GATE][:, cols])
        upward = dot(v.normed[...], whole[UP][:, cols])
        square = gate * gate
        bent = jnp.tanh(0.7978845608028654 * (gate + 0.044715 * gate * square))
        open_half = 0.5 * (1.0 + bent)
        smooth = gate * open_half
        steep = open_half + gate * (1.0 - bent * bent) * (
            0.3989422804014327 * (1.0 + 3.0 * 0.044715 * square)
        )
        v.active[:, cols] = (smooth * upward).astype(bf16)
        v.bend[:, cols] = smooth.astype(bf16)
        v.slope[:, cols] = (steep * upward).astype(bf16)

    by_columns(inner, feed)
    weight_cross(DOWN)
    weight_ready(DOWN)

    v.d_tokens[...] = dot(v.active[...], whole[DOWN][...])

    def last_norm(here_rows, start):
        x = v.d_tokens[here_rows, :]
        scale = inverse_root(x)
        second_out = x * scale * gain_row(3)
        final = v.hidden[here_rows, :] + second_out
        v.output[here_rows, :] = final
        valid = valid_rows(start, CHUNK)
        v.squares[2:3, :] += column_sum(valid * (second_out * second_out))
        v.squares[3:4, :] += column_sum(valid * (final * final))
        upstream = v.cotangent[here_rows, :].astype(f32)
        v.normed[here_rows, :] = norm_back(x, scale, upstream, gain_row(3), 3).astype(bf16)

    by_rows(last_norm)

    def first_across(number, half):
        return any(one == (number, half) for one, _ in PAIRS)

    def chip_copy(number, half):
        return remote(
            stage[number].at[half, :, :, 1 - core],
            chip[number].at[half],
            v.chip_send.at[number, half],
            v.chip_recv.at[number, half],
            device(me ^ CORE),
        )

    def pair_copy(number, half):
        if first_across(number, half):
            src, where = chip[number].at[half, :, 1 - across], me ^ ACROSS
        else:
            src, where = chip[number].at[half, 1 - along], me ^ ALONG
        return remote(
            src,
            pair[number].at[half],
            v.pair_send.at[number, half],
            v.pair_recv.at[number, half],
            device(where),
        )

    def plane_copy(number, half):
        if first_across(number, half):
            src, where = pair[number].at[half, 1 - along], me ^ ALONG
        else:
            src, where = pair[number].at[half, 1 - across], me ^ ACROSS
        return remote(
            src,
            plane[number].at[half],
            v.plane_send.at[number, half],
            v.plane_recv.at[number, half],
            device(where),
        )

    def added(one, two):
        return one + two

    def chip_begin(number, half):
        chip_copy(number, half).start()

    def chip_end(number, half):
        chip_copy(number, half).wait_recv()

        @pl.loop(0, 4)
        def _(k):
            one, two = k // 2, k % 2
            chip[number][half, one, two] = added(
                chip[number][half, one, two], stage[number][half, one, two, core]
            )

        pair_copy(number, half).start()

    def pair_end(number, half):
        pair_copy(number, half).wait_recv()

        @pl.loop(0, 2)
        def _(k):
            if first_across(number, half):
                mine = chip[number][half, k, across]
            else:
                mine = chip[number][half, along, k]
            pair[number][half, k] = added(pair[number][half, k], mine)

        plane_copy(number, half).start()

    def plane_end(number, half):
        plane_copy(number, half).wait_recv()
        kept = along if first_across(number, half) else across
        plane[number][half] = added(plane[number][half], pair[number][half, kept])

        @pl.when(at_end)
        def _():
            line_send(number, half)

    order = [half for both in PAIRS for half in both]

    on_left = rep < reps // 2
    inward = jnp.where(on_left, 1, -1)
    at_end = (rep == 0) | (rep == reps - 1)
    at_middle = (rep == reps // 2 - 1) | (rep == reps // 2)

    def line_copy(number, half, way):
        return remote(
            plane[number].at[half],
            line[number].at[half, way],
            v.line_send.at[number, half],
            v.line_recv.at[number, half, way],
            (rep + inward, here),
        )

    def total_copy(number, half):
        return remote(
            total[number].at[half],
            total[number].at[half],
            v.total_send.at[number, half],
            v.total_recv.at[number, half],
            (rep - inward, here),
        )

    def line_send(number, half):
        @pl.when(jnp.logical_not(at_middle))
        def _():
            line_copy(number, half, 0).start()

        @pl.when(at_middle)
        def _():
            line_copy(number, half, 1).start()

    def line_begin(number, half):
        @pl.when(jnp.logical_not(at_end))
        def _():
            line_copy(number, half, 0).wait_recv()
            plane[number][half] = added(plane[number][half], line[number][half, 0])
            line_send(number, half)

    def line_end(number, half):
        @pl.when(at_middle)
        def _():
            line_copy(number, half, 1).wait_recv()
            total[number][half] = added(plane[number][half], line[number][half, 1])

            @pl.when(jnp.logical_not(at_end))
            def _():
                total_copy(number, half).start()

    def total_end(number, half):
        @pl.when(jnp.logical_not(at_middle))
        def _():
            total_copy(number, half).wait_recv()

            @pl.when(jnp.logical_not(at_end))
            def _():
                total_copy(number, half).start()

    def for_pair(action, index):
        for number, half in PAIRS[index]:
            action(number, half)

    def keep_columns(number, col_half, col, found):
        height = shapes[number][0]
        for member in range(GROUP):
            stage[number][
                col_half, member // 4, (member // 2) % 2, member % 2, :, pl.ds(col, TILE)
            ] = found[member * height : (member + 1) * height].astype(bf16)

    down_rows = shapes[DOWN][0]
    halved = inner // 2 // TILE

    def feed_back(side, begin, end):
        @pl.loop(begin, end)
        def _(k):
            col = pl.multiple_of(k * TILE, TILE)
            start = pl.multiple_of(side * (inner // 2) + k * TILE, TILE)
            cols = pl.ds(start, TILE)
            d_active = dot_nt(v.normed[...], whole[DOWN][cols, :])
            d_gate = (d_active * v.slope[:, cols].astype(f32)).astype(bf16)
            d_upward = (d_active * v.bend[:, cols].astype(f32)).astype(bf16)
            v.slope[:, cols] = d_gate
            v.bend[:, cols] = d_upward
            keep_columns(GATE, side, col, dot(v.two_t[...], d_gate))
            keep_columns(UP, side, col, dot(v.two_t[...], d_upward))
            found = dot_tn(v.active[:, cols], v.normed[...]).astype(bf16)
            per = TILE // down_rows
            for part in range(per):
                member = (side * halved + k) * per + part
                y, x, c = member // 4, (member // 2) % 2, member % 2
                base = part * down_rows
                stage[DOWN][0, y, x, c] = found[base : base + down_rows // 2]
                stage[DOWN][1, y, x, c] = found[base + down_rows // 2 : base + down_rows]

    feed_back(0, 0, halved)
    for_pair(chip_begin, 0)
    feed_back(1, 0, halved // 2)
    for_pair(chip_end, 0)
    feed_back(1, halved // 2, halved)
    for_pair(chip_begin, 1)
    for_pair(chip_begin, 2)
    v.d_tokens[...] = dot_nt(v.slope[...], whole[GATE][...])
    for_pair(chip_end, 1)
    v.d_tokens[...] += dot_nt(v.bend[...], whole[UP][...])
    for_pair(chip_end, 2)

    def middle_norms(here_rows, start):
        x = v.hidden[here_rows, :]
        flow = norm_back(x, inverse_root(x), v.d_tokens[here_rows, :], gain_row(2), 2)
        d_hidden = v.cotangent[here_rows, :].astype(f32) + flow
        v.d_tokens[here_rows, :] = d_hidden
        x = v.branch[here_rows, :]
        flow = norm_back(x, inverse_root(x), d_hidden, gain_row(1), 1)
        v.normed[here_rows, :] = flow.astype(bf16)

    by_rows(middle_norms)
    for_pair(pair_end, 0)
    out_rows = shapes[OUT][0]
    v.att[...] = dot_nt(v.normed[...], whole[OUT][...]).astype(bf16)

    @pl.loop(0, GROUP // 2)
    def _(k):
        start = pl.multiple_of(k * 2 * out_rows, 2 * out_rows)
        found = dot(v.att_t[pl.ds(start, 2 * out_rows), :], v.normed[...]).astype(bf16)
        for part in range(4):
            stage[OUT][part % 2, k // 2, k % 2, part // 2] = found[
                part * (out_rows // 2) : (part + 1) * (out_rows // 2)
            ]

    for_pair(chip_begin, 3)
    for_pair(pair_end, 1)
    for_pair(plane_end, 0)

    def attend_back(begin, end):
        @pl.loop(begin, end)
        def _(k):
            head = k // blocks
            start = pl.multiple_of(lax.rem(k, blocks) * TILE, TILE)
            here_rows = pl.ds(start, TILE)
            bent, power, query = scores(head, start)
            soft = power * v.inverse[pl.ds(head, 1), here_rows]
            flow = v.att[here_rows, head_columns(head)]
            d_soft = dot_nt(v.value[...], flow)
            v.d_value[...] += dot(soft.astype(bf16), flow)
            level = column_sum(d_soft * soft)
            d_raw = soft * (d_soft - level) * ((1.0 - bent * bent) * HEAD_DIM ** (-0.5))
            d_raw = d_raw.astype(bf16)
            v.d_key[...] += dot(d_raw, query)
            d_query = dot(v.key_t[...], d_raw).T
            first, second = d_query[:, :half_dim], d_query[:, half_dim:]
            cosine, sine = v.cosine[here_rows, :], v.sine[here_rows, :]
            base = pl.multiple_of(head * HEAD_DIM, HEAD_DIM)
            v.proj[here_rows, pl.ds(base, half_dim)] = (first * cosine + second * sine).astype(
                bf16
            )
            v.proj[here_rows, pl.ds(base + half_dim, half_dim)] = (
                second * cosine - first * sine
            ).astype(bf16)

    swap = remote(
        v.att.at[:, 0 : 2 * HEAD_DIM],
        v.swap_in,
        v.swap_send.at[0],
        v.swap_recv.at[0],
        (rep, here ^ 1),
    )

    attend_back(0 * blocks, 1 * blocks)
    for_pair(chip_end, 3)
    attend_back(1 * blocks, 2 * blocks)
    for_pair(pair_end, 2)
    attend_back(2 * blocks, 3 * blocks)
    for_pair(line_begin, 0)
    for_pair(plane_end, 1)
    attend_back(3 * blocks, 4 * blocks)
    v.att[:, 0:HEAD_DIM] = v.d_key[other_rows, :].astype(bf16)
    v.att[:, HEAD_DIM : 2 * HEAD_DIM] = v.d_value[other_rows, :].astype(bf16)
    swap.start()
    for_pair(pair_end, 3)

    qkv_half = split_shape(QKV, shapes[QKV])[1] // TILE

    def projection_grad(tile):
        found = dot(v.one_t[...], v.proj[:, tile * TILE : (tile + 1) * TILE])
        keep_columns(QKV, tile // qkv_half, (tile % qkv_half) * TILE, found)

    for tile in range(qkv_half):
        projection_grad(tile)
    chip_begin(QKV, 0)
    swap.wait_recv()
    d_key = v.d_key[own_rows, :] + v.swap_in[:, 0:HEAD_DIM].astype(f32)
    first, second = rotate(d_key, -1.0)
    v.proj[:, feats : feats + half_dim] = first.astype(bf16)
    v.proj[:, feats + half_dim : feats + HEAD_DIM] = second.astype(bf16)
    v.proj[:, feats + HEAD_DIM :] = (
        v.d_value[own_rows, :] + v.swap_in[:, HEAD_DIM:].astype(f32)
    ).astype(bf16)
    for tile in range(qkv_half, 2 * qkv_half):
        projection_grad(tile)
    chip_begin(QKV, 1)
    for_pair(chip_end, 4)
    for_pair(line_begin, 1)
    for_pair(plane_end, 2)
    for_pair(line_end, 0)
    v.branch[...] = dot_nt(v.proj[...], whole[QKV][...])
    for_pair(plane_end, 3)

    def first_norm_back(here_rows, start):
        x = v.tokens[here_rows, :].astype(f32)
        flow = norm_back(x, inverse_root(x), v.branch[here_rows, :], gain_row(0), 0)
        v.d_tokens[here_rows, :] += flow

    by_rows(first_norm_back)

    def small_copy(step):
        return remote(
            v.small_parts.at[me],
            v.small_parts.at[me],
            v.small_send.at[step],
            v.small_recv.at[step],
            device(me ^ step),
        )

    def reps_copy(step):
        return remote(
            v.small_reps.at[rep],
            v.small_reps.at[rep],
            v.reps_send.at[step],
            v.reps_recv.at[step],
            (lax.rem(rep + step, reps), here),
        )

    spot = lax.broadcasted_iota(jnp.int32, (1, width), 1)
    numbers = jnp.where(spot == 4, column_sum(valid_rows(0, rows)), 0.0)
    for k in range(4):
        summed = jnp.sum(v.squares[k : k + 1, :], axis=1, keepdims=True)
        numbers = numbers + jnp.where(spot == k, summed, 0.0)
    v.d_gains[4:5, :] = numbers
    v.small_parts[me] = v.d_gains[...]
    for step in range(1, GROUP):
        small_copy(step).start()
    for_pair(line_end, 1)
    for_pair(total_end, 0)
    for_pair(pair_end, 4)
    for_pair(line_begin, 2)
    for_pair(line_begin, 3)
    for_pair(total_end, 1)
    for step in range(1, GROUP):
        small_copy(step).wait_recv()
    v.small_reps[rep] = jnp.sum(v.small_parts[...], axis=0)
    for step in range(1, reps):
        reps_copy(step).start()
    for_pair(line_end, 2)
    for_pair(plane_end, 4)
    for_pair(line_end, 3)
    for_pair(total_end, 2)
    for_pair(line_begin, 4)
    for_pair(total_end, 3)
    for_pair(line_end, 4)
    for_pair(total_end, 4)
    for step in range(1, reps):
        reps_copy(step).wait_recv()
    v.small[...] = jnp.sum(v.small_reps[...], axis=0)
    results = [
        pltpu.make_async_copy(total[number], result[number], v.result_sem.at[number])
        for number in range(5)
    ]
    for copy in results:
        copy.start()

    for number in range(5):
        for kind in range(11):
            weight_copy(number, kind).wait_send()
    for number in range(2):
        key_copy(number).wait_send()
    swap.wait_send()
    for step in range(1, GROUP):
        gain_copy(step).wait_send()
        small_copy(step).wait_send()
    for step in range(1, reps):
        reps_copy(step).wait_send()
    for number, half in order:
        chip_copy(number, half).wait_send()
        pair_copy(number, half).wait_send()
        plane_copy(number, half).wait_send()
        line_copy(number, half, 0).wait_send()

        @pl.when(jnp.logical_not(at_end))
        def _():
            total_copy(number, half).wait_send()

    for copy in results:
        copy.wait()


def layer(prefix, tokens, cotangent, frequency, gain_block, weights, reps):
    shapes = tuple(w.shape for w in weights)
    rows, width = tokens.shape
    spaces = layer_names(rows, 2 * rows, width, shapes, reps)
    halves = [split_shape(number, shape) for number, shape in enumerate(shapes)]
    inputs = ["prefix", "tokens", "cotangent", "frequency", "gain_block"]
    inputs += ["w_qkv", "w_out", "w_gate", "w_up", "w_down"]
    outputs = ["output", "d_tokens", "small"] + [f"grad{number}" for number in range(5)]
    vmem = pl.BlockSpec(memory_space=pltpu.VMEM)
    names = inputs + outputs + list(spaces)
    out = pl.pallas_call(
        lambda *refs: layer_kernel(names, shapes, *refs),
        out_shape=[
            jax.ShapeDtypeStruct((rows, width), f32),
            jax.ShapeDtypeStruct((rows, width), f32),
            jax.ShapeDtypeStruct((8, width), f32),
        ]
        + [jax.ShapeDtypeStruct((2,) + half, bf16) for half in halves],
        in_specs=[pl.BlockSpec(memory_space=pltpu.SMEM)]
        + [vmem] * 4
        + [pl.BlockSpec(memory_space=pl.ANY)] * 5,
        out_specs=[vmem] * 3 + [pl.BlockSpec(memory_space=pl.ANY)] * 5,
        scratch_shapes=list(spaces.values()),
        compiler_params=pltpu.CompilerParams(
            collective_id=2, has_side_effects=True, vmem_limit_bytes=64 * 2**20
        ),
        name="layer",
    )(prefix, tokens, cotangent, frequency, gain_block, *weights)
    return out[0], out[1], out[2], out[3:]


OWNERS = (6, 7, 0, 2, 4)
FLIPPED = (False, True, False, False, True)


def gram_into(x_ref, gram):
    rows = gram.shape[0]
    starts = list(range(0, rows, 256))
    for j in starts:
        n = min(256, rows - j)
        gram[j:rows, j : j + n] = dot_nt(x_ref[j:rows, :], x_ref[j : j + n, :])
    for j in starts:
        n = min(256, rows - j)
        if j + n < rows:
            gram[j : j + n, j + n : rows] = gram[j + n : rows, j : j + n].T


def newton_step(x_ref, gram, mixer, high, low, first, refined):
    gram_into(x_ref, gram)
    rows = gram.shape[0]
    same = lax.broadcasted_iota(jnp.int32, (rows, rows), 0) == lax.broadcasted_iota(
        jnp.int32, (rows, rows), 1
    )
    whole = gram[...]
    scale = None
    if first is not None:
        trace = jnp.sum(jnp.where(same, whole, 0.0))
        scale = jnp.where(first, 1.0 / (jnp.sqrt(trace) + frobenius_epsilon), 1.0)
        whole = whole * (scale * scale)
        gram[...] = whole
    high[...] = whole.astype(bf16)
    squared = dot(high[...], high[...])
    if refined:
        low[...] = (gram[...] - high[...].astype(f32)).astype(bf16)
        cross = dot(high[...], low[...])
        squared = squared + cross + dot(low[...], high[...])
    mix = (
        jnp.where(same, newton_first, 0.0) + newton_second * gram[...] + newton_third * squared
    )
    if scale is not None:
        mix = mix * scale
    mixer[...] = mix.astype(bf16)
    x_ref[...] = dot(mixer[...], x_ref[...]).astype(bf16)


def muon_kernel(shapes, *refs):
    sources, results = refs[0:10], refs[10:15]
    outgoing, arrived = refs[15:20], refs[20:25]
    x_all, gram, mixer, high, low = refs[25:30]
    gather_send, gather_recv, scatter_send, scatter_recv, load_sem = refs[30:35]
    loaded = refs[35:45]
    grads, moments = loaded[0:5], loaded[5:10]
    loads = [
        pltpu.make_async_copy(source, target, load_sem.at[k])
        for k, (source, target) in enumerate(zip(sources, loaded))
    ]
    for load in loads:
        load.start()
    rep, me, lane, lanes = place()

    def device(member):
        return (rep, member * lanes + lane)

    owner_here = me == OWNERS[0]
    for owner in OWNERS[1:]:
        owner_here = owner_here | (me == owner)

    @pl.when(owner_here)
    def _():
        x_all[...] = jnp.zeros_like(x_all)

    barrier = pltpu.get_barrier_semaphore()
    for step in range(1, GROUP):
        pl.semaphore_signal(
            barrier, inc=1, device_id=device(me ^ step), device_id_type=MESH
        )

    def block(number, member):
        rows, cols = shapes[number]
        if FLIPPED[number]:
            return x_all.at[:, pl.ds(member * rows, rows)]
        return x_all.at[pl.ds(member * rows, rows), pl.ds(0, cols)]

    def gather_copy(number, member, sender):
        rows, _ = shapes[number]
        if FLIPPED[number]:
            start = pl.multiple_of(sender * rows, rows)
            target = x_all.at[:, pl.ds(start, rows)]
        else:
            start = pl.multiple_of(sender * rows, 16)
            target = x_all.at[pl.ds(start, rows), pl.ds(0, shapes[number][1])]
        return pltpu.make_async_remote_copy(
            src_ref=outgoing[number],
            dst_ref=target,
            send_sem=gather_send.at[number],
            recv_sem=gather_recv.at[sender],
            device_id=device(member),
            device_id_type=MESH,
        )

    pl.semaphore_wait(barrier, GROUP - 1)
    for number in (2, 3, 4, 0, 1):
        loads[number].wait()
        loads[5 + number].wait()
        grad = jnp.concatenate(
            [grads[number][0], grads[number][1]], axis=0 if number in (OUT, DOWN) else 1
        ).astype(f32)
        new = momentum_decay * moments[number][...] + (1.0 - momentum_decay) * grad
        nesterov = (1.0 - momentum_decay) * grad + momentum_decay * new
        if FLIPPED[number]:
            nesterov = nesterov.T
        outgoing[number][...] = nesterov.astype(bf16)

        @pl.when(me != OWNERS[number])
        def _():
            gather_copy(number, OWNERS[number], me).start()

    for number in range(5):
        owner = OWNERS[number]

        @pl.when(me == owner)
        def _():
            rows, cols = shapes[number]
            if FLIPPED[number]:
                x_all[:, owner * rows : (owner + 1) * rows] = outgoing[number][...]
            else:
                x_all[owner * rows : (owner + 1) * rows, 0:cols] = outgoing[number][...]
            for step in range(1, GROUP):
                gather_copy(number, owner, owner ^ step).wait_recv()

    @pl.when(owner_here)
    def _():
        @pl.loop(0, NS_STEPS - 2)
        def _(k):
            newton_step(x_all, gram, mixer, high, low, k == 0, False)

        @pl.loop(0, 2)
        def _(k):
            newton_step(x_all, gram, mixer, high, low, None, True)

    def scatter_copy(number, member):
        rows, cols = shapes[number]
        return pltpu.make_async_remote_copy(
            src_ref=block(number, member),
            dst_ref=arrived[number],
            send_sem=scatter_send.at[member],
            recv_sem=scatter_recv.at[number],
            device_id=device(member),
            device_id_type=MESH,
        )

    for number in range(5):
        owner = OWNERS[number]

        @pl.when(me == owner)
        def _():
            for step in range(1, GROUP):
                scatter_copy(number, owner ^ step).start()
            arrived[number][...] = block(number, owner)[...]

    for number in range(5):
        owner = OWNERS[number]

        @pl.when(me != owner)
        def _():
            scatter_copy(number, owner).wait_recv()

        update = arrived[number][...]
        if FLIPPED[number]:
            update = update.astype(f32).T.astype(bf16)
        results[number][...] = update

    for number in range(5):
        owner = OWNERS[number]

        @pl.when(me == owner)
        def _():
            for step in range(1, GROUP):
                scatter_copy(number, owner ^ step).wait_send()

        @pl.when(me != owner)
        def _():
            gather_copy(number, owner, me).wait_send()


def muon(grads, moments):
    shapes = tuple(moment.shape for moment in moments)
    flipped = [s[::-1] if flip else s for s, flip in zip(shapes, FLIPPED)]
    side = shapes[0][0] * GROUP
    width = max(s[0] * GROUP if flip else s[1] for s, flip in zip(shapes, FLIPPED))
    vmem = pl.BlockSpec(memory_space=pltpu.VMEM)
    return pl.pallas_call(
        lambda *refs: muon_kernel(shapes, *refs),
        out_shape=[jax.ShapeDtypeStruct(s, bf16) for s in shapes],
        in_specs=[pl.BlockSpec(memory_space=pl.ANY)] * 10,
        out_specs=[vmem] * 5,
        scratch_shapes=[pltpu.VMEM(s, bf16) for s in flipped]
        + [pltpu.VMEM(s, bf16) for s in flipped]
        + [
            pltpu.VMEM((side, width), bf16),
            pltpu.VMEM((side, side), f32),
            pltpu.VMEM((side, side), bf16),
            pltpu.VMEM((side, side), bf16),
            pltpu.VMEM((side, side), bf16),
            pltpu.SemaphoreType.DMA((5,)),
            pltpu.SemaphoreType.DMA((GROUP,)),
            pltpu.SemaphoreType.DMA((GROUP,)),
            pltpu.SemaphoreType.DMA((5,)),
            pltpu.SemaphoreType.DMA((10,)),
        ]
        + [pltpu.VMEM(term.shape, term.dtype) for term in (*grads, *moments)],
        compiler_params=pltpu.CompilerParams(
            collective_id=1, has_side_effects=True, vmem_limit_bytes=63 * 2**20
        ),
        name="muon",
    )(*grads, *moments)


def finish_kernel(factors, *refs):
    grads, updates, moments, weights = refs[0:5], refs[5:10], refs[10:15], refs[15:20]
    streams, (small, gains, first, second) = refs[20:22], refs[22:26]
    wide, news, masters = refs[26:31], refs[31:36], refs[36:41]
    stream_out = refs[41:43]
    gain_grad, first_new, second_new, master_gains, statistics = refs[43:48]
    here = lax.axis_index("fsdp")
    for number in range(5):
        grad = grads[number][0].astype(f32)
        wide[number][...] = grad
        news[number][...] = (
            momentum_decay * moments[number][...] + (1.0 - momentum_decay) * grad
        )
        masters[number][...] = weights[number][...].astype(f32) - factors[number] * updates[
            number
        ][...].astype(f32)
    for source, target in zip(streams, stream_out):
        target[...] = source[...]

    @pl.when(pl.program_id(0) == 0)
    def _():
        kinds, count = gains.shape
        width = small.shape[1]
        shift = lax.rem(width - here * count, width)
        grad = pltpu.roll(small[...], shift, 1)[0:kinds, 0:count]
        gain_grad[...] = grad
        gains_local = gains[...].astype(f32)
        first_next = first_decay * first[...] + (1.0 - first_decay) * grad
        second_next = second_decay * second[...] + (1.0 - second_decay) * grad * grad
        first_new[...] = first_next
        second_new[...] = second_next
        first_hat = first_next / (1.0 - first_decay**ADAM_STEP)
        second_hat = second_next / (1.0 - second_decay**ADAM_STEP)
        master_gains[...] = gains_local - adam_rate * (
            first_hat / (jnp.sqrt(second_hat) + adam_epsilon) + weight_decay * gains_local
        )
        statistics[...] = jnp.sqrt(small[4:5, 0:4] / (small[4:5, 4:5] * width))


def finish(grads, updates, moments, weights, streams, small, gains, first, second):
    steps = 2
    per = steps // 2
    shapes = tuple(moment.shape for moment in moments)
    factors = [max(1.0, s[0] * GROUP / s[1]) ** 0.5 * muon_rate for s in shapes]
    halves, wholes = [], []
    for number, (rows, cols) in enumerate(shapes):
        if number in (OUT, DOWN):
            halves.append(
                pl.BlockSpec((1, rows // steps, cols), lambda j: (j // per, j % per, 0))
            )
            wholes.append(pl.BlockSpec((rows // steps, cols), lambda j: (j, 0)))
        else:
            halves.append(
                pl.BlockSpec((1, rows, cols // steps), lambda j: (j // per, 0, j % per))
            )
            wholes.append(pl.BlockSpec((rows, cols // steps), lambda j: (0, j)))
    lines = [
        pl.BlockSpec((s.shape[0] // steps, s.shape[1]), lambda j: (j, 0)) for s in streams
    ]
    single = lambda shape: pl.BlockSpec(shape, lambda j: (0, 0))
    table = single(gains.shape)
    out = pl.pallas_call(
        lambda *refs: finish_kernel(factors, *refs),
        grid=(steps,),
        out_shape=[jax.ShapeDtypeStruct(s, f32) for s in shapes * 3]
        + [jax.ShapeDtypeStruct(s.shape, f32) for s in streams]
        + [jax.ShapeDtypeStruct(gains.shape, f32)] * 4
        + [jax.ShapeDtypeStruct((1, 4), f32)],
        in_specs=halves + wholes * 3 + lines + [single(small.shape)] + [table] * 3,
        out_specs=wholes * 3 + lines + [table] * 4 + [single((1, 4))],
        compiler_params=pltpu.CompilerParams(vmem_limit_bytes=63 * 2**20),
        name="finish",
    )(*grads, *updates, *moments, *weights, *streams, small, gains, first, second)
    return out[0:5], out[5:10], out[10:15], out[15:17], out[17:21], out[21]


def shards(
    tokens,
    cotangent,
    prefix,
    w_qkv,
    w_out,
    w_gate,
    w_up,
    w_down,
    gains,
    moment_qkv,
    moment_out,
    moment_gate,
    moment_up,
    moment_down,
    gain_first,
    gain_second,
):
    reps = lax.axis_size("rep")
    _, _, lane, lanes = place()
    teams = [[member * lanes + k for k in range(lanes)] for member in range(GROUP)]

    def joined(shard):
        if lanes == 1:
            return shard
        return lax.all_gather(shard, "fsdp", axis=0, tiled=True, axis_index_groups=teams)

    def summed(term):
        if lanes == 1:
            return term
        parts = lax.all_gather(term, "fsdp", axis_index_groups=teams)
        return jnp.sum(parts.astype(f32), axis=0).astype(term.dtype)

    def parted(block):
        if lanes == 1:
            return block
        size = block.shape[0] // lanes
        return lax.dynamic_slice_in_dim(block, lane * size, size, 0)

    half_dim = jnp.arange(HEAD_DIM // 2, dtype=f32)
    frequency = (rotary_base ** (-(half_dim * 2.0 / HEAD_DIM)))[None, :]
    weights = [joined(term) for term in (w_qkv, w_out, w_gate, w_up, w_down)]
    moments = [
        joined(term)
        for term in (moment_qkv, moment_out, moment_gate, moment_up, moment_down)
    ]
    output, d_tokens, small, halves = layer(
        prefix, tokens, cotangent, frequency, joined(gains).T, weights, reps
    )
    halves = [summed(term) for term in halves]
    small = summed(small)
    updates = muon(halves, moments)
    grads, news, masters, streams, gain_terms, statistics = finish(
        halves,
        updates,
        moments,
        weights,
        (output, d_tokens),
        small,
        gains.T,
        gain_first.T,
        gain_second.T,
    )
    gain_terms = [term.T for term in gain_terms]
    grads, news, masters = (
        [parted(term) for term in group] for group in (grads, news, masters)
    )
    return (
        *streams,
        *grads,
        gain_terms[0],
        *news,
        *masters,
        *gain_terms[1:],
        statistics.reshape(4),
    )


def solution(mesh):
    in_specs = (
        P(("rep", "fsdp"), None),
        P(("rep", "fsdp"), None),
        P(),
        P("fsdp", None),
        P("fsdp", None),
        P("fsdp", None),
        P("fsdp", None),
        P("fsdp", None),
        P("fsdp", None),
        P("fsdp", None),
        P("fsdp", None),
        P("fsdp", None),
        P("fsdp", None),
        P("fsdp", None),
        P("fsdp", None),
        P("fsdp", None),
    )
    out_specs = (
        P(("rep", "fsdp"), None),
        P(("rep", "fsdp"), None),
        P("fsdp", None),
        P("fsdp", None),
        P("fsdp", None),
        P("fsdp", None),
        P("fsdp", None),
        P("fsdp", None),
        P("fsdp", None),
        P("fsdp", None),
        P("fsdp", None),
        P("fsdp", None),
        P("fsdp", None),
        P("fsdp", None),
        P("fsdp", None),
        P("fsdp", None),
        P("fsdp", None),
        P("fsdp", None),
        P("fsdp", None),
        P("fsdp", None),
        P("fsdp", None),
        P(),
    )
    return jax.shard_map(shards, mesh=mesh, in_specs=in_specs, out_specs=out_specs, check_vma=False)
```

```python
import jax
import jax.numpy as jnp
from jax import lax
from jax.experimental import pallas as pl
from jax.experimental.pallas import tpu as pltpu
from jax.sharding import PartitionSpec as P

HEADS = 4
HEAD_DIM = 256
NS_STEPS = 5
ADAM_STEP = 10


norm_epsilon = 1e-06
soft_cap = 50.0
rotary_base = 10000.0
newton_first = 3.4445
newton_second = -4.775
newton_third = 2.0315
momentum_decay = 0.95
muon_rate = 1.0
first_decay = 0.9
second_decay = 0.95
adam_rate = 1.0
weight_decay = 0.1
adam_epsilon = 1e-08
frobenius_epsilon = 1e-07

GROUP = 8
MESH = pl.DeviceIdType.MESH
f32 = jnp.float32
bf16 = jnp.bfloat16


def dot(a, b):
    return lax.dot_general(a, b, (((1,), (0,)), ((), ())), preferred_element_type=f32)


def dot_nt(a, b):
    return lax.dot_general(a, b, (((1,), (1,)), ((), ())), preferred_element_type=f32)


def dot_tn(a, b):
    return lax.dot_general(a, b, (((0,), (0,)), ((), ())), preferred_element_type=f32)


def place():
    size = lax.axis_size("fsdp")
    lanes = size // GROUP
    here = lax.axis_index("fsdp")
    return lax.axis_index("rep"), here // lanes, lax.rem(here, lanes), lanes


QKV, OUT, GATE, UP, DOWN = range(5)
CORE, ACROSS, ALONG = 1, 2, 4
PAIRS = (
    ((GATE, 0), (UP, 0)),
    ((DOWN, 0), (GATE, 1)),
    ((UP, 1), (DOWN, 1)),
    ((OUT, 0), (OUT, 1)),
    ((QKV, 0), (QKV, 1)),
)
CHUNK = 128
TILE = 256


def split_shape(number, shape):
    rows, cols = shape
    return (rows // 2, cols) if number in (OUT, DOWN) else (rows, cols // 2)


def layer_names(rows, keys, width, shapes, reps):
    halves = [split_shape(number, shape) for number, shape in enumerate(shapes)]
    feats = HEADS * HEAD_DIM
    inner = shapes[GATE][1]
    spaces = {}
    for number, (height, cols) in enumerate(shapes):
        spaces[f"whole{number}"] = pltpu.VMEM((height * GROUP, cols), bf16)
    spaces.update(
        cosine=pltpu.VMEM((rows, HEAD_DIM // 2), f32),
        sine=pltpu.VMEM((rows, HEAD_DIM // 2), f32),
        gain_parts=pltpu.VMEM((GROUP, 8, 128), f32),
        gains=pltpu.VMEM((8, width), f32),
        normed=pltpu.VMEM((rows, width), bf16),
        one_t=pltpu.VMEM((width, rows), bf16),
        two_t=pltpu.VMEM((width, rows), bf16),
        proj=pltpu.VMEM((rows, feats + 2 * HEAD_DIM), bf16),
        key=pltpu.VMEM((keys, HEAD_DIM), bf16),
        value=pltpu.VMEM((keys, HEAD_DIM), bf16),
        key_t=pltpu.VMEM((HEAD_DIM, keys), bf16),
        value_t=pltpu.VMEM((HEAD_DIM, keys), bf16),
        att=pltpu.VMEM((rows, feats), bf16),
        att_t=pltpu.VMEM((feats, rows), bf16),
        inverse=pltpu.VMEM((8, rows), f32),
        branch=pltpu.VMEM((rows, width), f32),
        hidden=pltpu.VMEM((rows, width), f32),
        slope=pltpu.VMEM((rows, inner), bf16),
        bend=pltpu.VMEM((rows, inner), bf16),
        active=pltpu.VMEM((rows, inner), bf16),
        d_key=pltpu.VMEM((keys, HEAD_DIM), f32),
        d_value=pltpu.VMEM((keys, HEAD_DIM), f32),
        swap_in=pltpu.VMEM((rows, 2 * HEAD_DIM), bf16),
        squares=pltpu.VMEM((8, width), f32),
        d_gains=pltpu.VMEM((8, width), f32),
        small_parts=pltpu.VMEM((GROUP, 8, width), f32),
        small_reps=pltpu.VMEM((reps, 8, width), f32),
    )
    for number, half in enumerate(halves):
        spaces[f"stage{number}"] = pltpu.VMEM((2, 2, 2, 2) + half, bf16)
        spaces[f"chip{number}"] = pltpu.VMEM((2, 2, 2) + half, bf16)
        spaces[f"pair{number}"] = pltpu.VMEM((2, 2) + half, bf16)
        spaces[f"plane{number}"] = pltpu.VMEM((2,) + half, bf16)
        spaces[f"line{number}"] = pltpu.VMEM((2, 2) + half, bf16)
        spaces[f"total{number}"] = pltpu.VMEM((2,) + half, bf16)
    dma = pltpu.SemaphoreType.DMA
    spaces.update(
        own_sem=dma((5,)),
        result_sem=dma((5,)),
        weight_send=dma((5, 11)),
        weight_recv=dma((5, 11)),
        gain_send=dma((GROUP,)),
        gain_recv=dma((GROUP,)),
        key_send=dma((2,)),
        key_recv=dma((2,)),
        swap_send=dma((1,)),
        swap_recv=dma((1,)),
        chip_send=dma((5, 2)),
        chip_recv=dma((5, 2)),
        pair_send=dma((5, 2)),
        pair_recv=dma((5, 2)),
        plane_send=dma((5, 2)),
        plane_recv=dma((5, 2)),
        line_send=dma((5, 2)),
        line_recv=dma((5, 2, 2)),
        total_send=dma((5, 2)),
        total_recv=dma((5, 2)),
        small_send=dma((GROUP,)),
        small_recv=dma((GROUP,)),
        reps_send=dma((reps,)),
        reps_recv=dma((reps,)),
    )
    return spaces


class Refs:
    def __init__(self, names, refs):
        self.__dict__.update(zip(names, refs))


def column_sum(x):
    return jnp.sum(x, axis=0, keepdims=True)


def row_mean(x):
    return jnp.mean(x, axis=-1, keepdims=True)


def layer_kernel(names, shapes, *refs):
    v = Refs(names, refs)
    rep, me, lane, lanes = place()
    reps = lax.axis_size("rep")
    here = lax.axis_index("fsdp")
    core, across, along = me % 2, (me // 2) % 2, me // 4
    rows, width = v.tokens.shape
    parity = here % 2
    weights = [v.w_qkv, v.w_out, v.w_gate, v.w_up, v.w_down]
    named = lambda name: [getattr(v, f"{name}{number}") for number in range(5)]
    whole, stage, chip, pair = named("whole"), named("stage"), named("chip"), named("pair")
    plane, line, total, result = named("plane"), named("line"), named("total"), named("grad")

    def device(member):
        return (rep, member * lanes + lane)

    def remote(src, dst, send, recv, where):
        return pltpu.make_async_remote_copy(
            src_ref=src,
            dst_ref=dst,
            send_sem=send,
            recv_sem=recv,
            device_id=where,
            device_id_type=MESH,
        )

    barrier = pltpu.get_barrier_semaphore()
    greeted = [device(me ^ step) for step in range(1, GROUP)]
    greeted += [(lax.rem(rep + step, reps), here) for step in range(1, reps)]
    if lanes > 1:
        greeted.append((rep, here ^ 1))
    for where in greeted:
        pl.semaphore_signal(barrier, inc=1, device_id=where, device_id_type=MESH)
    pl.semaphore_wait(barrier, len(greeted))

    odd = rep % 2

    def parts(number):
        rows_or_cols, tile = shapes[number][1], 128
        if number in (OUT, DOWN):
            rows_or_cols, tile = shapes[number][0], 16
        outer = (rows_or_cols // tile + 1) // 3 * tile
        return outer, rows_or_cols - 2 * outer, tile

    def window(number, member, start, size, tile):
        height = shapes[number][0]
        base = pl.multiple_of(member * height, 16)
        if number in (OUT, DOWN):
            return whole[number].at[pl.ds(pl.multiple_of(base + start, 16), size), :]
        return whole[number].at[pl.ds(base, height), pl.ds(pl.multiple_of(start, 128), size)]

    def slot(number, member):
        height = shapes[number][0]
        return whole[number].at[pl.ds(pl.multiple_of(member * height, 16), height), :]

    def outer_part(number, member):
        outer, middle, tile = parts(number)
        return window(number, member, odd * (outer + middle), outer, tile)

    def middle_part(number, member):
        outer, middle, tile = parts(number)
        return window(number, member, outer, middle, tile)

    def own_parts(number):
        outer, middle, tile = parts(number)
        start = pl.multiple_of(odd * outer, tile)
        if number in (OUT, DOWN):
            return weights[number].at[pl.ds(start, outer + middle), :]
        return weights[number].at[:, pl.ds(start, outer + middle)]

    def both_parts(number, member):
        outer, middle, tile = parts(number)
        return window(number, member, odd * outer, outer + middle, tile)

    def weight_copy(number, kind):
        beside, ahead = me ^ ACROSS, me ^ ALONG
        corner = beside ^ ALONG
        if kind == 0:
            src, dst, where = weights[number], slot(number, me), device(me ^ CORE)
        elif kind < 3:
            src, dst = own_parts(number), both_parts(number, me)
            where = device((beside, ahead)[kind - 1])
        elif kind < 5:
            src = outer_part(number, beside) if kind == 3 else middle_part(number, ahead)
            dst, where = src, device((ahead, beside)[kind - 3])
        elif kind < 8:
            src = outer_part(number, (beside, ahead, corner)[kind - 5])
            dst, where = src, (rep + 1 - 2 * odd, here)
        else:
            src = slot(number, (beside, ahead, corner)[kind - 8])
            dst, where = src, device(me ^ CORE)
        return remote(
            src, dst, v.weight_send.at[number, kind], v.weight_recv.at[number, kind], where
        )

    def own_copy(number):
        return pltpu.make_async_copy(weights[number], slot(number, me), v.own_sem.at[number])

    def weight_begin(number):
        for kind in (1, 2, 0):
            weight_copy(number, kind).start()
        own_copy(number).start()

    def weight_forward(number):
        weight_copy(number, 1).wait_recv()
        weight_copy(number, 3).start()
        weight_copy(number, 5).start()
        weight_copy(number, 2).wait_recv()
        weight_copy(number, 4).start()
        weight_copy(number, 6).start()

    def weight_corner(number):
        weight_copy(number, 3).wait_recv()
        weight_copy(number, 7).start()

    def weight_cross(number):
        weight_copy(number, 5).wait_recv()
        weight_copy(number, 8).start()
        weight_copy(number, 6).wait_recv()
        weight_copy(number, 9).start()
        weight_copy(number, 4).wait_recv()
        weight_copy(number, 7).wait_recv()
        weight_copy(number, 10).start()

    def weight_ready(number):
        own_copy(number).wait()
        for kind in (0, 8, 9, 10):
            weight_copy(number, kind).wait_recv()

    weight_begin(QKV)

    def gain_copy(step):
        return remote(
            v.gain_parts.at[me],
            v.gain_parts.at[me],
            v.gain_send.at[step],
            v.gain_recv.at[step],
            device(me ^ step),
        )

    gain_count, gain_rows = v.gain_block.shape
    v.gain_parts[me] = jnp.zeros_like(v.gain_parts[me])
    v.gain_parts[me, 0:gain_count, 0:gain_rows] = v.gain_block[...].astype(f32)
    for step in range(1, GROUP):
        gain_copy(step).start()
    weight_begin(OUT)
    weight_begin(GATE)
    v.squares[...] = jnp.zeros_like(v.squares)
    v.d_gains[...] = jnp.zeros_like(v.d_gains)
    v.d_key[...] = jnp.zeros_like(v.d_key)
    v.d_value[...] = jnp.zeros_like(v.d_value)
    spot = lax.broadcasted_iota(jnp.int32, (rows, HEAD_DIM // 2), 0) + parity * rows
    angles = spot.astype(f32) * v.frequency[...]
    v.cosine[...] = jnp.cos(angles)
    v.sine[...] = jnp.sin(angles)
    for step in range(1, GROUP):
        gain_copy(step).wait_recv()
    for member in range(GROUP):
        v.gains[:, member * gain_rows : (member + 1) * gain_rows] = v.gain_parts[
            member, :, 0:gain_rows
        ]

    prefix = v.prefix[(rep * lax.axis_size("fsdp") + here) // 2]

    def valid_rows(start, count):
        spot = lax.broadcasted_iota(jnp.int32, (count, 1), 0) + (parity * rows + start)
        return jnp.where(spot >= prefix, 1.0, 0.0)

    def by_rows(body):
        @pl.loop(0, rows // CHUNK)
        def _(k):
            start = pl.multiple_of(k * CHUNK, CHUNK)
            body(pl.ds(start, CHUNK), start)

    def by_columns(count, body):
        @pl.loop(0, count // TILE)
        def _(k):
            body(pl.ds(pl.multiple_of(k * TILE, TILE), TILE), k)

    def inverse_root(x):
        return lax.rsqrt(row_mean(x * x) + norm_epsilon)

    def norm_back(x, scale, upstream, gain, row):
        v.d_gains[row : row + 1, :] += column_sum(upstream * x * scale)
        spread = upstream * gain
        return scale * spread - x * (scale * scale * scale * row_mean(x * spread))

    gain_row = lambda k: v.gains[k : k + 1, :]

    def first_norm(here_rows, start):
        x = v.tokens[here_rows, :].astype(f32)
        normed = x * inverse_root(x) * gain_row(0)
        v.normed[here_rows, :] = normed.astype(bf16)
        v.one_t[:, here_rows] = normed.T.astype(bf16)
        v.squares[0:1, :] += column_sum(valid_rows(start, CHUNK) * (x * x))

    by_rows(first_norm)
    weight_forward(QKV)
    weight_corner(QKV)
    weight_forward(OUT)
    weight_begin(UP)
    weight_cross(QKV)
    weight_corner(OUT)
    weight_ready(QKV)

    feats = HEADS * HEAD_DIM
    half_dim = HEAD_DIM // 2
    own_rows = pl.ds(pl.multiple_of(parity * rows, rows), rows)
    other_rows = pl.ds(pl.multiple_of((1 - parity) * rows, rows), rows)

    def rotate(x, sign):
        first, second = x[:, :half_dim], x[:, half_dim:]
        cosine, sine = v.cosine[...], v.sine[...] * sign
        return first * cosine - second * sine, second * cosine + first * sine

    def key_copy(number):
        ref = (v.key, v.value)[number]
        return remote(
            ref.at[own_rows, :],
            ref.at[own_rows, :],
            v.key_send.at[number],
            v.key_recv.at[number],
            (rep, here ^ 1),
        )

    key_part = dot(v.normed[...], whole[QKV][:, feats : feats + HEAD_DIM])
    first, second = rotate(key_part, 1.0)
    v.key[own_rows, :half_dim] = first.astype(bf16)
    v.key[own_rows, half_dim:] = second.astype(bf16)
    key_copy(0).start()
    v.value[own_rows, :] = dot(v.normed[...], whole[QKV][:, feats + HEAD_DIM :]).astype(bf16)
    key_copy(1).start()

    @pl.loop(0, HEADS)
    def _(head):
        start = pl.multiple_of(head * HEAD_DIM, HEAD_DIM)
        part = dot(v.normed[...], whole[QKV][:, pl.ds(start, HEAD_DIM)])
        first, second = rotate(part, 1.0)
        v.proj[:, pl.ds(start, half_dim)] = first.astype(bf16)
        v.proj[:, pl.ds(start + half_dim, half_dim)] = second.astype(bf16)

    weight_forward(GATE)
    weight_begin(DOWN)
    for number in range(2):
        key_copy(number).wait_recv()
    v.key_t[...] = v.key[...].astype(f32).T.astype(bf16)
    v.value_t[...] = v.value[...].astype(f32).T.astype(bf16)

    keys = v.key.shape[0]
    bend_scale = HEAD_DIM ** (-0.5) / soft_cap

    def head_columns(head):
        return pl.ds(pl.multiple_of(head * HEAD_DIM, HEAD_DIM), HEAD_DIM)

    def scores(head, start):
        here_rows = pl.ds(start, TILE)
        query = v.proj[here_rows, head_columns(head)]
        bent = jnp.tanh(dot_nt(v.key[...], query) * bend_scale)
        spot = lax.broadcasted_iota(jnp.int32, (1, TILE), 1) + (parity * rows + start)
        last = jnp.maximum(spot, prefix - 1)
        allowed = lax.broadcasted_iota(jnp.int32, (keys, TILE), 0) <= last
        return bent, jnp.where(allowed, jnp.exp(soft_cap * bent), 0.0), query

    blocks = rows // TILE

    def attend(begin, end):
        @pl.loop(begin, end)
        def _(k):
            head = k // blocks
            start = pl.multiple_of(lax.rem(k, blocks) * TILE, TILE)
            cols, here_rows = head_columns(head), pl.ds(start, TILE)
            _, power, _ = scores(head, start)
            inverse = 1.0 / column_sum(power)
            v.inverse[pl.ds(head, 1), here_rows] = inverse
            mixed = dot(v.value_t[...], (power * inverse).astype(bf16))
            v.att_t[cols, here_rows] = mixed.astype(bf16)
            v.att[here_rows, cols] = mixed.T.astype(bf16)

    weight_cross(OUT)
    weight_corner(GATE)
    weight_forward(UP)
    attend(0, 2)
    weight_cross(GATE)
    attend(2, 4)
    weight_corner(UP)
    weight_forward(DOWN)
    attend(4, 6)
    weight_cross(UP)
    weight_corner(DOWN)
    attend(6, 8)
    weight_ready(OUT)

    v.branch[...] = dot(v.att[...], whole[OUT][...])

    def second_norm(here_rows, start):
        x = v.branch[here_rows, :]
        first_out = x * inverse_root(x) * gain_row(1)
        hidden = v.tokens[here_rows, :].astype(f32) + first_out
        v.hidden[here_rows, :] = hidden
        normed = hidden * inverse_root(hidden) * gain_row(2)
        v.normed[here_rows, :] = normed.astype(bf16)
        v.two_t[:, here_rows] = normed.T.astype(bf16)
        v.squares[1:2, :] += column_sum(valid_rows(start, CHUNK) * (first_out * first_out))

    by_rows(second_norm)
    weight_ready(GATE)
    weight_ready(UP)
    inner = shapes[GATE][1]

    def feed(cols, k):
        gate = dot(v.normed[...], whole[GATE][:, cols])
        upward = dot(v.normed[...], whole[UP][:, cols])
        square = gate * gate
        bent = jnp.tanh(0.7978845608028654 * (gate + 0.044715 * gate * square))
        open_half = 0.5 * (1.0 + bent)
        smooth = gate * open_half
        steep = open_half + gate * (1.0 - bent * bent) * (
            0.3989422804014327 * (1.0 + 3.0 * 0.044715 * square)
        )
        v.active[:, cols] = (smooth * upward).astype(bf16)
        v.bend[:, cols] = smooth.astype(bf16)
        v.slope[:, cols] = (steep * upward).astype(bf16)

    by_columns(inner, feed)
    weight_cross(DOWN)
    weight_ready(DOWN)

    v.d_tokens[...] = dot(v.active[...], whole[DOWN][...])

    def last_norm(here_rows, start):
        x = v.d_tokens[here_rows, :]
        scale = inverse_root(x)
        second_out = x * scale * gain_row(3)
        final = v.hidden[here_rows, :] + second_out
        v.output[here_rows, :] = final
        valid = valid_rows(start, CHUNK)
        v.squares[2:3, :] += column_sum(valid * (second_out * second_out))
        v.squares[3:4, :] += column_sum(valid * (final * final))
        upstream = v.cotangent[here_rows, :].astype(f32)
        v.normed[here_rows, :] = norm_back(x, scale, upstream, gain_row(3), 3).astype(bf16)

    by_rows(last_norm)

    def first_across(number, half):
        return any(one == (number, half) for one, _ in PAIRS)

    def chip_copy(number, half):
        return remote(
            stage[number].at[half, :, :, 1 - core],
            chip[number].at[half],
            v.chip_send.at[number, half],
            v.chip_recv.at[number, half],
            device(me ^ CORE),
        )

    def pair_copy(number, half):
        if first_across(number, half):
            src, where = chip[number].at[half, :, 1 - across], me ^ ACROSS
        else:
            src, where = chip[number].at[half, 1 - along], me ^ ALONG
        return remote(
            src,
            pair[number].at[half],
            v.pair_send.at[number, half],
            v.pair_recv.at[number, half],
            device(where),
        )

    def plane_copy(number, half):
        if first_across(number, half):
            src, where = pair[number].at[half, 1 - along], me ^ ALONG
        else:
            src, where = pair[number].at[half, 1 - across], me ^ ACROSS
        return remote(
            src,
            plane[number].at[half],
            v.plane_send.at[number, half],
            v.plane_recv.at[number, half],
            device(where),
        )

    def added(one, two):
        return one + two

    def chip_begin(number, half):
        chip_copy(number, half).start()

    def chip_end(number, half):
        chip_copy(number, half).wait_recv()

        @pl.loop(0, 4)
        def _(k):
            one, two = k // 2, k % 2
            chip[number][half, one, two] = added(
                chip[number][half, one, two], stage[number][half, one, two, core]
            )

        pair_copy(number, half).start()

    def pair_end(number, half):
        pair_copy(number, half).wait_recv()

        @pl.loop(0, 2)
        def _(k):
            if first_across(number, half):
                mine = chip[number][half, k, across]
            else:
                mine = chip[number][half, along, k]
            pair[number][half, k] = added(pair[number][half, k], mine)

        plane_copy(number, half).start()

    def plane_end(number, half):
        plane_copy(number, half).wait_recv()
        kept = along if first_across(number, half) else across
        plane[number][half] = added(plane[number][half], pair[number][half, kept])

        @pl.when(at_end)
        def _():
            line_send(number, half)

    order = [half for both in PAIRS for half in both]

    on_left = rep < reps // 2
    inward = jnp.where(on_left, 1, -1)
    at_end = (rep == 0) | (rep == reps - 1)
    at_middle = (rep == reps // 2 - 1) | (rep == reps // 2)

    def line_copy(number, half, way):
        return remote(
            plane[number].at[half],
            line[number].at[half, way],
            v.line_send.at[number, half],
            v.line_recv.at[number, half, way],
            (rep + inward, here),
        )

    def total_copy(number, half):
        return remote(
            total[number].at[half],
            total[number].at[half],
            v.total_send.at[number, half],
            v.total_recv.at[number, half],
            (rep - inward, here),
        )

    def line_send(number, half):
        @pl.when(jnp.logical_not(at_middle))
        def _():
            line_copy(number, half, 0).start()

        @pl.when(at_middle)
        def _():
            line_copy(number, half, 1).start()

    def line_begin(number, half):
        @pl.when(jnp.logical_not(at_end))
        def _():
            line_copy(number, half, 0).wait_recv()
            plane[number][half] = added(plane[number][half], line[number][half, 0])
            line_send(number, half)

    def line_end(number, half):
        @pl.when(at_middle)
        def _():
            line_copy(number, half, 1).wait_recv()
            total[number][half] = added(plane[number][half], line[number][half, 1])

            @pl.when(jnp.logical_not(at_end))
            def _():
                total_copy(number, half).start()

    def total_end(number, half):
        @pl.when(jnp.logical_not(at_middle))
        def _():
            total_copy(number, half).wait_recv()

            @pl.when(jnp.logical_not(at_end))
            def _():
                total_copy(number, half).start()

    def for_pair(action, index):
        for number, half in PAIRS[index]:
            action(number, half)

    def keep_columns(number, col_half, col, found):
        height = shapes[number][0]
        for member in range(GROUP):
            stage[number][
                col_half, member // 4, (member // 2) % 2, member % 2, :, pl.ds(col, TILE)
            ] = found[member * height : (member + 1) * height].astype(bf16)

    down_rows = shapes[DOWN][0]
    halved = inner // 2 // TILE

    def feed_back(side, begin, end):
        @pl.loop(begin, end)
        def _(k):
            col = pl.multiple_of(k * TILE, TILE)
            start = pl.multiple_of(side * (inner // 2) + k * TILE, TILE)
            cols = pl.ds(start, TILE)
            d_active = dot_nt(v.normed[...], whole[DOWN][cols, :])
            d_gate = (d_active * v.slope[:, cols].astype(f32)).astype(bf16)
            d_upward = (d_active * v.bend[:, cols].astype(f32)).astype(bf16)
            v.slope[:, cols] = d_gate
            v.bend[:, cols] = d_upward
            keep_columns(GATE, side, col, dot(v.two_t[...], d_gate))
            keep_columns(UP, side, col, dot(v.two_t[...], d_upward))
            found = dot_tn(v.active[:, cols], v.normed[...]).astype(bf16)
            per = TILE // down_rows
            for part in range(per):
                member = (side * halved + k) * per + part
                y, x, c = member // 4, (member // 2) % 2, member % 2
                base = part * down_rows
                stage[DOWN][0, y, x, c] = found[base : base + down_rows // 2]
                stage[DOWN][1, y, x, c] = found[base + down_rows // 2 : base + down_rows]

    feed_back(0, 0, halved)
    for_pair(chip_begin, 0)
    feed_back(1, 0, halved // 2)
    for_pair(chip_end, 0)
    feed_back(1, halved // 2, halved)
    for_pair(chip_begin, 1)
    for_pair(chip_begin, 2)
    v.d_tokens[...] = dot_nt(v.slope[...], whole[GATE][...])
    for_pair(chip_end, 1)
    v.d_tokens[...] += dot_nt(v.bend[...], whole[UP][...])
    for_pair(chip_end, 2)

    def middle_norms(here_rows, start):
        x = v.hidden[here_rows, :]
        flow = norm_back(x, inverse_root(x), v.d_tokens[here_rows, :], gain_row(2), 2)
        d_hidden = v.cotangent[here_rows, :].astype(f32) + flow
        v.d_tokens[here_rows, :] = d_hidden
        x = v.branch[here_rows, :]
        flow = norm_back(x, inverse_root(x), d_hidden, gain_row(1), 1)
        v.normed[here_rows, :] = flow.astype(bf16)

    by_rows(middle_norms)
    for_pair(pair_end, 0)
    out_rows = shapes[OUT][0]
    v.att[...] = dot_nt(v.normed[...], whole[OUT][...]).astype(bf16)

    @pl.loop(0, GROUP // 2)
    def _(k):
        start = pl.multiple_of(k * 2 * out_rows, 2 * out_rows)
        found = dot(v.att_t[pl.ds(start, 2 * out_rows), :], v.normed[...]).astype(bf16)
        for part in range(4):
            stage[OUT][part % 2, k // 2, k % 2, part // 2] = found[
                part * (out_rows // 2) : (part + 1) * (out_rows // 2)
            ]

    for_pair(chip_begin, 3)
    for_pair(pair_end, 1)
    for_pair(plane_end, 0)

    def attend_back(begin, end):
        @pl.loop(begin, end)
        def _(k):
            head = k // blocks
            start = pl.multiple_of(lax.rem(k, blocks) * TILE, TILE)
            here_rows = pl.ds(start, TILE)
            bent, power, query = scores(head, start)
            soft = power * v.inverse[pl.ds(head, 1), here_rows]
            flow = v.att[here_rows, head_columns(head)]
            d_soft = dot_nt(v.value[...], flow)
            v.d_value[...] += dot(soft.astype(bf16), flow)
            level = column_sum(d_soft * soft)
            d_raw = soft * (d_soft - level) * ((1.0 - bent * bent) * HEAD_DIM ** (-0.5))
            d_raw = d_raw.astype(bf16)
            v.d_key[...] += dot(d_raw, query)
            d_query = dot(v.key_t[...], d_raw).T
            first, second = d_query[:, :half_dim], d_query[:, half_dim:]
            cosine, sine = v.cosine[here_rows, :], v.sine[here_rows, :]
            base = pl.multiple_of(head * HEAD_DIM, HEAD_DIM)
            v.proj[here_rows, pl.ds(base, half_dim)] = (first * cosine + second * sine).astype(
                bf16
            )
            v.proj[here_rows, pl.ds(base + half_dim, half_dim)] = (
                second * cosine - first * sine
            ).astype(bf16)

    swap = remote(
        v.att.at[:, 0 : 2 * HEAD_DIM],
        v.swap_in,
        v.swap_send.at[0],
        v.swap_recv.at[0],
        (rep, here ^ 1),
    )

    attend_back(0 * blocks, 1 * blocks)
    for_pair(chip_end, 3)
    attend_back(1 * blocks, 2 * blocks)
    for_pair(pair_end, 2)
    attend_back(2 * blocks, 3 * blocks)
    for_pair(line_begin, 0)
    for_pair(plane_end, 1)
    attend_back(3 * blocks, 4 * blocks)
    v.att[:, 0:HEAD_DIM] = v.d_key[other_rows, :].astype(bf16)
    v.att[:, HEAD_DIM : 2 * HEAD_DIM] = v.d_value[other_rows, :].astype(bf16)
    swap.start()
    for_pair(pair_end, 3)

    qkv_half = split_shape(QKV, shapes[QKV])[1] // TILE

    def projection_grad(tile):
        found = dot(v.one_t[...], v.proj[:, tile * TILE : (tile + 1) * TILE])
        keep_columns(QKV, tile // qkv_half, (tile % qkv_half) * TILE, found)

    for tile in range(qkv_half):
        projection_grad(tile)
    chip_begin(QKV, 0)
    swap.wait_recv()
    d_key = v.d_key[own_rows, :] + v.swap_in[:, 0:HEAD_DIM].astype(f32)
    first, second = rotate(d_key, -1.0)
    v.proj[:, feats : feats + half_dim] = first.astype(bf16)
    v.proj[:, feats + half_dim : feats + HEAD_DIM] = second.astype(bf16)
    v.proj[:, feats + HEAD_DIM :] = (
        v.d_value[own_rows, :] + v.swap_in[:, HEAD_DIM:].astype(f32)
    ).astype(bf16)
    for tile in range(qkv_half, 2 * qkv_half):
        projection_grad(tile)
    chip_begin(QKV, 1)
    for_pair(chip_end, 4)
    for_pair(line_begin, 1)
    for_pair(plane_end, 2)
    for_pair(line_end, 0)
    v.branch[...] = dot_nt(v.proj[...], whole[QKV][...])
    for_pair(plane_end, 3)

    def first_norm_back(here_rows, start):
        x = v.tokens[here_rows, :].astype(f32)
        flow = norm_back(x, inverse_root(x), v.branch[here_rows, :], gain_row(0), 0)
        v.d_tokens[here_rows, :] += flow

    by_rows(first_norm_back)

    def small_copy(step):
        return remote(
            v.small_parts.at[me],
            v.small_parts.at[me],
            v.small_send.at[step],
            v.small_recv.at[step],
            device(me ^ step),
        )

    def reps_copy(step):
        return remote(
            v.small_reps.at[rep],
            v.small_reps.at[rep],
            v.reps_send.at[step],
            v.reps_recv.at[step],
            (lax.rem(rep + step, reps), here),
        )

    spot = lax.broadcasted_iota(jnp.int32, (1, width), 1)
    numbers = jnp.where(spot == 4, column_sum(valid_rows(0, rows)), 0.0)
    for k in range(4):
        summed = jnp.sum(v.squares[k : k + 1, :], axis=1, keepdims=True)
        numbers = numbers + jnp.where(spot == k, summed, 0.0)
    v.d_gains[4:5, :] = numbers
    v.small_parts[me] = v.d_gains[...]
    for step in range(1, GROUP):
        small_copy(step).start()
    for_pair(line_end, 1)
    for_pair(total_end, 0)
    for_pair(pair_end, 4)
    for_pair(line_begin, 2)
    for_pair(line_begin, 3)
    for_pair(total_end, 1)
    for step in range(1, GROUP):
        small_copy(step).wait_recv()
    v.small_reps[rep] = jnp.sum(v.small_parts[...], axis=0)
    for step in range(1, reps):
        reps_copy(step).start()
    for_pair(line_end, 2)
    for_pair(plane_end, 4)
    for_pair(line_end, 3)
    for_pair(total_end, 2)
    for_pair(line_begin, 4)
    for_pair(total_end, 3)
    for_pair(line_end, 4)
    for_pair(total_end, 4)
    for step in range(1, reps):
        reps_copy(step).wait_recv()
    v.small[...] = jnp.sum(v.small_reps[...], axis=0)
    results = [
        pltpu.make_async_copy(total[number], result[number], v.result_sem.at[number])
        for number in range(5)
    ]
    for copy in results:
        copy.start()

    for number in range(5):
        for kind in range(11):
            weight_copy(number, kind).wait_send()
    for number in range(2):
        key_copy(number).wait_send()
    swap.wait_send()
    for step in range(1, GROUP):
        gain_copy(step).wait_send()
        small_copy(step).wait_send()
    for step in range(1, reps):
        reps_copy(step).wait_send()
    for number, half in order:
        chip_copy(number, half).wait_send()
        pair_copy(number, half).wait_send()
        plane_copy(number, half).wait_send()
        line_copy(number, half, 0).wait_send()

        @pl.when(jnp.logical_not(at_end))
        def _():
            total_copy(number, half).wait_send()

    for copy in results:
        copy.wait()


def layer(prefix, tokens, cotangent, frequency, gain_block, weights, reps):
    shapes = tuple(w.shape for w in weights)
    rows, width = tokens.shape
    spaces = layer_names(rows, 2 * rows, width, shapes, reps)
    halves = [split_shape(number, shape) for number, shape in enumerate(shapes)]
    inputs = ["prefix", "tokens", "cotangent", "frequency", "gain_block"]
    inputs += ["w_qkv", "w_out", "w_gate", "w_up", "w_down"]
    outputs = ["output", "d_tokens", "small"] + [f"grad{number}" for number in range(5)]
    vmem = pl.BlockSpec(memory_space=pltpu.VMEM)
    names = inputs + outputs + list(spaces)
    out = pl.pallas_call(
        lambda *refs: layer_kernel(names, shapes, *refs),
        out_shape=[
            jax.ShapeDtypeStruct((rows, width), f32),
            jax.ShapeDtypeStruct((rows, width), f32),
            jax.ShapeDtypeStruct((8, width), f32),
        ]
        + [jax.ShapeDtypeStruct((2,) + half, bf16) for half in halves],
        in_specs=[pl.BlockSpec(memory_space=pltpu.SMEM)]
        + [vmem] * 4
        + [pl.BlockSpec(memory_space=pl.ANY)] * 5,
        out_specs=[vmem] * 3 + [pl.BlockSpec(memory_space=pl.ANY)] * 5,
        scratch_shapes=list(spaces.values()),
        compiler_params=pltpu.CompilerParams(
            collective_id=2, has_side_effects=True, vmem_limit_bytes=64 * 2**20
        ),
        name="layer",
    )(prefix, tokens, cotangent, frequency, gain_block, *weights)
    return out[0], out[1], out[2], out[3:]


OWNERS = (6, 7, 0, 2, 4)
FLIPPED = (False, True, False, False, True)


def gram_into(x_ref, gram):
    rows = gram.shape[0]
    starts = list(range(0, rows, 256))
    for j in starts:
        n = min(256, rows - j)
        gram[j:rows, j : j + n] = dot_nt(x_ref[j:rows, :], x_ref[j : j + n, :])
    for j in starts:
        n = min(256, rows - j)
        if j + n < rows:
            gram[j : j + n, j + n : rows] = gram[j + n : rows, j : j + n].T


def newton_step(x_ref, gram, mixer, high, low, first, refined):
    gram_into(x_ref, gram)
    rows = gram.shape[0]
    same = lax.broadcasted_iota(jnp.int32, (rows, rows), 0) == lax.broadcasted_iota(
        jnp.int32, (rows, rows), 1
    )
    whole = gram[...]
    scale = None
    if first is not None:
        trace = jnp.sum(jnp.where(same, whole, 0.0))
        scale = jnp.where(first, 1.0 / (jnp.sqrt(trace) + frobenius_epsilon), 1.0)
        whole = whole * (scale * scale)
        gram[...] = whole
    high[...] = whole.astype(bf16)
    squared = dot(high[...], high[...])
    if refined:
        low[...] = (gram[...] - high[...].astype(f32)).astype(bf16)
        squared = squared + dot(high[...], low[...]) + dot(low[...], high[...])
    mix = (
        jnp.where(same, newton_first, 0.0) + newton_second * gram[...] + newton_third * squared
    )
    if scale is not None:
        mix = mix * scale
    mixer[...] = mix.astype(bf16)
    x_ref[...] = dot(mixer[...], x_ref[...]).astype(bf16)


def muon_kernel(shapes, *refs):
    sources, results = refs[0:10], refs[10:15]
    outgoing, arrived = refs[15:20], refs[20:25]
    x_all, gram, mixer, high, low = refs[25:30]
    gather_send, gather_recv, scatter_send, scatter_recv, load_sem = refs[30:35]
    loaded = refs[35:45]
    grads, moments = loaded[0:5], loaded[5:10]
    loads = [
        pltpu.make_async_copy(source, target, load_sem.at[k])
        for k, (source, target) in enumerate(zip(sources, loaded))
    ]
    for load in loads:
        load.start()
    rep, me, lane, lanes = place()

    def device(member):
        return (rep, member * lanes + lane)

    owner_here = me == OWNERS[0]
    for owner in OWNERS[1:]:
        owner_here = owner_here | (me == owner)

    @pl.when(owner_here)
    def _():
        x_all[...] = jnp.zeros_like(x_all)

    barrier = pltpu.get_barrier_semaphore()
    for step in range(1, GROUP):
        pl.semaphore_signal(
            barrier, inc=1, device_id=device(me ^ step), device_id_type=MESH
        )

    def block(number, member):
        rows, cols = shapes[number]
        if FLIPPED[number]:
            return x_all.at[:, pl.ds(member * rows, rows)]
        return x_all.at[pl.ds(member * rows, rows), pl.ds(0, cols)]

    def gather_copy(number, member, sender):
        rows, _ = shapes[number]
        if FLIPPED[number]:
            start = pl.multiple_of(sender * rows, rows)
            target = x_all.at[:, pl.ds(start, rows)]
        else:
            start = pl.multiple_of(sender * rows, 16)
            target = x_all.at[pl.ds(start, rows), pl.ds(0, shapes[number][1])]
        return pltpu.make_async_remote_copy(
            src_ref=outgoing[number],
            dst_ref=target,
            send_sem=gather_send.at[number],
            recv_sem=gather_recv.at[sender],
            device_id=device(member),
            device_id_type=MESH,
        )

    pl.semaphore_wait(barrier, GROUP - 1)
    for number in (2, 3, 4, 0, 1):
        loads[number].wait()
        loads[5 + number].wait()
        grad = jnp.concatenate(
            [grads[number][0], grads[number][1]], axis=0 if number in (OUT, DOWN) else 1
        ).astype(f32)
        new = momentum_decay * moments[number][...] + (1.0 - momentum_decay) * grad
        nesterov = (1.0 - momentum_decay) * grad + momentum_decay * new
        if FLIPPED[number]:
            nesterov = nesterov.T
        outgoing[number][...] = nesterov.astype(bf16)

        @pl.when(me != OWNERS[number])
        def _():
            gather_copy(number, OWNERS[number], me).start()

    for number in range(5):
        owner = OWNERS[number]

        @pl.when(me == owner)
        def _():
            rows, cols = shapes[number]
            if FLIPPED[number]:
                x_all[:, owner * rows : (owner + 1) * rows] = outgoing[number][...]
            else:
                x_all[owner * rows : (owner + 1) * rows, 0:cols] = outgoing[number][...]
            for step in range(1, GROUP):
                gather_copy(number, owner, owner ^ step).wait_recv()

    @pl.when(owner_here)
    def _():
        @pl.loop(0, NS_STEPS - 2)
        def _(k):
            newton_step(x_all, gram, mixer, high, low, k == 0, False)

        @pl.loop(0, 2)
        def _(k):
            newton_step(x_all, gram, mixer, high, low, None, True)

    def scatter_copy(number, member):
        rows, cols = shapes[number]
        return pltpu.make_async_remote_copy(
            src_ref=block(number, member),
            dst_ref=arrived[number],
            send_sem=scatter_send.at[member],
            recv_sem=scatter_recv.at[number],
            device_id=device(member),
            device_id_type=MESH,
        )

    for number in range(5):
        owner = OWNERS[number]

        @pl.when(me == owner)
        def _():
            for step in range(1, GROUP):
                scatter_copy(number, owner ^ step).start()
            arrived[number][...] = block(number, owner)[...]

    for number in range(5):
        owner = OWNERS[number]

        @pl.when(me != owner)
        def _():
            scatter_copy(number, owner).wait_recv()

        update = arrived[number][...]
        if FLIPPED[number]:
            update = update.astype(f32).T.astype(bf16)
        results[number][...] = update

    for number in range(5):
        owner = OWNERS[number]

        @pl.when(me == owner)
        def _():
            for step in range(1, GROUP):
                scatter_copy(number, owner ^ step).wait_send()

        @pl.when(me != owner)
        def _():
            gather_copy(number, owner, me).wait_send()


def muon(grads, moments):
    shapes = tuple(moment.shape for moment in moments)
    flipped = [s[::-1] if flip else s for s, flip in zip(shapes, FLIPPED)]
    side = shapes[0][0] * GROUP
    width = max(s[0] * GROUP if flip else s[1] for s, flip in zip(shapes, FLIPPED))
    vmem = pl.BlockSpec(memory_space=pltpu.VMEM)
    return pl.pallas_call(
        lambda *refs: muon_kernel(shapes, *refs),
        out_shape=[jax.ShapeDtypeStruct(s, bf16) for s in shapes],
        in_specs=[pl.BlockSpec(memory_space=pl.ANY)] * 10,
        out_specs=[vmem] * 5,
        scratch_shapes=[pltpu.VMEM(s, bf16) for s in flipped]
        + [pltpu.VMEM(s, bf16) for s in flipped]
        + [
            pltpu.VMEM((side, width), bf16),
            pltpu.VMEM((side, side), f32),
            pltpu.VMEM((side, side), bf16),
            pltpu.VMEM((side, side), bf16),
            pltpu.VMEM((side, side), bf16),
            pltpu.SemaphoreType.DMA((5,)),
            pltpu.SemaphoreType.DMA((GROUP,)),
            pltpu.SemaphoreType.DMA((GROUP,)),
            pltpu.SemaphoreType.DMA((5,)),
            pltpu.SemaphoreType.DMA((10,)),
        ]
        + [pltpu.VMEM(term.shape, term.dtype) for term in (*grads, *moments)],
        compiler_params=pltpu.CompilerParams(
            collective_id=1, has_side_effects=True, vmem_limit_bytes=63 * 2**20
        ),
        name="muon",
    )(*grads, *moments)


def finish_kernel(factors, *refs):
    grads, updates, moments, weights = refs[0:5], refs[5:10], refs[10:15], refs[15:20]
    streams, (small, gains, first, second) = refs[20:22], refs[22:26]
    wide, news, masters = refs[26:31], refs[31:36], refs[36:41]
    stream_out = refs[41:43]
    gain_grad, first_new, second_new, master_gains, statistics = refs[43:48]
    here = lax.axis_index("fsdp")
    for number in range(5):
        grad = grads[number][0].astype(f32)
        wide[number][...] = grad
        news[number][...] = (
            momentum_decay * moments[number][...] + (1.0 - momentum_decay) * grad
        )
        masters[number][...] = weights[number][...].astype(f32) - factors[number] * updates[
            number
        ][...].astype(f32)
    for source, target in zip(streams, stream_out):
        target[...] = source[...]

    @pl.when(pl.program_id(0) == 0)
    def _():
        kinds, count = gains.shape
        width = small.shape[1]
        shift = lax.rem(width - here * count, width)
        grad = pltpu.roll(small[...], shift, 1)[0:kinds, 0:count]
        gain_grad[...] = grad
        gains_local = gains[...].astype(f32)
        first_next = first_decay * first[...] + (1.0 - first_decay) * grad
        second_next = second_decay * second[...] + (1.0 - second_decay) * grad * grad
        first_new[...] = first_next
        second_new[...] = second_next
        first_hat = first_next / (1.0 - first_decay**ADAM_STEP)
        second_hat = second_next / (1.0 - second_decay**ADAM_STEP)
        master_gains[...] = gains_local - adam_rate * (
            first_hat / (jnp.sqrt(second_hat) + adam_epsilon) + weight_decay * gains_local
        )
        statistics[...] = jnp.sqrt(small[4:5, 0:4] / (small[4:5, 4:5] * width))


def finish(grads, updates, moments, weights, streams, small, gains, first, second):
    steps = 2
    per = steps // 2
    shapes = tuple(moment.shape for moment in moments)
    factors = [max(1.0, s[0] * GROUP / s[1]) ** 0.5 * muon_rate for s in shapes]
    halves, wholes = [], []
    for number, (rows, cols) in enumerate(shapes):
        if number in (OUT, DOWN):
            halves.append(
                pl.BlockSpec((1, rows // steps, cols), lambda j: (j // per, j % per, 0))
            )
            wholes.append(pl.BlockSpec((rows // steps, cols), lambda j: (j, 0)))
        else:
            halves.append(
                pl.BlockSpec((1, rows, cols // steps), lambda j: (j // per, 0, j % per))
            )
            wholes.append(pl.BlockSpec((rows, cols // steps), lambda j: (0, j)))
    lines = [
        pl.BlockSpec((s.shape[0] // steps, s.shape[1]), lambda j: (j, 0)) for s in streams
    ]
    single = lambda shape: pl.BlockSpec(shape, lambda j: (0, 0))
    table = single(gains.shape)
    out = pl.pallas_call(
        lambda *refs: finish_kernel(factors, *refs),
        grid=(steps,),
        out_shape=[jax.ShapeDtypeStruct(s, f32) for s in shapes * 3]
        + [jax.ShapeDtypeStruct(s.shape, f32) for s in streams]
        + [jax.ShapeDtypeStruct(gains.shape, f32)] * 4
        + [jax.ShapeDtypeStruct((1, 4), f32)],
        in_specs=halves + wholes * 3 + lines + [single(small.shape)] + [table] * 3,
        out_specs=wholes * 3 + lines + [table] * 4 + [single((1, 4))],
        compiler_params=pltpu.CompilerParams(vmem_limit_bytes=63 * 2**20),
        name="finish",
    )(*grads, *updates, *moments, *weights, *streams, small, gains, first, second)
    return out[0:5], out[5:10], out[10:15], out[15:17], out[17:21], out[21]


def shards(
    tokens,
    cotangent,
    prefix,
    w_qkv,
    w_out,
    w_gate,
    w_up,
    w_down,
    gains,
    moment_qkv,
    moment_out,
    moment_gate,
    moment_up,
    moment_down,
    gain_first,
    gain_second,
):
    reps = lax.axis_size("rep")
    _, _, lane, lanes = place()
    teams = [[member * lanes + k for k in range(lanes)] for member in range(GROUP)]

    def joined(shard):
        if lanes == 1:
            return shard
        return lax.all_gather(shard, "fsdp", axis=0, tiled=True, axis_index_groups=teams)

    def summed(term):
        if lanes == 1:
            return term
        parts = lax.all_gather(term, "fsdp", axis_index_groups=teams)
        return jnp.sum(parts.astype(f32), axis=0).astype(term.dtype)

    def parted(block):
        if lanes == 1:
            return block
        size = block.shape[0] // lanes
        return lax.dynamic_slice_in_dim(block, lane * size, size, 0)

    half_dim = jnp.arange(HEAD_DIM // 2, dtype=f32)
    frequency = (rotary_base ** (-(half_dim * 2.0 / HEAD_DIM)))[None, :]
    weights = [joined(term) for term in (w_qkv, w_out, w_gate, w_up, w_down)]
    moments = [
        joined(term)
        for term in (moment_qkv, moment_out, moment_gate, moment_up, moment_down)
    ]
    output, d_tokens, small, halves = layer(
        prefix, tokens, cotangent, frequency, joined(gains).T, weights, reps
    )
    halves = [summed(term) for term in halves]
    small = summed(small)
    updates = muon(halves, moments)
    grads, news, masters, streams, gain_terms, statistics = finish(
        halves,
        updates,
        moments,
        weights,
        (output, d_tokens),
        small,
        gains.T,
        gain_first.T,
        gain_second.T,
    )
    gain_terms = [term.T for term in gain_terms]
    grads, news, masters = (
        [parted(term) for term in group] for group in (grads, news, masters)
    )
    return (
        *streams,
        *grads,
        gain_terms[0],
        *news,
        *masters,
        *gain_terms[1:],
        statistics.reshape(4),
    )


def solution(mesh):
    in_specs = (
        P(("rep", "fsdp"), None),
        P(("rep", "fsdp"), None),
        P(),
        P("fsdp", None),
        P("fsdp", None),
        P("fsdp", None),
        P("fsdp", None),
        P("fsdp", None),
        P("fsdp", None),
        P("fsdp", None),
        P("fsdp", None),
        P("fsdp", None),
        P("fsdp", None),
        P("fsdp", None),
        P("fsdp", None),
        P("fsdp", None),
    )
    out_specs = (
        P(("rep", "fsdp"), None),
        P(("rep", "fsdp"), None),
        P("fsdp", None),
        P("fsdp", None),
        P("fsdp", None),
        P("fsdp", None),
        P("fsdp", None),
        P("fsdp", None),
        P("fsdp", None),
        P("fsdp", None),
        P("fsdp", None),
        P("fsdp", None),
        P("fsdp", None),
        P("fsdp", None),
        P("fsdp", None),
        P("fsdp", None),
        P("fsdp", None),
        P("fsdp", None),
        P("fsdp", None),
        P("fsdp", None),
        P("fsdp", None),
        P(),
    )
    return jax.shard_map(shards, mesh=mesh, in_specs=in_specs, out_specs=out_specs, check_vma=False)
```

```python
import jax
import jax.numpy as jnp
from jax import lax
from jax.experimental import pallas as pl
from jax.experimental.pallas import tpu as pltpu
from jax.sharding import PartitionSpec as P

HEADS = 4
HEAD_DIM = 256
NS_STEPS = 5
ADAM_STEP = 10


norm_epsilon = 1e-06
soft_cap = 50.0
rotary_base = 10000.0
newton_first = 3.4445
newton_second = -4.775
newton_third = 2.0315
momentum_decay = 0.95
muon_rate = 1.0
first_decay = 0.9
second_decay = 0.95
adam_rate = 1.0
weight_decay = 0.1
adam_epsilon = 1e-08
frobenius_epsilon = 1e-07

GROUP = 8
MESH = pl.DeviceIdType.MESH
f32 = jnp.float32
bf16 = jnp.bfloat16


def dot(a, b):
    return lax.dot_general(a, b, (((1,), (0,)), ((), ())), preferred_element_type=f32)


def dot_nt(a, b):
    return lax.dot_general(a, b, (((1,), (1,)), ((), ())), preferred_element_type=f32)


def dot_tn(a, b):
    return lax.dot_general(a, b, (((0,), (0,)), ((), ())), preferred_element_type=f32)


def place():
    size = lax.axis_size("fsdp")
    lanes = size // GROUP
    here = lax.axis_index("fsdp")
    return lax.axis_index("rep"), here // lanes, lax.rem(here, lanes), lanes


QKV, OUT, GATE, UP, DOWN = range(5)
CORE, ACROSS, ALONG = 1, 2, 4
PAIRS = (
    ((GATE, 0), (UP, 0)),
    ((DOWN, 0), (GATE, 1)),
    ((UP, 1), (DOWN, 1)),
    ((OUT, 0), (OUT, 1)),
    ((QKV, 0), (QKV, 1)),
)
CHUNK = 128
TILE = 256


def split_shape(number, shape):
    rows, cols = shape
    return (rows // 2, cols) if number in (OUT, DOWN) else (rows, cols // 2)


def layer_names(rows, keys, width, shapes, reps):
    halves = [split_shape(number, shape) for number, shape in enumerate(shapes)]
    feats = HEADS * HEAD_DIM
    inner = shapes[GATE][1]
    spaces = {}
    for number, (height, cols) in enumerate(shapes):
        spaces[f"whole{number}"] = pltpu.VMEM((height * GROUP, cols), bf16)
    spaces.update(
        cosine=pltpu.VMEM((rows, HEAD_DIM // 2), f32),
        sine=pltpu.VMEM((rows, HEAD_DIM // 2), f32),
        gain_parts=pltpu.VMEM((GROUP, 8, 128), f32),
        gains=pltpu.VMEM((8, width), f32),
        normed=pltpu.VMEM((rows, width), bf16),
        one_t=pltpu.VMEM((width, rows), bf16),
        two_t=pltpu.VMEM((width, rows), bf16),
        proj=pltpu.VMEM((rows, feats + 2 * HEAD_DIM), bf16),
        key=pltpu.VMEM((keys, HEAD_DIM), bf16),
        value=pltpu.VMEM((keys, HEAD_DIM), bf16),
        key_t=pltpu.VMEM((HEAD_DIM, keys), bf16),
        value_t=pltpu.VMEM((HEAD_DIM, keys), bf16),
        att=pltpu.VMEM((rows, feats), bf16),
        att_t=pltpu.VMEM((feats, rows), bf16),
        inverse=pltpu.VMEM((8, rows), f32),
        branch=pltpu.VMEM((rows, width), f32),
        hidden=pltpu.VMEM((rows, width), f32),
        slope=pltpu.VMEM((rows, inner), bf16),
        bend=pltpu.VMEM((rows, inner), bf16),
        active=pltpu.VMEM((rows, inner), bf16),
        d_key=pltpu.VMEM((keys, HEAD_DIM), f32),
        d_value=pltpu.VMEM((keys, HEAD_DIM), f32),
        swap_in=pltpu.VMEM((rows, 2 * HEAD_DIM), bf16),
        squares=pltpu.VMEM((8, width), f32),
        d_gains=pltpu.VMEM((8, width), f32),
        small_parts=pltpu.VMEM((GROUP, 8, width), f32),
        small_reps=pltpu.VMEM((reps, 8, width), f32),
    )
    for number, half in enumerate(halves):
        spaces[f"stage{number}"] = pltpu.VMEM((2, 2, 2, 2) + half, bf16)
        spaces[f"chip{number}"] = pltpu.VMEM((2, 2, 2) + half, bf16)
        spaces[f"pair{number}"] = pltpu.VMEM((2, 2) + half, bf16)
        spaces[f"plane{number}"] = pltpu.VMEM((2,) + half, bf16)
        spaces[f"line{number}"] = pltpu.VMEM((2, 2) + half, bf16)
        spaces[f"total{number}"] = pltpu.VMEM((2,) + half, bf16)
    dma = pltpu.SemaphoreType.DMA
    spaces.update(
        own_sem=dma((5,)),
        result_sem=dma((5,)),
        weight_send=dma((5, 11)),
        weight_recv=dma((5, 11)),
        gain_send=dma((GROUP,)),
        gain_recv=dma((GROUP,)),
        key_send=dma((2,)),
        key_recv=dma((2,)),
        swap_send=dma((1,)),
        swap_recv=dma((1,)),
        chip_send=dma((5, 2)),
        chip_recv=dma((5, 2)),
        pair_send=dma((5, 2)),
        pair_recv=dma((5, 2)),
        plane_send=dma((5, 2)),
        plane_recv=dma((5, 2)),
        line_send=dma((5, 2)),
        line_recv=dma((5, 2, 2)),
        total_send=dma((5, 2)),
        total_recv=dma((5, 2)),
        small_send=dma((GROUP,)),
        small_recv=dma((GROUP,)),
        reps_send=dma((reps,)),
        reps_recv=dma((reps,)),
    )
    return spaces


class Refs:
    def __init__(self, names, refs):
        self.__dict__.update(zip(names, refs))


def column_sum(x):
    return jnp.sum(x, axis=0, keepdims=True)


def row_mean(x):
    return jnp.mean(x, axis=-1, keepdims=True)


def layer_kernel(names, shapes, *refs):
    v = Refs(names, refs)
    rep, me, lane, lanes = place()
    reps = lax.axis_size("rep")
    here = lax.axis_index("fsdp")
    core, across, along = me % 2, (me // 2) % 2, me // 4
    rows, width = v.tokens.shape
    parity = here % 2
    weights = [v.w_qkv, v.w_out, v.w_gate, v.w_up, v.w_down]
    named = lambda name: [getattr(v, f"{name}{number}") for number in range(5)]
    whole, stage, chip, pair = named("whole"), named("stage"), named("chip"), named("pair")
    plane, line, total, result = named("plane"), named("line"), named("total"), named("grad")

    def device(member):
        return (rep, member * lanes + lane)

    def remote(src, dst, send, recv, where):
        return pltpu.make_async_remote_copy(
            src_ref=src,
            dst_ref=dst,
            send_sem=send,
            recv_sem=recv,
            device_id=where,
            device_id_type=MESH,
        )

    barrier = pltpu.get_barrier_semaphore()
    greeted = [device(me ^ step) for step in range(1, GROUP)]
    greeted += [(lax.rem(rep + step, reps), here) for step in range(1, reps)]
    if lanes > 1:
        greeted.append((rep, here ^ 1))
    for where in greeted:
        pl.semaphore_signal(barrier, inc=1, device_id=where, device_id_type=MESH)
    pl.semaphore_wait(barrier, len(greeted))

    odd = rep % 2

    def parts(number):
        rows_or_cols, tile = shapes[number][1], 128
        if number in (OUT, DOWN):
            rows_or_cols, tile = shapes[number][0], 16
        outer = (rows_or_cols // tile + 1) // 3 * tile
        return outer, rows_or_cols - 2 * outer, tile

    def window(number, member, start, size, tile):
        height = shapes[number][0]
        base = pl.multiple_of(member * height, 16)
        if number in (OUT, DOWN):
            return whole[number].at[pl.ds(pl.multiple_of(base + start, 16), size), :]
        return whole[number].at[pl.ds(base, height), pl.ds(pl.multiple_of(start, 128), size)]

    def slot(number, member):
        height = shapes[number][0]
        return whole[number].at[pl.ds(pl.multiple_of(member * height, 16), height), :]

    def outer_part(number, member):
        outer, middle, tile = parts(number)
        return window(number, member, odd * (outer + middle), outer, tile)

    def middle_part(number, member):
        outer, middle, tile = parts(number)
        return window(number, member, outer, middle, tile)

    def own_parts(number):
        outer, middle, tile = parts(number)
        start = pl.multiple_of(odd * outer, tile)
        if number in (OUT, DOWN):
            return weights[number].at[pl.ds(start, outer + middle), :]
        return weights[number].at[:, pl.ds(start, outer + middle)]

    def both_parts(number, member):
        outer, middle, tile = parts(number)
        return window(number, member, odd * outer, outer + middle, tile)

    def weight_copy(number, kind):
        beside, ahead = me ^ ACROSS, me ^ ALONG
        corner = beside ^ ALONG
        if kind == 0:
            src, dst, where = weights[number], slot(number, me), device(me ^ CORE)
        elif kind < 3:
            src, dst = own_parts(number), both_parts(number, me)
            where = device((beside, ahead)[kind - 1])
        elif kind < 5:
            src = outer_part(number, beside) if kind == 3 else middle_part(number, ahead)
            dst, where = src, device((ahead, beside)[kind - 3])
        elif kind < 8:
            src = outer_part(number, (beside, ahead, corner)[kind - 5])
            dst, where = src, (rep + 1 - 2 * odd, here)
        else:
            src = slot(number, (beside, ahead, corner)[kind - 8])
            dst, where = src, device(me ^ CORE)
        return remote(
            src, dst, v.weight_send.at[number, kind], v.weight_recv.at[number, kind], where
        )

    def own_copy(number):
        return pltpu.make_async_copy(weights[number], slot(number, me), v.own_sem.at[number])

    def weight_begin(number):
        for kind in (1, 2, 0):
            weight_copy(number, kind).start()
        own_copy(number).start()

    def weight_forward(number):
        weight_copy(number, 1).wait_recv()
        weight_copy(number, 3).start()
        weight_copy(number, 5).start()
        weight_copy(number, 2).wait_recv()
        weight_copy(number, 4).start()
        weight_copy(number, 6).start()

    def weight_corner(number):
        weight_copy(number, 3).wait_recv()
        weight_copy(number, 7).start()

    def weight_cross(number):
        weight_copy(number, 5).wait_recv()
        weight_copy(number, 8).start()
        weight_copy(number, 6).wait_recv()
        weight_copy(number, 9).start()
        weight_copy(number, 4).wait_recv()
        weight_copy(number, 7).wait_recv()
        weight_copy(number, 10).start()

    def weight_ready(number):
        own_copy(number).wait()
        for kind in (0, 8, 9, 10):
            weight_copy(number, kind).wait_recv()

    weight_begin(QKV)

    def gain_copy(step):
        return remote(
            v.gain_parts.at[me],
            v.gain_parts.at[me],
            v.gain_send.at[step],
            v.gain_recv.at[step],
            device(me ^ step),
        )

    gain_count, gain_rows = v.gain_block.shape
    v.gain_parts[me] = jnp.zeros_like(v.gain_parts[me])
    v.gain_parts[me, 0:gain_count, 0:gain_rows] = v.gain_block[...].astype(f32)
    for step in range(1, GROUP):
        gain_copy(step).start()
    weight_begin(OUT)
    weight_begin(GATE)
    v.squares[...] = jnp.zeros_like(v.squares)
    v.d_gains[...] = jnp.zeros_like(v.d_gains)
    v.d_key[...] = jnp.zeros_like(v.d_key)
    v.d_value[...] = jnp.zeros_like(v.d_value)
    spot = lax.broadcasted_iota(jnp.int32, (rows, HEAD_DIM // 2), 0) + parity * rows
    angles = spot.astype(f32) * v.frequency[...]
    v.cosine[...] = jnp.cos(angles)
    v.sine[...] = jnp.sin(angles)
    for step in range(1, GROUP):
        gain_copy(step).wait_recv()
    for member in range(GROUP):
        v.gains[:, member * gain_rows : (member + 1) * gain_rows] = v.gain_parts[
            member, :, 0:gain_rows
        ]

    prefix = v.prefix[(rep * lax.axis_size("fsdp") + here) // 2]

    def valid_rows(start, count):
        spot = lax.broadcasted_iota(jnp.int32, (count, 1), 0) + (parity * rows + start)
        return jnp.where(spot >= prefix, 1.0, 0.0)

    def by_rows(body):
        @pl.loop(0, rows // CHUNK)
        def _(k):
            start = pl.multiple_of(k * CHUNK, CHUNK)
            body(pl.ds(start, CHUNK), start)

    def by_columns(count, body):
        @pl.loop(0, count // TILE)
        def _(k):
            body(pl.ds(pl.multiple_of(k * TILE, TILE), TILE), k)

    def inverse_root(x):
        return lax.rsqrt(row_mean(x * x) + norm_epsilon)

    def norm_back(x, scale, upstream, gain, row):
        v.d_gains[row : row + 1, :] += column_sum(upstream * x * scale)
        spread = upstream * gain
        return scale * spread - x * (scale * scale * scale * row_mean(x * spread))

    gain_row = lambda k: v.gains[k : k + 1, :]

    def first_norm(here_rows, start):
        x = v.tokens[here_rows, :].astype(f32)
        normed = x * inverse_root(x) * gain_row(0)
        v.normed[here_rows, :] = normed.astype(bf16)
        v.one_t[:, here_rows] = normed.T.astype(bf16)
        v.squares[0:1, :] += column_sum(valid_rows(start, CHUNK) * (x * x))

    by_rows(first_norm)
    weight_forward(QKV)
    weight_corner(QKV)
    weight_forward(OUT)
    weight_begin(UP)
    weight_cross(QKV)
    weight_corner(OUT)
    weight_ready(QKV)

    feats = HEADS * HEAD_DIM
    half_dim = HEAD_DIM // 2
    own_rows = pl.ds(pl.multiple_of(parity * rows, rows), rows)
    other_rows = pl.ds(pl.multiple_of((1 - parity) * rows, rows), rows)

    def rotate(x, sign):
        first, second = x[:, :half_dim], x[:, half_dim:]
        cosine, sine = v.cosine[...], v.sine[...] * sign
        return first * cosine - second * sine, second * cosine + first * sine

    def key_copy(number):
        ref = (v.key, v.value)[number]
        return remote(
            ref.at[own_rows, :],
            ref.at[own_rows, :],
            v.key_send.at[number],
            v.key_recv.at[number],
            (rep, here ^ 1),
        )

    key_part = dot(v.normed[...], whole[QKV][:, feats : feats + HEAD_DIM])
    first, second = rotate(key_part, 1.0)
    v.key[own_rows, :half_dim] = first.astype(bf16)
    v.key[own_rows, half_dim:] = second.astype(bf16)
    key_copy(0).start()
    v.value[own_rows, :] = dot(v.normed[...], whole[QKV][:, feats + HEAD_DIM :]).astype(bf16)
    key_copy(1).start()

    @pl.loop(0, HEADS)
    def _(head):
        start = pl.multiple_of(head * HEAD_DIM, HEAD_DIM)
        part = dot(v.normed[...], whole[QKV][:, pl.ds(start, HEAD_DIM)])
        first, second = rotate(part, 1.0)
        v.proj[:, pl.ds(start, half_dim)] = first.astype(bf16)
        v.proj[:, pl.ds(start + half_dim, half_dim)] = second.astype(bf16)

    weight_forward(GATE)
    weight_begin(DOWN)
    for number in range(2):
        key_copy(number).wait_recv()
    v.key_t[...] = v.key[...].astype(f32).T.astype(bf16)
    v.value_t[...] = v.value[...].astype(f32).T.astype(bf16)

    keys = v.key.shape[0]
    bend_scale = HEAD_DIM ** (-0.5) / soft_cap

    def head_columns(head):
        return pl.ds(pl.multiple_of(head * HEAD_DIM, HEAD_DIM), HEAD_DIM)

    def scores(head, start):
        here_rows = pl.ds(start, TILE)
        query = v.proj[here_rows, head_columns(head)]
        bent = jnp.tanh(dot_nt(v.key[...], query) * bend_scale)
        spot = lax.broadcasted_iota(jnp.int32, (1, TILE), 1) + (parity * rows + start)
        last = jnp.maximum(spot, prefix - 1)
        allowed = lax.broadcasted_iota(jnp.int32, (keys, TILE), 0) <= last
        return bent, jnp.where(allowed, jnp.exp(soft_cap * bent), 0.0), query

    blocks = rows // TILE

    def attend(begin, end):
        @pl.loop(begin, end)
        def _(k):
            head = k // blocks
            start = pl.multiple_of(lax.rem(k, blocks) * TILE, TILE)
            cols, here_rows = head_columns(head), pl.ds(start, TILE)
            _, power, _ = scores(head, start)
            inverse = 1.0 / column_sum(power)
            v.inverse[pl.ds(head, 1), here_rows] = inverse
            mixed = dot(v.value_t[...], (power * inverse).astype(bf16))
            v.att_t[cols, here_rows] = mixed.astype(bf16)
            v.att[here_rows, cols] = mixed.T.astype(bf16)

    weight_cross(OUT)
    weight_corner(GATE)
    weight_forward(UP)
    attend(0, 2)
    weight_cross(GATE)
    attend(2, 4)
    weight_corner(UP)
    weight_forward(DOWN)
    attend(4, 6)
    weight_cross(UP)
    weight_corner(DOWN)
    attend(6, 8)
    weight_ready(OUT)

    v.branch[...] = dot(v.att[...], whole[OUT][...])

    def second_norm(here_rows, start):
        x = v.branch[here_rows, :]
        first_out = x * inverse_root(x) * gain_row(1)
        hidden = v.tokens[here_rows, :].astype(f32) + first_out
        v.hidden[here_rows, :] = hidden
        normed = hidden * inverse_root(hidden) * gain_row(2)
        v.normed[here_rows, :] = normed.astype(bf16)
        v.two_t[:, here_rows] = normed.T.astype(bf16)
        v.squares[1:2, :] += column_sum(valid_rows(start, CHUNK) * (first_out * first_out))

    by_rows(second_norm)
    weight_ready(GATE)
    weight_ready(UP)
    inner = shapes[GATE][1]

    def feed(cols, k):
        gate = dot(v.normed[...], whole[GATE][:, cols])
        upward = dot(v.normed[...], whole[UP][:, cols])
        square = gate * gate
        bent = jnp.tanh(0.7978845608028654 * (gate + 0.044715 * gate * square))
        open_half = 0.5 * (1.0 + bent)
        smooth = gate * open_half
        steep = open_half + gate * (1.0 - bent * bent) * (
            0.3989422804014327 * (1.0 + 3.0 * 0.044715 * square)
        )
        v.active[:, cols] = (smooth * upward).astype(bf16)
        v.bend[:, cols] = smooth.astype(bf16)
        v.slope[:, cols] = (steep * upward).astype(bf16)

    by_columns(inner, feed)
    weight_cross(DOWN)
    weight_ready(DOWN)

    v.d_tokens[...] = dot(v.active[...], whole[DOWN][...])

    def last_norm(here_rows, start):
        x = v.d_tokens[here_rows, :]
        scale = inverse_root(x)
        second_out = x * scale * gain_row(3)
        final = v.hidden[here_rows, :] + second_out
        v.output[here_rows, :] = final
        valid = valid_rows(start, CHUNK)
        v.squares[2:3, :] += column_sum(valid * (second_out * second_out))
        v.squares[3:4, :] += column_sum(valid * (final * final))
        upstream = v.cotangent[here_rows, :].astype(f32)
        v.normed[here_rows, :] = norm_back(x, scale, upstream, gain_row(3), 3).astype(bf16)

    by_rows(last_norm)

    def first_across(number, half):
        return any(one == (number, half) for one, _ in PAIRS)

    def chip_copy(number, half):
        return remote(
            stage[number].at[half, :, :, 1 - core],
            chip[number].at[half],
            v.chip_send.at[number, half],
            v.chip_recv.at[number, half],
            device(me ^ CORE),
        )

    def pair_copy(number, half):
        if first_across(number, half):
            src, where = chip[number].at[half, :, 1 - across], me ^ ACROSS
        else:
            src, where = chip[number].at[half, 1 - along], me ^ ALONG
        return remote(
            src,
            pair[number].at[half],
            v.pair_send.at[number, half],
            v.pair_recv.at[number, half],
            device(where),
        )

    def plane_copy(number, half):
        if first_across(number, half):
            src, where = pair[number].at[half, 1 - along], me ^ ALONG
        else:
            src, where = pair[number].at[half, 1 - across], me ^ ACROSS
        return remote(
            src,
            plane[number].at[half],
            v.plane_send.at[number, half],
            v.plane_recv.at[number, half],
            device(where),
        )

    def added(one, two):
        return one + two

    def chip_begin(number, half):
        chip_copy(number, half).start()

    def chip_end(number, half):
        chip_copy(number, half).wait_recv()

        @pl.loop(0, 4)
        def _(k):
            one, two = k // 2, k % 2
            chip[number][half, one, two] = added(
                chip[number][half, one, two], stage[number][half, one, two, core]
            )

        pair_copy(number, half).start()

    def pair_end(number, half):
        pair_copy(number, half).wait_recv()

        @pl.loop(0, 2)
        def _(k):
            if first_across(number, half):
                mine = chip[number][half, k, across]
            else:
                mine = chip[number][half, along, k]
            pair[number][half, k] = added(pair[number][half, k], mine)

        plane_copy(number, half).start()

    def plane_end(number, half):
        plane_copy(number, half).wait_recv()
        kept = along if first_across(number, half) else across
        plane[number][half] = added(plane[number][half], pair[number][half, kept])

        @pl.when(at_end)
        def _():
            line_send(number, half)

    order = [half for both in PAIRS for half in both]

    on_left = rep < reps // 2
    inward = jnp.where(on_left, 1, -1)
    at_end = (rep == 0) | (rep == reps - 1)
    at_middle = (rep == reps // 2 - 1) | (rep == reps // 2)

    def line_copy(number, half, way):
        return remote(
            plane[number].at[half],
            line[number].at[half, way],
            v.line_send.at[number, half],
            v.line_recv.at[number, half, way],
            (rep + inward, here),
        )

    def total_copy(number, half):
        return remote(
            total[number].at[half],
            total[number].at[half],
            v.total_send.at[number, half],
            v.total_recv.at[number, half],
            (rep - inward, here),
        )

    def line_send(number, half):
        @pl.when(jnp.logical_not(at_middle))
        def _():
            line_copy(number, half, 0).start()

        @pl.when(at_middle)
        def _():
            line_copy(number, half, 1).start()

    def line_begin(number, half):
        @pl.when(jnp.logical_not(at_end))
        def _():
            line_copy(number, half, 0).wait_recv()
            plane[number][half] = added(plane[number][half], line[number][half, 0])
            line_send(number, half)

    def line_end(number, half):
        @pl.when(at_middle)
        def _():
            line_copy(number, half, 1).wait_recv()
            total[number][half] = added(plane[number][half], line[number][half, 1])

            @pl.when(jnp.logical_not(at_end))
            def _():
                total_copy(number, half).start()

    def total_end(number, half):
        @pl.when(jnp.logical_not(at_middle))
        def _():
            total_copy(number, half).wait_recv()

            @pl.when(jnp.logical_not(at_end))
            def _():
                total_copy(number, half).start()

    def for_pair(action, index):
        for number, half in PAIRS[index]:
            action(number, half)

    def keep_columns(number, col_half, col, found):
        height = shapes[number][0]
        for member in range(GROUP):
            stage[number][
                col_half, member // 4, (member // 2) % 2, member % 2, :, pl.ds(col, TILE)
            ] = found[member * height : (member + 1) * height].astype(bf16)

    down_rows = shapes[DOWN][0]
    halved = inner // 2 // TILE

    def feed_back(side, begin, end):
        @pl.loop(begin, end)
        def _(k):
            col = pl.multiple_of(k * TILE, TILE)
            start = pl.multiple_of(side * (inner // 2) + k * TILE, TILE)
            cols = pl.ds(start, TILE)
            d_active = dot_nt(v.normed[...], whole[DOWN][cols, :])
            d_gate = (d_active * v.slope[:, cols].astype(f32)).astype(bf16)
            d_upward = (d_active * v.bend[:, cols].astype(f32)).astype(bf16)
            v.slope[:, cols] = d_gate
            v.bend[:, cols] = d_upward
            keep_columns(GATE, side, col, dot(v.two_t[...], d_gate))
            keep_columns(UP, side, col, dot(v.two_t[...], d_upward))
            found = dot_tn(v.active[:, cols], v.normed[...]).astype(bf16)
            per = TILE // down_rows
            for part in range(per):
                member = (side * halved + k) * per + part
                y, x, c = member // 4, (member // 2) % 2, member % 2
                base = part * down_rows
                stage[DOWN][0, y, x, c] = found[base : base + down_rows // 2]
                stage[DOWN][1, y, x, c] = found[base + down_rows // 2 : base + down_rows]

    feed_back(0, 0, halved)
    for_pair(chip_begin, 0)
    feed_back(1, 0, halved // 2)
    for_pair(chip_end, 0)
    feed_back(1, halved // 2, halved)
    for_pair(chip_begin, 1)
    for_pair(chip_begin, 2)
    v.d_tokens[...] = dot_nt(v.slope[...], whole[GATE][...])
    for_pair(chip_end, 1)
    v.d_tokens[...] += dot_nt(v.bend[...], whole[UP][...])
    for_pair(chip_end, 2)

    def middle_norms(here_rows, start):
        x = v.hidden[here_rows, :]
        flow = norm_back(x, inverse_root(x), v.d_tokens[here_rows, :], gain_row(2), 2)
        d_hidden = v.cotangent[here_rows, :].astype(f32) + flow
        v.d_tokens[here_rows, :] = d_hidden
        x = v.branch[here_rows, :]
        flow = norm_back(x, inverse_root(x), d_hidden, gain_row(1), 1)
        v.normed[here_rows, :] = flow.astype(bf16)

    by_rows(middle_norms)
    for_pair(pair_end, 0)
    out_rows = shapes[OUT][0]
    v.att[...] = dot_nt(v.normed[...], whole[OUT][...]).astype(bf16)

    @pl.loop(0, GROUP // 2)
    def _(k):
        start = pl.multiple_of(k * 2 * out_rows, 2 * out_rows)
        found = dot(v.att_t[pl.ds(start, 2 * out_rows), :], v.normed[...]).astype(bf16)
        for part in range(4):
            stage[OUT][part % 2, k // 2, k % 2, part // 2] = found[
                part * (out_rows // 2) : (part + 1) * (out_rows // 2)
            ]


    for_pair(chip_begin, 3)
    for_pair(pair_end, 1)
    for_pair(plane_end, 0)
    def attend_back(begin, end):
        @pl.loop(begin, end)
        def _(k):
            head = k // blocks
            start = pl.multiple_of(lax.rem(k, blocks) * TILE, TILE)
            here_rows = pl.ds(start, TILE)
            bent, power, query = scores(head, start)
            soft = power * v.inverse[pl.ds(head, 1), here_rows]
            flow = v.att[here_rows, head_columns(head)]
            d_soft = dot_nt(v.value[...], flow)
            v.d_value[...] += dot(soft.astype(bf16), flow)
            level = column_sum(d_soft * soft)
            d_raw = soft * (d_soft - level) * ((1.0 - bent * bent) * HEAD_DIM ** (-0.5))
            d_raw = d_raw.astype(bf16)
            v.d_key[...] += dot(d_raw, query)
            d_query = dot(v.key_t[...], d_raw).T
            first, second = d_query[:, :half_dim], d_query[:, half_dim:]
            cosine, sine = v.cosine[here_rows, :], v.sine[here_rows, :]
            base = pl.multiple_of(head * HEAD_DIM, HEAD_DIM)
            v.proj[here_rows, pl.ds(base, half_dim)] = (first * cosine + second * sine).astype(
                bf16
            )
            v.proj[here_rows, pl.ds(base + half_dim, half_dim)] = (
                second * cosine - first * sine
            ).astype(bf16)

    swap = remote(
        v.att.at[:, 0 : 2 * HEAD_DIM],
        v.swap_in,
        v.swap_send.at[0],
        v.swap_recv.at[0],
        (rep, here ^ 1),
    )

    attend_back(0 * blocks, 1 * blocks)
    attend_back(1 * blocks, 2 * blocks)
    for_pair(pair_end, 2)
    attend_back(2 * blocks, 3 * blocks)
    for_pair(line_begin, 0)
    for_pair(plane_end, 1)
    attend_back(3 * blocks, 4 * blocks)
    v.att[:, 0:HEAD_DIM] = v.d_key[other_rows, :].astype(bf16)
    v.att[:, HEAD_DIM : 2 * HEAD_DIM] = v.d_value[other_rows, :].astype(bf16)
    swap.start()
    for_pair(chip_end, 3)

    qkv_half = split_shape(QKV, shapes[QKV])[1] // TILE

    def projection_grad(tile):
        found = dot(v.one_t[...], v.proj[:, tile * TILE : (tile + 1) * TILE])
        keep_columns(QKV, tile // qkv_half, (tile % qkv_half) * TILE, found)

    for tile in range(qkv_half):
        projection_grad(tile)
    chip_begin(QKV, 0)
    swap.wait_recv()
    d_key = v.d_key[own_rows, :] + v.swap_in[:, 0:HEAD_DIM].astype(f32)
    first, second = rotate(d_key, -1.0)
    v.proj[:, feats : feats + half_dim] = first.astype(bf16)
    v.proj[:, feats + half_dim : feats + HEAD_DIM] = second.astype(bf16)
    v.proj[:, feats + HEAD_DIM :] = (
        v.d_value[own_rows, :] + v.swap_in[:, HEAD_DIM:].astype(f32)
    ).astype(bf16)
    for tile in range(qkv_half, 2 * qkv_half):
        projection_grad(tile)
    chip_begin(QKV, 1)
    for_pair(chip_end, 4)
    for_pair(line_begin, 1)
    for_pair(plane_end, 2)
    for_pair(line_end, 0)
    v.branch[...] = dot_nt(v.proj[...], whole[QKV][...])
    for_pair(pair_end, 3)

    def first_norm_back(here_rows, start):
        x = v.tokens[here_rows, :].astype(f32)
        flow = norm_back(x, inverse_root(x), v.branch[here_rows, :], gain_row(0), 0)
        v.d_tokens[here_rows, :] += flow

    by_rows(first_norm_back)

    def small_copy(step):
        return remote(
            v.small_parts.at[me],
            v.small_parts.at[me],
            v.small_send.at[step],
            v.small_recv.at[step],
            device(me ^ step),
        )

    def reps_copy(step):
        return remote(
            v.small_reps.at[rep],
            v.small_reps.at[rep],
            v.reps_send.at[step],
            v.reps_recv.at[step],
            (lax.rem(rep + step, reps), here),
        )

    spot = lax.broadcasted_iota(jnp.int32, (1, width), 1)
    numbers = jnp.where(spot == 4, column_sum(valid_rows(0, rows)), 0.0)
    for k in range(4):
        summed = jnp.sum(v.squares[k : k + 1, :], axis=1, keepdims=True)
        numbers = numbers + jnp.where(spot == k, summed, 0.0)
    v.d_gains[4:5, :] = numbers
    v.small_parts[me] = v.d_gains[...]
    for step in range(1, GROUP):
        small_copy(step).start()
    for_pair(line_end, 1)
    for_pair(total_end, 0)
    for_pair(line_begin, 2)
    for_pair(plane_end, 3)
    for_pair(pair_end, 4)
    for_pair(total_end, 1)
    for step in range(1, GROUP):
        small_copy(step).wait_recv()
    v.small_reps[rep] = jnp.sum(v.small_parts[...], axis=0)
    for step in range(1, reps):
        reps_copy(step).start()
    for_pair(line_end, 2)
    for_pair(line_begin, 3)
    for_pair(plane_end, 4)
    for_pair(total_end, 2)
    for_pair(line_end, 3)
    for_pair(line_begin, 4)
    for_pair(total_end, 3)
    for_pair(line_end, 4)
    for_pair(total_end, 4)
    for step in range(1, reps):
        reps_copy(step).wait_recv()
    v.small[...] = jnp.sum(v.small_reps[...], axis=0)
    results = [
        pltpu.make_async_copy(total[number], result[number], v.result_sem.at[number])
        for number in range(5)
    ]
    for copy in results:
        copy.start()

    for number in range(5):
        for kind in range(11):
            weight_copy(number, kind).wait_send()
    for number in range(2):
        key_copy(number).wait_send()
    swap.wait_send()
    for step in range(1, GROUP):
        gain_copy(step).wait_send()
        small_copy(step).wait_send()
    for step in range(1, reps):
        reps_copy(step).wait_send()
    for number, half in order:
        chip_copy(number, half).wait_send()
        pair_copy(number, half).wait_send()
        plane_copy(number, half).wait_send()
        line_copy(number, half, 0).wait_send()

        @pl.when(jnp.logical_not(at_end))
        def _():
            total_copy(number, half).wait_send()

    for copy in results:
        copy.wait()


def layer(prefix, tokens, cotangent, frequency, gain_block, weights, reps):
    shapes = tuple(w.shape for w in weights)
    rows, width = tokens.shape
    spaces = layer_names(rows, 2 * rows, width, shapes, reps)
    halves = [split_shape(number, shape) for number, shape in enumerate(shapes)]
    inputs = ["prefix", "tokens", "cotangent", "frequency", "gain_block"]
    inputs += ["w_qkv", "w_out", "w_gate", "w_up", "w_down"]
    outputs = ["output", "d_tokens", "small"] + [f"grad{number}" for number in range(5)]
    vmem = pl.BlockSpec(memory_space=pltpu.VMEM)
    names = inputs + outputs + list(spaces)
    out = pl.pallas_call(
        lambda *refs: layer_kernel(names, shapes, *refs),
        out_shape=[
            jax.ShapeDtypeStruct((rows, width), f32),
            jax.ShapeDtypeStruct((rows, width), f32),
            jax.ShapeDtypeStruct((8, width), f32),
        ]
        + [jax.ShapeDtypeStruct((2,) + half, bf16) for half in halves],
        in_specs=[pl.BlockSpec(memory_space=pltpu.SMEM)]
        + [vmem] * 4
        + [pl.BlockSpec(memory_space=pl.ANY)] * 5,
        out_specs=[vmem] * 3 + [pl.BlockSpec(memory_space=pl.ANY)] * 5,
        scratch_shapes=list(spaces.values()),
        compiler_params=pltpu.CompilerParams(
            collective_id=2, has_side_effects=True, vmem_limit_bytes=64 * 2**20
        ),
        name="layer",
    )(prefix, tokens, cotangent, frequency, gain_block, *weights)
    return out[0], out[1], out[2], out[3:]


OWNERS = (6, 7, 0, 2, 4)
FLIPPED = (False, True, False, False, True)


def gram_into(x_ref, gram):
    rows = gram.shape[0]
    starts = list(range(0, rows, 256))
    for j in starts:
        n = min(256, rows - j)
        gram[j:rows, j : j + n] = dot_nt(x_ref[j:rows, :], x_ref[j : j + n, :])
    for j in starts:
        n = min(256, rows - j)
        if j + n < rows:
            gram[j : j + n, j + n : rows] = gram[j + n : rows, j : j + n].T


def newton_step(x_ref, gram, mixer, high, low, first, refined):
    gram_into(x_ref, gram)
    rows = gram.shape[0]
    same = lax.broadcasted_iota(jnp.int32, (rows, rows), 0) == lax.broadcasted_iota(
        jnp.int32, (rows, rows), 1
    )
    whole = gram[...]
    scale = None
    if first is not None:
        trace = jnp.sum(jnp.where(same, whole, 0.0))
        scale = jnp.where(first, 1.0 / (jnp.sqrt(trace) + frobenius_epsilon), 1.0)
        whole = whole * (scale * scale)
        gram[...] = whole
    high[...] = whole.astype(bf16)
    squared = dot(high[...], high[...])
    if refined:
        low[...] = (gram[...] - high[...].astype(f32)).astype(bf16)
        squared = squared + dot(high[...], low[...]) + dot(low[...], high[...])
    mix = (
        jnp.where(same, newton_first, 0.0) + newton_second * gram[...] + newton_third * squared
    )
    if scale is not None:
        mix = mix * scale
    mixer[...] = mix.astype(bf16)
    x_ref[...] = dot(mixer[...], x_ref[...]).astype(bf16)


def muon_kernel(shapes, *refs):
    sources, results = refs[0:10], refs[10:15]
    outgoing, arrived = refs[15:20], refs[20:25]
    x_all, gram, mixer, high, low = refs[25:30]
    gather_send, gather_recv, scatter_send, scatter_recv, load_sem = refs[30:35]
    loaded = refs[35:45]
    grads, moments = loaded[0:5], loaded[5:10]
    loads = [
        pltpu.make_async_copy(source, target, load_sem.at[k])
        for k, (source, target) in enumerate(zip(sources, loaded))
    ]
    for load in loads:
        load.start()
    rep, me, lane, lanes = place()

    def device(member):
        return (rep, member * lanes + lane)

    owner_here = me == OWNERS[0]
    for owner in OWNERS[1:]:
        owner_here = owner_here | (me == owner)

    @pl.when(owner_here)
    def _():
        x_all[...] = jnp.zeros_like(x_all)

    barrier = pltpu.get_barrier_semaphore()
    for step in range(1, GROUP):
        pl.semaphore_signal(
            barrier, inc=1, device_id=device(me ^ step), device_id_type=MESH
        )

    def block(number, member):
        rows, cols = shapes[number]
        if FLIPPED[number]:
            return x_all.at[:, pl.ds(member * rows, rows)]
        return x_all.at[pl.ds(member * rows, rows), pl.ds(0, cols)]

    def gather_copy(number, member, sender):
        rows, _ = shapes[number]
        if FLIPPED[number]:
            start = pl.multiple_of(sender * rows, rows)
            target = x_all.at[:, pl.ds(start, rows)]
        else:
            start = pl.multiple_of(sender * rows, 16)
            target = x_all.at[pl.ds(start, rows), pl.ds(0, shapes[number][1])]
        return pltpu.make_async_remote_copy(
            src_ref=outgoing[number],
            dst_ref=target,
            send_sem=gather_send.at[number],
            recv_sem=gather_recv.at[sender],
            device_id=device(member),
            device_id_type=MESH,
        )

    pl.semaphore_wait(barrier, GROUP - 1)
    for number in (2, 3, 4, 0, 1):
        loads[number].wait()
        loads[5 + number].wait()
        grad = jnp.concatenate(
            [grads[number][0], grads[number][1]], axis=0 if number in (OUT, DOWN) else 1
        ).astype(f32)
        new = momentum_decay * moments[number][...] + (1.0 - momentum_decay) * grad
        nesterov = (1.0 - momentum_decay) * grad + momentum_decay * new
        if FLIPPED[number]:
            nesterov = nesterov.T
        outgoing[number][...] = nesterov.astype(bf16)

        @pl.when(me != OWNERS[number])
        def _():
            gather_copy(number, OWNERS[number], me).start()

    for number in range(5):
        owner = OWNERS[number]

        @pl.when(me == owner)
        def _():
            rows, cols = shapes[number]
            if FLIPPED[number]:
                x_all[:, owner * rows : (owner + 1) * rows] = outgoing[number][...]
            else:
                x_all[owner * rows : (owner + 1) * rows, 0:cols] = outgoing[number][...]
            for step in range(1, GROUP):
                gather_copy(number, owner, owner ^ step).wait_recv()

    @pl.when(owner_here)
    def _():
        @pl.loop(0, NS_STEPS - 2)
        def _(k):
            newton_step(x_all, gram, mixer, high, low, k == 0, False)

        @pl.loop(0, 2)
        def _(k):
            newton_step(x_all, gram, mixer, high, low, None, True)

    def scatter_copy(number, member):
        rows, cols = shapes[number]
        return pltpu.make_async_remote_copy(
            src_ref=block(number, member),
            dst_ref=arrived[number],
            send_sem=scatter_send.at[member],
            recv_sem=scatter_recv.at[number],
            device_id=device(member),
            device_id_type=MESH,
        )

    for number in range(5):
        owner = OWNERS[number]

        @pl.when(me == owner)
        def _():
            for step in range(1, GROUP):
                scatter_copy(number, owner ^ step).start()
            arrived[number][...] = block(number, owner)[...]

    for number in range(5):
        owner = OWNERS[number]

        @pl.when(me != owner)
        def _():
            scatter_copy(number, owner).wait_recv()

        update = arrived[number][...]
        if FLIPPED[number]:
            update = update.astype(f32).T.astype(bf16)
        results[number][...] = update

    for number in range(5):
        owner = OWNERS[number]

        @pl.when(me == owner)
        def _():
            for step in range(1, GROUP):
                scatter_copy(number, owner ^ step).wait_send()

        @pl.when(me != owner)
        def _():
            gather_copy(number, owner, me).wait_send()


def muon(grads, moments):
    shapes = tuple(moment.shape for moment in moments)
    flipped = [s[::-1] if flip else s for s, flip in zip(shapes, FLIPPED)]
    side = shapes[0][0] * GROUP
    width = max(s[0] * GROUP if flip else s[1] for s, flip in zip(shapes, FLIPPED))
    vmem = pl.BlockSpec(memory_space=pltpu.VMEM)
    return pl.pallas_call(
        lambda *refs: muon_kernel(shapes, *refs),
        out_shape=[jax.ShapeDtypeStruct(s, bf16) for s in shapes],
        in_specs=[pl.BlockSpec(memory_space=pl.ANY)] * 10,
        out_specs=[vmem] * 5,
        scratch_shapes=[pltpu.VMEM(s, bf16) for s in flipped]
        + [pltpu.VMEM(s, bf16) for s in flipped]
        + [
            pltpu.VMEM((side, width), bf16),
            pltpu.VMEM((side, side), f32),
            pltpu.VMEM((side, side), bf16),
            pltpu.VMEM((side, side), bf16),
            pltpu.VMEM((side, side), bf16),
            pltpu.SemaphoreType.DMA((5,)),
            pltpu.SemaphoreType.DMA((GROUP,)),
            pltpu.SemaphoreType.DMA((GROUP,)),
            pltpu.SemaphoreType.DMA((5,)),
            pltpu.SemaphoreType.DMA((10,)),
        ]
        + [pltpu.VMEM(term.shape, term.dtype) for term in (*grads, *moments)],
        compiler_params=pltpu.CompilerParams(
            collective_id=1, has_side_effects=True, vmem_limit_bytes=63 * 2**20
        ),
        name="muon",
    )(*grads, *moments)


def finish_kernel(factors, *refs):
    grads, updates, moments, weights = refs[0:5], refs[5:10], refs[10:15], refs[15:20]
    streams, (small, gains, first, second) = refs[20:22], refs[22:26]
    wide, news, masters = refs[26:31], refs[31:36], refs[36:41]
    stream_out = refs[41:43]
    gain_grad, first_new, second_new, master_gains, statistics = refs[43:48]
    here = lax.axis_index("fsdp")
    for number in range(5):
        grad = grads[number][0].astype(f32)
        wide[number][...] = grad
        news[number][...] = (
            momentum_decay * moments[number][...] + (1.0 - momentum_decay) * grad
        )
        masters[number][...] = weights[number][...].astype(f32) - factors[number] * updates[
            number
        ][...].astype(f32)
    for source, target in zip(streams, stream_out):
        target[...] = source[...]

    @pl.when(pl.program_id(0) == 0)
    def _():
        kinds, count = gains.shape
        width = small.shape[1]
        shift = lax.rem(width - here * count, width)
        grad = pltpu.roll(small[...], shift, 1)[0:kinds, 0:count]
        gain_grad[...] = grad
        gains_local = gains[...].astype(f32)
        first_next = first_decay * first[...] + (1.0 - first_decay) * grad
        second_next = second_decay * second[...] + (1.0 - second_decay) * grad * grad
        first_new[...] = first_next
        second_new[...] = second_next
        first_hat = first_next / (1.0 - first_decay**ADAM_STEP)
        second_hat = second_next / (1.0 - second_decay**ADAM_STEP)
        master_gains[...] = gains_local - adam_rate * (
            first_hat / (jnp.sqrt(second_hat) + adam_epsilon) + weight_decay * gains_local
        )
        statistics[...] = jnp.sqrt(small[4:5, 0:4] / (small[4:5, 4:5] * width))


def finish(grads, updates, moments, weights, streams, small, gains, first, second):
    steps = 2
    per = steps // 2
    shapes = tuple(moment.shape for moment in moments)
    factors = [max(1.0, s[0] * GROUP / s[1]) ** 0.5 * muon_rate for s in shapes]
    halves, wholes = [], []
    for number, (rows, cols) in enumerate(shapes):
        if number in (OUT, DOWN):
            halves.append(
                pl.BlockSpec((1, rows // steps, cols), lambda j: (j // per, j % per, 0))
            )
            wholes.append(pl.BlockSpec((rows // steps, cols), lambda j: (j, 0)))
        else:
            halves.append(
                pl.BlockSpec((1, rows, cols // steps), lambda j: (j // per, 0, j % per))
            )
            wholes.append(pl.BlockSpec((rows, cols // steps), lambda j: (0, j)))
    lines = [
        pl.BlockSpec((s.shape[0] // steps, s.shape[1]), lambda j: (j, 0)) for s in streams
    ]
    single = lambda shape: pl.BlockSpec(shape, lambda j: (0, 0))
    table = single(gains.shape)
    out = pl.pallas_call(
        lambda *refs: finish_kernel(factors, *refs),
        grid=(steps,),
        out_shape=[jax.ShapeDtypeStruct(s, f32) for s in shapes * 3]
        + [jax.ShapeDtypeStruct(s.shape, f32) for s in streams]
        + [jax.ShapeDtypeStruct(gains.shape, f32)] * 4
        + [jax.ShapeDtypeStruct((1, 4), f32)],
        in_specs=halves + wholes * 3 + lines + [single(small.shape)] + [table] * 3,
        out_specs=wholes * 3 + lines + [table] * 4 + [single((1, 4))],
        compiler_params=pltpu.CompilerParams(vmem_limit_bytes=63 * 2**20),
        name="finish",
    )(*grads, *updates, *moments, *weights, *streams, small, gains, first, second)
    return out[0:5], out[5:10], out[10:15], out[15:17], out[17:21], out[21]


def shards(
    tokens,
    cotangent,
    prefix,
    w_qkv,
    w_out,
    w_gate,
    w_up,
    w_down,
    gains,
    moment_qkv,
    moment_out,
    moment_gate,
    moment_up,
    moment_down,
    gain_first,
    gain_second,
):
    reps = lax.axis_size("rep")
    _, _, lane, lanes = place()
    teams = [[member * lanes + k for k in range(lanes)] for member in range(GROUP)]

    def joined(shard):
        if lanes == 1:
            return shard
        return lax.all_gather(shard, "fsdp", axis=0, tiled=True, axis_index_groups=teams)

    def summed(term):
        if lanes == 1:
            return term
        parts = lax.all_gather(term, "fsdp", axis_index_groups=teams)
        return jnp.sum(parts.astype(f32), axis=0).astype(term.dtype)

    def parted(block):
        if lanes == 1:
            return block
        size = block.shape[0] // lanes
        return lax.dynamic_slice_in_dim(block, lane * size, size, 0)

    half_dim = jnp.arange(HEAD_DIM // 2, dtype=f32)
    frequency = (rotary_base ** (-(half_dim * 2.0 / HEAD_DIM)))[None, :]
    weights = [joined(term) for term in (w_qkv, w_out, w_gate, w_up, w_down)]
    moments = [
        joined(term)
        for term in (moment_qkv, moment_out, moment_gate, moment_up, moment_down)
    ]
    output, d_tokens, small, halves = layer(
        prefix, tokens, cotangent, frequency, joined(gains).T, weights, reps
    )
    halves = [summed(term) for term in halves]
    small = summed(small)
    updates = muon(halves, moments)
    grads, news, masters, streams, gain_terms, statistics = finish(
        halves,
        updates,
        moments,
        weights,
        (output, d_tokens),
        small,
        gains.T,
        gain_first.T,
        gain_second.T,
    )
    gain_terms = [term.T for term in gain_terms]
    grads, news, masters = (
        [parted(term) for term in group] for group in (grads, news, masters)
    )
    return (
        *streams,
        *grads,
        gain_terms[0],
        *news,
        *masters,
        *gain_terms[1:],
        statistics.reshape(4),
    )


def solution(mesh):
    in_specs = (
        P(("rep", "fsdp"), None),
        P(("rep", "fsdp"), None),
        P(),
        P("fsdp", None),
        P("fsdp", None),
        P("fsdp", None),
        P("fsdp", None),
        P("fsdp", None),
        P("fsdp", None),
        P("fsdp", None),
        P("fsdp", None),
        P("fsdp", None),
        P("fsdp", None),
        P("fsdp", None),
        P("fsdp", None),
        P("fsdp", None),
    )
    out_specs = (
        P(("rep", "fsdp"), None),
        P(("rep", "fsdp"), None),
        P("fsdp", None),
        P("fsdp", None),
        P("fsdp", None),
        P("fsdp", None),
        P("fsdp", None),
        P("fsdp", None),
        P("fsdp", None),
        P("fsdp", None),
        P("fsdp", None),
        P("fsdp", None),
        P("fsdp", None),
        P("fsdp", None),
        P("fsdp", None),
        P("fsdp", None),
        P("fsdp", None),
        P("fsdp", None),
        P("fsdp", None),
        P("fsdp", None),
        P("fsdp", None),
        P(),
    )
    return jax.shard_map(shards, mesh=mesh, in_specs=in_specs, out_specs=out_specs, check_vma=False)
```
